32 devices in a mesh: dp: 8 (over y, x, core), slot: 4 (over z).
Axes of the slice: x: 2, y: 2, z: 4, core: 2. Of those that a mesh axis runs over, the one named last changes fastest.
Arguments:
- tokens: bfloat16 [24576, 512], P('dp'), may hold values from -6 to 6
- segment_ids: int32 [24576], P('dp'), may hold values from 0 to 47, as said below
- w_query: bfloat16 [512, 512], P(('dp', 'slot')), may hold values from -0.5 to 0.5
- w_key: bfloat16 [512, 512], P(('dp', 'slot')), may hold values from -0.25 to 0.25
- w_value: bfloat16 [512, 512], P(('dp', 'slot')), may hold values from -0.25 to 0.25
- w_out: bfloat16 [512, 512], P(('dp', 'slot')), may hold values from -1 to 1
- w_control: bfloat16 [512, 8, 64], P('dp', None, 'slot'), may hold values from -0.75 to 0.75
- w_up: bfloat16 [512, 2048], P(('dp', 'slot')), may hold values from -0.25 to 0.25
- w_down: bfloat16 [2048, 512], P(('dp', 'slot')), may hold values from -0.125 to 0.125
- norm1_gain: bfloat16 [512], P(('dp', 'slot')), may hold values from 0.099609375 to 1.8984375
- norm1_bias: bfloat16 [512], P(('dp', 'slot')), may hold values from -2.5 to 2.5
- norm2_gain: bfloat16 [512], P(('dp', 'slot')), may hold values from 0.099609375 to 1.8984375
- norm2_bias: bfloat16 [512], P(('dp', 'slot')), may hold values from -2.5 to 2.5
- out_grad: bfloat16 [24576, 512], P(('dp', 'slot')), may hold values from -6 to 6
Outputs:
- output: bfloat16 [24576, 512], P(('dp', 'slot'))
- tokens_grad: float32 [24576, 512], P(('dp', 'slot'))
- w_query_grad: float32 [512, 512], P(('dp', 'slot'))
- w_key_grad: float32 [512, 512], P(('dp', 'slot'))
- w_value_grad: float32 [512, 512], P(('dp', 'slot'))
- w_out_grad: float32 [512, 512], P(('dp', 'slot'))
- w_control_grad: float32 [512, 8, 64], P('dp', None, 'slot')
- w_up_grad: float32 [512, 2048], P(('dp', 'slot'))
- w_down_grad: float32 [2048, 512], P(('dp', 'slot'))
- norm1_gain_grad: float32 [512], P(('dp', 'slot'))
- norm1_bias_grad: float32 [512], P(('dp', 'slot'))
- norm2_gain_grad: float32 [512], P(('dp', 'slot'))
- norm2_bias_grad: float32 [512], P(('dp', 'slot'))
The draws below stay inside these ranges and needn't reach their ends.
Inputs may be any that keep to these rules, and one draw needn't show every extreme that they name: segment_ids never fall; all tokens of one id lie in one aligned block of 3072 rows, and block b uses ids from b * (6) on.
All inputs are finite; a program needn't handle non-finite values.
Results may differ from the reference program's by a relative error of at most 0.04.
Values may be sent and summed in bfloat16 or wider, within the bound.
A program may use at most 576 MiB of HBM per device.

```python
import jax
import jax.numpy as jnp
from jax import lax

D = 512
HEADS = 8
HEAD_DIM = 64
SLOTS = 64
FF = 2048
TOK_DEV = 3072
SHORT_LEN = 512
TOKENS = 24576
N_SLOT = 4


def draw_segment_ids(key, part):
    key = jax.random.fold_in(key, 11)
    groups = TOKENS // TOK_DEV
    pieces = TOK_DEV // SHORT_LEN
    key_kind, key_cuts = jax.random.split(key)
    long_short = jax.random.randint(key_kind, (groups,), 0, 2)
    long_short = long_short.at[0].set(0).at[groups - 1].set(1)
    reach = SHORT_LEN // 4
    offsets = jax.random.randint(key_cuts, (groups, pieces - 1), -reach, reach + 1)
    cuts = (jnp.arange(1, pieces) * SHORT_LEN)[None, :] + offsets
    positions = jnp.arange(TOK_DEV)
    local_ids = jnp.sum((positions[None, :, None] >= cuts[:, None, :]).astype(jnp.int32), axis=2)
    local_ids = local_ids * long_short[:, None]
    all_ids = local_ids + (jnp.arange(groups) * pieces)[:, None]
    return all_ids.reshape(TOKENS).astype(jnp.int32)


def shard_levels(stream_key, dims, cuts, low, largest):
    def one(axis_at, blocks):
        draws = jax.random.uniform(jax.random.fold_in(jax.random.fold_in(stream_key, 6), axis_at), (blocks,), jnp.float32, low / len(cuts), largest / len(cuts))
        return jnp.repeat(jnp.exp(draws), dims[axis_at] // blocks).reshape((-1,) + (1,) * (len(dims) - axis_at - 1))

    factor_of = one(*cuts[0])
    for cut in cuts[1:]:
        factor_of = factor_of * one(*cut)
    return factor_of


def noise(stream_key, shape, scale, limit, cuts=(), kind=jnp.bfloat16):
    drawn = jax.random.normal(stream_key, shape, jnp.float32) * scale
    if len(cuts) > 0:
        drawn = shard_levels(stream_key, shape, cuts, -0.22, 0.18) * drawn
    return jnp.clip(drawn, min=-limit, max=limit).astype(kind)


def setup_inputs(seed: int = 0) -> dict:
    keys = jax.random.split(jax.random.key(seed), 15)
    return {
        "tokens": noise(keys[0], (TOKENS, D), 1.0, 6.0, ((0, 8),)),
        "segment_ids": draw_segment_ids(jax.random.fold_in(keys[14], 71), 0),
        "w_query": noise(keys[2], (D, D), (D // 4) ** -0.5, 0.5, ((0, 32),)),
        "w_key": noise(keys[3], (D, D), D ** -0.5, 0.25, ((0, 32),)),
        "w_value": noise(keys[4], (D, D), D ** -0.5, 0.25, ((0, 32),)),
        "w_out": noise(keys[5], (D, D), (D // 16) ** -0.5, 1.0, ((0, 32),)),
        "w_control": noise(keys[6], (D, HEADS, SLOTS), (D // 9) ** -0.5, 0.75, ((0, 8), (2, 4))),
        "w_up": noise(keys[7], (D, FF), D ** -0.5, 0.25, ((0, 32),)),
        "w_down": noise(keys[8], (FF, D), FF ** -0.5, 0.125, ((0, 32),)),
        "norm1_gain": jnp.clip(1.0 + 0.18 * jax.random.normal(keys[9], (D,), jnp.float32), 0.099609375, 1.8984375).astype(jnp.bfloat16),
        "norm1_bias": noise(keys[10], (D,), 0.3, 2.5, ((0, 32),)),
        "norm2_gain": jnp.clip(1.0 + 0.18 * jax.random.normal(keys[11], (D,), jnp.float32), 0.099609375, 1.8984375).astype(jnp.bfloat16),
        "norm2_bias": noise(keys[12], (D,), 0.3, 2.5, ((0, 32),)),
        "out_grad": noise(keys[13], (TOKENS, D), 1.0, 6.0, ((0, 32),)),
    }


NORM_EPS = 1e-05
HIGHEST_PREC = lax.Precision.HIGHEST

@jax.custom_vjp
def low(v):
    return lax.optimization_barrier(v.astype(jnp.bfloat16)).astype(jnp.float32)

@jax.custom_vjp
def low_back(v):
    return v

def low_keep(v):
    return (low(v), None)

def low_pass(kept, grad):
    return (grad,)

def back_keep(v):
    return (v, None)

def back_low(kept, grad):
    return (low(grad),)
low.defvjp(low_keep, low_pass)
low_back.defvjp(back_keep, back_low)

def layer_norm(values, gain_vec, bias_vec):
    center = values - lax.optimization_barrier(jnp.mean(values, axis=-1, keepdims=True))
    spread = lax.optimization_barrier(jnp.mean(center * center, axis=-1, keepdims=True))
    return center * lax.rsqrt(spread + NORM_EPS) * gain_vec + bias_vec

def attend_rows(queries, keys_all, values, weights, seg_ids, start_row):
    row_block = min(256, keys_all.shape[0])
    q_rows = lax.dynamic_slice_in_dim(queries, start_row, row_block, 0)
    seg_rows = lax.dynamic_slice_in_dim(seg_ids, start_row, row_block, 0)
    key_pos = jnp.arange(keys_all.shape[0], dtype=jnp.int32)
    row_pos = start_row + jnp.arange(row_block, dtype=jnp.int32)
    allowed = ((key_pos[None, :] <= row_pos[:, None]) & (seg_ids[None, :] == seg_rows[:, None])).astype(jnp.float32)
    scores = jnp.einsum('bhd,khd->hbk', q_rows, keys_all, precision=HIGHEST_PREC) * HEAD_DIM ** (-0.5) * allowed[None]
    copies = low_back(low(jnp.broadcast_to(scores, (N_SLOT,) + scores.shape)))
    numerator = low_back(jnp.einsum('jhbk,khjs->bhjs', copies, weights, precision=HIGHEST_PREC))
    totals = low_back(jnp.einsum('bk,khjs->bhjs', allowed, weights, precision=HIGHEST_PREC))
    logits = numerator / totals
    top_val = lax.optimization_barrier(jnp.max(logits, axis=(2, 3), keepdims=True))
    exponent = jnp.exp(logits - top_val)
    probability = exponent / lax.optimization_barrier(jnp.sum(exponent, axis=(2, 3), keepdims=True))
    scaled_probs = low(probability / totals)
    mixing = low_back(low(jnp.einsum('bhjs,khjs->jhbk', scaled_probs, weights, precision=HIGHEST_PREC) * allowed[None, None]))
    return jnp.einsum('jhbk,khd->bhd', mixing, values, precision=HIGHEST_PREC)

def layer(w_query, w_key, w_value, w_out, w_control, w_up, w_down, norm1_gain, norm1_bias, norm2_gain, norm2_bias, block_in, seg_ids):
    row_count = block_in.shape[0]
    normed = low(layer_norm(block_in, norm1_gain, norm1_bias))
    queries = low_back(low(jnp.dot(normed, w_query, precision=HIGHEST_PREC))).reshape(row_count, HEADS, HEAD_DIM)
    keys_all = low_back(low(jnp.dot(normed, w_key, precision=HIGHEST_PREC))).reshape(row_count, HEADS, HEAD_DIM)
    values = low_back(low(jnp.dot(normed, w_value, precision=HIGHEST_PREC))).reshape(row_count, HEADS, HEAD_DIM)
    control = low_back(jnp.einsum('td,dhs->ths', normed, w_control, precision=HIGHEST_PREC))
    weights = low(jnp.exp(control)).reshape(row_count, HEADS, N_SLOT, SLOTS // N_SLOT)
    row_block = min(256, row_count)
    starts = (jnp.arange(row_count // row_block) * row_block).astype(jnp.int32)
    blockwise = jax.checkpoint(attend_rows)
    mixture = lax.map(lambda start_row: blockwise(queries, keys_all, values, weights, seg_ids, start_row), starts)
    mixture = low_back(low(mixture.reshape(row_count, D)))
    hidden = block_in + low_back(jnp.dot(mixture, w_out, precision=HIGHEST_PREC))
    normed_two = low(layer_norm(hidden, norm2_gain, norm2_bias))
    upward = low_back(jnp.dot(normed_two, w_up, precision=HIGHEST_PREC))
    activated = low_back(low(jax.nn.gelu(upward)))
    return hidden + low_back(jnp.dot(activated, w_down, precision=HIGHEST_PREC))

def reference(tokens, segment_ids, w_query, w_key, w_value, w_out, w_control, w_up, w_down, norm1_gain, norm1_bias, norm2_gain, norm2_bias, out_grad):
    params = tuple((entry_val.astype(jnp.float32) for entry_val in (w_query, w_key, w_value, w_out, w_control, w_up, w_down, norm1_gain, norm1_bias, norm2_gain, norm2_bias)))
    blocks_in = tokens.astype(jnp.float32).reshape(-1, TOK_DEV, D)
    seg_blocks = segment_ids.reshape(-1, TOK_DEV)
    grad_blocks = out_grad.astype(jnp.float32).reshape(-1, TOK_DEV, D)

    def one_block(running, entry_val):
        block_in, seg_ids, block_grad = entry_val
        result, pullback = jax.vjp(lambda *args_all: layer(*args_all, seg_ids), *params, block_in)
        gradients = pullback(block_grad)
        running = tuple((acc_part + new_part for acc_part, new_part in zip(running, gradients[:-1])))
        return (running, (result, gradients[-1]))
    zero_acc = tuple((jnp.zeros_like(entry_val) for entry_val in params))
    grad_sums, (outputs, input_grads) = lax.scan(one_block, zero_acc, (blocks_in, seg_blocks, grad_blocks))
    return (outputs.reshape(-1, D).astype(jnp.bfloat16), input_grads.reshape(-1, D), grad_sums[0], grad_sums[1], grad_sums[2], grad_sums[3], grad_sums[4], grad_sums[5], grad_sums[6], grad_sums[7], grad_sums[8], grad_sums[9], grad_sums[10])
```

```python
import functools
import math

import jax
import jax.numpy as jnp
from jax import lax
from jax.experimental import pallas as pl
from jax.experimental.pallas import tpu as pltpu
from jax.sharding import PartitionSpec as P

D = 512
HEADS = 8
HEAD_DIM = 64
SLOTS = 64
FF = 2048
EPS = 1e-05
CH = 128
PAIRS = HEADS // 2
F32 = jnp.float32
BF16 = jnp.bfloat16
MESH = pl.DeviceIdType.MESH

K0, N0, C0, V0, Q0, O0, U0, W0, END = 0, 16, 32, 48, 64, 80, 96, 160, 224
GRID = (2, 2, 2, 4)
GATHER = ((K0, C0), (C0, V0), (V0, Q0), (Q0, O0), (O0, W0), (W0, END))
SCATTER = ((W0, END), (O0, W0), (V0, Q0), (Q0, O0), (K0, N0), (C0, V0))
G_DOWN, G_UP, G_V, G_Q, G_K, G_C, G_NORM = range(7)


def mm(a, b):
    return jnp.dot(a, b, preferred_element_type=F32)


def mm_t(a, b):
    return lax.dot_general(a, b, (((1,), (1,)), ((), ())), preferred_element_type=F32)


def t_mm(a, b):
    return lax.dot_general(a, b, (((0,), (0,)), ((), ())), preferred_element_type=F32)


def half_lanes(dtype):
    lane = lax.broadcasted_iota(jnp.int32, (1, CH), 1)
    left = jnp.where(lane < HEAD_DIM, 1.0, 0.0)
    return left.astype(dtype), (1.0 - left).astype(dtype)


def stack2(x, left, right):
    return jnp.concatenate([x * left, x * right], axis=0)


def per_head(op, x, fill):
    lane = lax.broadcasted_iota(jnp.int32, x.shape, 1)
    first = lane < HEAD_DIM
    a = op(jnp.where(first, x, fill), axis=1, keepdims=True)
    b = op(jnp.where(first, fill, x), axis=1, keepdims=True)
    return jnp.where(first, a, b)


def norm_stats(x):
    center = x - jnp.mean(x, axis=-1, keepdims=True)
    rstd = lax.rsqrt(jnp.mean(center * center, axis=-1, keepdims=True) + EPS)
    return center * rstd, rstd


def norm_back(dn, nh, rstd, gain):
    e = dn * gain
    return (e - jnp.mean(e, axis=-1, keepdims=True) - nh * jnp.mean(e * nh, axis=-1, keepdims=True)) * rstd


def kernel_body(cfg, *refs):
    refs = list(refs)
    take = lambda n: [refs.pop(0) for _ in range(n)]
    rows, n_slot, comm = cfg["rows"], cfg["n_slot"], cfg["comm"]
    n_ch = rows // CH
    rb = 256 if rows % 256 == 0 else 128
    n_rb = rows // rb
    (tok_in, seg_in, og_in) = take(3)
    if comm:
        (wq_in, wk_in, wv_in, wo_in, wc_in, wu_in, wd_in, norm_in) = take(8)
        (out_o, tg_o, wq_o, wk_o, wv_o, wo_o, wc_o, wu_o, wd_o, ng_o) = take(10)
    else:
        (g_in,) = take(1)
        (out_o, tg_o, pg, ng_o) = take(4)
    (g, xb, seg, og, n1, qs, kk_, vv_, wb, ew, num, inv_z, prob, rr_, oo_, hid, n2, act, du, da, do) = take(21)
    (s_kw, s_wv, z_st, s_r, s_n, z_r) = take(6)
    (cur_a, cur_b, cur_z, e_a, e_b, e_z) = take(6)
    (msk, mskt, g_prev, g_last, g_next, g_first) = take(6)
    (snd_a, snd_b, rcv_a, rcv_b, snd_c, snd_d, rcv_c, rcv_d) = take(8)
    (wc_s, st_send, st_recv, in_sem) = take(4)
    if comm:
        (pg, ngp, rc, rx1, ry1, ry2, rx2, rz, nrc, nrx, nry, nrz) = take(12)
        (ag_send, ag_recv, rs_send, rs_recv) = take(4)
    assert not refs

    dp = lax.axis_index("dp")
    z = lax.axis_index("slot")
    left, right = half_lanes(BF16)
    leftf, rightf = half_lanes(F32)
    ri = lax.broadcasted_iota(jnp.int32, (CH, CH), 0)
    ci = lax.broadcasted_iota(jnp.int32, (CH, CH), 1)
    block_diag = jnp.where((ri < HEAD_DIM) == (ci < HEAD_DIM), 1.0, 0.0).astype(F32)

    if comm:
        ny, nx, nc, nz = GRID
        py, px, pc = dp // (nx * nc), lax.rem(dp // nc, nx), lax.rem(dp, nc)
        at_x = ((py * nx + (1 - px)) * nc + pc, z)
        at_y = (((1 - py) * nx + px) * nc + pc, z)
        at_c = ((py * nx + px) * nc + (1 - pc), z)

    def at_z(s):
        return (dp, lax.rem(z + s, n_slot))

    pending = []

    def send(src, dst, sems, sem_r, idx, where):
        copy = pltpu.make_async_remote_copy(
            src_ref=src, dst_ref=dst, send_sem=sems.at[idx], recv_sem=sem_r.at[idx], device_id=where, device_id_type=MESH
        )
        copy.start()
        pending.append(copy)
        return copy

    for ref in (rcv_a, rcv_b, rcv_c, rcv_d):
        ref[...] = jnp.zeros_like(ref)
    loads = []

    def load(src, dst):
        copy = pltpu.make_async_copy(src, dst, in_sem.at[len(loads)])
        copy.start()
        loads.append(copy)

    my = None
    if comm:
        my = g.at[py, px, pc, z]
        load(wk_in, my.at[K0 : K0 + 16])
        load(norm_in, my.at[N0 : N0 + 16])
        for i in range(4):
            load(wc_in.at[16 * i : 16 * i + 16], my.at[C0 : C0 + 16, CH * i : CH * i + CH])
        load(wv_in, my.at[V0 : V0 + 16])
        load(wq_in, my.at[Q0 : Q0 + 16])
        load(wo_in, my.at[O0 : O0 + 16])
        for i in range(4):
            load(wu_in.at[:, D * i : D * i + D], my.at[U0 + 16 * i : U0 + 16 * i + 16])
        load(wd_in, my.at[W0:END])
    else:
        load(g_in, g)
    n_w = len(loads)
    load(tok_in.at[pl.ds(pl.multiple_of(z * rows, CH), rows)], xb)
    load(seg_in, seg)
    load(og_in, og)

    bar = pltpu.get_barrier_semaphore()
    peers = [at_z(s) for s in range(1, n_slot)]
    if comm:
        peers += [at_x, at_y, at_c]
    for peer in peers:
        pl.semaphore_signal(bar, inc=1, device_id=peer, device_id_type=MESH)
    pl.semaphore_wait(bar, len(peers))

    gathers = {}

    def gather(p, stage):
        if not comm:
            return
        r0, r1 = GATHER[p]
        sl = pl.ds(r0, r1 - r0)
        la, lb = pl.ds(0, D // 2), pl.ds(D // 2, D // 2)
        if stage > 0:
            for copy in gathers[p]:
                copy.wait_recv()
        put = lambda ref, idx, where: send(ref, ref, ag_send, ag_recv, p * 8 + idx, where)
        if stage == 0:
            mine = g.at[py, px, pc, z, sl]
            gathers[p] = [put(mine, s - 1, at_z(s)) for s in range(1, n_slot)]
        elif stage == 1:
            gathers[p] = [
                put(g.at[py, px, pc, :, sl, la], 3, at_x),
                put(g.at[py, px, pc, :, sl, lb], 4, at_y),
            ]
        elif stage == 2:
            gathers[p] = [
                put(g.at[py, :, pc, :, sl, la], 5, at_y),
                put(g.at[:, px, pc, :, sl, lb], 6, at_x),
            ]
        elif stage == 3:
            gathers[p] = [put(g.at[:, :, pc, :, sl, :], 7, at_c)]

    def weight(r0):
        return g[:, :, :, :, r0 : r0 + 16, :].reshape(D, D)

    for copy in loads[:n_w]:
        copy.wait()
    for p in range(4):
        gather(p, 0)
    for copy in loads[n_w:]:
        copy.wait()

    seg_rows = seg.shape[0]

    def seg_row(i):
        return seg[pl.ds(jnp.clip(i, 0, seg_rows - 1), 1), :].astype(F32)

    def first_of(i):
        return seg_row(i)[:, 0:1]

    def last_of(i):
        return seg_row(i)[:, CH - 1 : CH]

    base = z * n_ch

    def same(a, b):
        return jnp.where(a == b, 1.0, 0.0).astype(F32)

    def make_masks(c, _):
        row = jnp.broadcast_to(seg_row(base + c), (CH, CH))
        col = row.T
        eq = row == col
        msk[c] = jnp.where(eq & (ci <= ri), 1.0, 0.0).astype(BF16)
        mskt[c] = jnp.where(eq & (ri <= ci), 1.0, 0.0).astype(BF16)
        g_prev[c] = same(col, last_of(base + c - 1)).astype(BF16)
        g_last[c] = same(col, last_of(base + c)).astype(BF16)
        g_next[c] = same(col, first_of(base + c + 1)).astype(BF16)
        g_first[c] = same(col, first_of(base + c)).astype(BF16)
        return 0

    lax.fori_loop(0, n_ch, make_masks, 0)

    for p in range(4):
        gather(p, 1)
    for p in range(4):
        gather(p, 2)
    for p in range(4):
        gather(p, 3)
    for p in range(4):
        gather(p, 4)
    for p in (4, 5):
        gather(p, 0)

    norms = jnp.sum(
        g[:, :, :, :, N0 : N0 + 16, :].astype(F32).reshape(32, 16, D), axis=0
    )
    gain1, bias1, gain2, bias2 = (norms[i : i + 1, :] for i in range(4))

    def permutation():
        gw = SLOTS // GRID[3]
        a = lax.broadcasted_iota(jnp.int32, (D, D), 0)
        b = lax.broadcasted_iota(jnp.int32, (D, D), 1)
        h, s = b // SLOTS, lax.rem(b, SLOTS)
        src = (s // gw) * (HEADS * gw) + h * gw + lax.rem(s, gw)
        return jnp.where(a == src, 1.0, 0.0).astype(BF16)

    def control_weight():
        parts = []
        for y in range(2):
            for x in range(2):
                for c in range(2):
                    for i in range(4):
                        tiles = [g[y, x, c, j, C0 : C0 + 16, CH * i : CH * i + CH] for j in range(4)]
                        parts.append(jnp.concatenate(tiles, axis=1))
        return jnp.concatenate(parts, axis=0)

    wc_s[...] = mm(control_weight(), permutation()).astype(BF16)

    def rows_at(i, n=rb):
        return pl.ds(pl.multiple_of(i * n, n), n)

    def project(i, _):
        at = rows_at(i)
        nh, _r = norm_stats(xb[at, :].astype(F32))
        n = (nh * gain1 + bias1).astype(BF16)
        n1[at, :] = n
        kk_[at, :] = mm(n, weight(K0)).astype(BF16)
        e = jnp.exp(mm(n, wc_s[...]))
        ew[at, :] = e
        wb[at, :] = e.astype(BF16)
        vv_[at, :] = mm(n, weight(V0)).astype(BF16)
        qs[at, :] = (mm(n, weight(Q0)).astype(BF16) * (HEAD_DIM**-0.5)).astype(BF16)
        return 0

    lax.fori_loop(0, n_rb, project, 0)
    for p in (4, 5):
        gather(p, 1)

    def lanes(p):
        return slice(CH * p, CH * p + CH)

    def compact(x):
        return x[0:HEAD_DIM, :] + x[HEAD_DIM:CH, :]

    def expand(x):
        return jnp.concatenate([x * leftf, x * rightf], axis=0)

    def pack_row(ref, row):
        hi = row.astype(BF16).astype(F32)
        lo = row - hi
        parts = [a[:, lanes(p)] for a in (hi, lo) for p in range(PAIRS)]
        parts.append(jnp.zeros((8, CH), F32))
        ref[256:272, :] = jnp.concatenate(parts, axis=0).astype(BF16)

    def unpack_row(x):
        x = x.astype(F32)
        x = x[0:PAIRS, :] + x[PAIRS : 2 * PAIRS, :]
        return jnp.concatenate([x[p : p + 1, :] for p in range(PAIRS)], axis=1)

    cur_a[...] = jnp.zeros_like(cur_a)
    cur_b[...] = jnp.zeros_like(cur_b)
    cur_z[...] = jnp.zeros_like(cur_z)

    def states(c, _):
        at = rows_at(c, CH)
        keep = same(last_of(base + c - 1), last_of(base + c))
        z_st[pl.ds(c, 1), :] = cur_z[0:1, :]
        gl = g_last[c]
        for p in range(PAIRS):
            k_p, w_p, v_p = kk_[at, lanes(p)], wb[at, lanes(p)], vv_[at, lanes(p)]
            s_kw[c, p] = cur_a[p].astype(BF16)
            s_wv[c, p] = cur_b[p].astype(BF16)
            cur_a[p] = keep * cur_a[p] + t_mm(k_p * gl, w_p) * block_diag
            cur_b[p] = keep * cur_b[p] + t_mm(w_p * gl, v_p) * block_diag
        zi = mm(msk[c], wb[at, :])
        inv_z[at, :] = zi
        cur_z[0:1, :] = keep * cur_z[0:1, :] + zi[CH - 1 : CH, :]
        return 0

    lax.fori_loop(0, n_ch, states, 0)

    def exchange_start(parts, idx, up):
        for s in range(1, n_slot):
            @pl.when((z + s < n_slot) if up else (z - s >= 0))
            def _():
                for i, (src, dst) in enumerate(parts):
                    k = (idx + i) * n_slot + s
                    pltpu.make_async_remote_copy(
                        src_ref=src, dst_ref=dst.at[z], send_sem=st_send.at[k], recv_sem=st_recv.at[k],
                        device_id=(dp, z + s if up else z - s), device_id_type=MESH,
                    ).start()

    def exchange_wait(parts, idx, up):
        for s in range(1, n_slot):
            for i, (src, dst) in enumerate(parts):
                k = (idx + i) * n_slot + s
                there = lambda d: pltpu.make_async_remote_copy(
                    src_ref=src, dst_ref=dst.at[d], send_sem=st_send.at[k], recv_sem=st_recv.at[k],
                    device_id=(dp, z), device_id_type=MESH,
                )
                @pl.when((z + s < n_slot) if up else (z - s >= 0))
                def _():
                    there(z).wait_send()
                @pl.when((z - s >= 0) if up else (z + s < n_slot))
                def _():
                    there(z - s if up else z + s).wait_recv()

    for p in range(PAIRS):
        snd_a[64 * p : 64 * p + 64, :] = compact(cur_a[p]).astype(BF16)
        snd_b[64 * p : 64 * p + 64, :] = compact(cur_b[p]).astype(BF16)
    pack_row(snd_a, cur_z[0:1, :])
    fwd_parts = [(snd_a, rcv_a), (snd_b, rcv_b)]
    exchange_start(fwd_parts, 0, True)

    def two(x):
        return jnp.concatenate([x, x], axis=1)

    def numerators(c, _):
        at = rows_at(c, CH)
        m2 = two(msk[c])
        for p in range(PAIRS):
            k2 = stack2(kk_[at, lanes(p)], left, right)
            w2 = stack2(wb[at, lanes(p)], left, right)
            sc = mm_t(qs[at, lanes(p)], k2).astype(BF16) * m2
            num[at, lanes(p)] = mm(sc, w2)
        return 0

    lax.fori_loop(0, n_ch, numerators, 0)
    for p in (4, 5):
        gather(p, 2)

    exchange_wait(fwd_parts, 0, True)

    def entering(buf_a, buf_b, up):
        edge = last_of(base - 1) if up else first_of(base + n_ch)
        gate = [same(last_of((a + 1) * n_ch - 1) if up else first_of(a * n_ch), edge) for a in range(n_slot)]
        for p in range(PAIRS):
            at = slice(64 * p, 64 * p + 64)
            e_a[p] = expand(sum(gate[a] * buf_a[a, at, :].astype(F32) for a in range(n_slot)))
            e_b[p] = expand(sum(gate[a] * buf_b[a, at, :].astype(F32) for a in range(n_slot)))
        e_z[0:1, :] = unpack_row(sum(gate[a] * buf_a[a, 256:272, :].astype(F32) for a in range(n_slot)))

    entering(rcv_a, rcv_b, True)

    def mixture(c, _):
        at = rows_at(c, CH)
        reach = same(last_of(base - 1), last_of(base + c - 1))
        m2 = two(msk[c])
        gp = g_prev[c]
        gpf = gp.astype(F32)
        z_in = z_st[pl.ds(c, 1), :] + reach * e_z[0:1, :]
        for p in range(PAIRS):
            skw = (s_kw[c, p].astype(F32) + reach * e_a[p]).astype(BF16)
            swv = (s_wv[c, p].astype(F32) + reach * e_b[p]).astype(BF16)
            s_kw[c, p] = skw
            s_wv[c, p] = swv
            zz = inv_z[at, lanes(p)] + gpf * z_in[:, lanes(p)]
            lg = (num[at, lanes(p)] + mm(qs[at, lanes(p)] * gp, skw)) / zz
            ex = jnp.exp(lg - per_head(jnp.max, lg, -jnp.inf))
            pr = ex / per_head(jnp.sum, ex, 0.0)
            iz = 1.0 / zz
            r = (pr * iz).astype(BF16)
            num[at, lanes(p)] = lg
            inv_z[at, lanes(p)] = iz
            prob[at, lanes(p)] = pr
            rr_[at, lanes(p)] = r
            w2 = stack2(wb[at, lanes(p)], left, right)
            v2 = stack2(vv_[at, lanes(p)], left, right)
            mix = mm_t(r, w2).astype(BF16) * m2
            oo_[at, lanes(p)] = (mm(mix, v2) + mm(r * gp, swv)).astype(BF16)
        return 0

    lax.fori_loop(0, n_ch, mixture, 0)
    for stage in (3, 4):
        for p in (4, 5):
            gather(p, stage)

    def up_w(j):
        return weight(U0 + 16 * j)

    def down_w(j):
        return g[j // 2, j % 2, :, :, W0:END, :].reshape(D, D)

    c0, c1 = math.sqrt(2.0 / math.pi), 0.044715

    def feed(i, acc):
        at = rows_at(i)
        h = xb[at, :].astype(F32) + mm(oo_[at, :], weight(O0))
        nh, rstd = norm_stats(h)
        n = (nh * gain2 + bias2).astype(BF16)
        n2[at, :] = n
        gr = og[at, :]
        down = jnp.zeros((rb, D), F32)
        dn = jnp.zeros((rb, D), F32)
        for j in range(4):
            u = mm(n, up_w(j))
            dg = mm_t(gr, down_w(j)).astype(BF16).astype(F32)
            sq = u * u
            t = jnp.tanh(c0 * u * (1.0 + c1 * sq))
            half = 0.5 * (1.0 + t)
            a = (u * half).astype(BF16)
            slope = half + 0.5 * u * (1.0 - t * t) * (c0 * (1.0 + 3.0 * c1 * sq))
            d = (dg * slope).astype(BF16)
            act[at, D * j : D * j + D] = a
            du[at, D * j : D * j + D] = d
            down = down + mm(a, down_w(j))
            dn = dn + mm_t(d, up_w(j))
        out_o[at, :] = (h + down).astype(BF16)
        dh = gr.astype(F32) + norm_back(dn, nh, rstd, gain2)
        hid[at, :] = dh
        a = dh.astype(BF16)
        da[at, :] = a
        do[at, :] = mm_t(a, weight(O0)).astype(BF16)
        gains = jnp.sum(dn * nh, axis=0, keepdims=True)
        biases = jnp.sum(dn, axis=0, keepdims=True)
        return (acc[0] + gains, acc[1] + biases)

    zero_row = jnp.zeros((1, D), F32)
    gain2_g, bias2_g = lax.fori_loop(0, n_rb, feed, (zero_row, zero_row))

    def put_grad(r0, y, val):
        pg[y, :, :, :, r0 : r0 + 16, :] = val.astype(BF16).reshape(2, 2, 4, 16, D)

    def down_grads(m, _):
        val = t_mm(act[:, pl.ds(pl.multiple_of(m * 256, 256), 256)], og[...])
        pg[m // 4, lax.rem(m // 2, 2), lax.rem(m, 2), :, W0:END, :] = val.astype(BF16).reshape(4, 64, D)
        return 0

    lax.fori_loop(0, 8, down_grads, 0)

    def up_grads(j, _):
        for y in range(2):
            val = t_mm(n2[:, 256 * y : 256 * y + 256], du[:, pl.ds(pl.multiple_of(j * D, D), D)])
            pg[y, :, :, :, pl.ds(pl.multiple_of(U0 + 16 * j, 16), 16), :] = val.astype(BF16).reshape(2, 2, 4, 16, D)
        return 0

    lax.fori_loop(0, 4, up_grads, 0)
    for y in range(2):
        put_grad(O0, y, t_mm(oo_[:, 256 * y : 256 * y + 256], da[...]))

    scatters = {}

    def add_to(dst, src):
        dst[...] = (dst[...].astype(F32) + src[...].astype(F32)).astype(BF16)

    def scatter(p, stage):
        if not comm:
            return
        if p == G_NORM:
            return scatter_norm(stage)
        r0, r1 = SCATTER[p]
        sl = pl.ds(r0, r1 - r0)
        la, lb = pl.ds(0, D // 2), pl.ds(D // 2, D // 2)
        if stage > 0:
            for copy in scatters[p]:
                copy.wait_recv()
        put = lambda src, dst, idx, where: send(src, dst, rs_send, rs_recv, p * 8 + idx, where)
        if stage == 0:
            scatters[p] = [put(pg.at[:, :, 1 - pc, :, sl, :], rc.at[:, :, :, sl, :], 0, at_c)]
        elif stage == 1:
            def body(i, _):
                y, x = i // 2, lax.rem(i, 2)
                add_to(pg.at[y, x, pc, :, sl, :], rc.at[y, x, :, sl, :])
                return 0
            lax.fori_loop(0, 4, body, 0)
            scatters[p] = [
                put(pg.at[:, 1 - px, pc, :, sl, la], rx1.at[:, :, sl, :], 1, at_x),
                put(pg.at[1 - py, :, pc, :, sl, lb], ry1.at[:, :, sl, :], 2, at_y),
            ]
        elif stage == 2:
            def body(i, _):
                add_to(pg.at[i, px, pc, :, sl, la], rx1.at[i, :, sl, :])
                add_to(pg.at[py, i, pc, :, sl, lb], ry1.at[i, :, sl, :])
                return 0
            lax.fori_loop(0, 2, body, 0)
            scatters[p] = [
                put(pg.at[1 - py, px, pc, :, sl, la], ry2.at[:, sl, :], 3, at_y),
                put(pg.at[py, 1 - px, pc, :, sl, lb], rx2.at[:, sl, :], 4, at_x),
            ]
        elif stage == 3:
            add_to(pg.at[py, px, pc, :, sl, la], ry2.at[:, sl, :])
            add_to(pg.at[py, px, pc, :, sl, lb], rx2.at[:, sl, :])
            scatters[p] = [
                put(pg.at[py, px, pc, lax.rem(z + s, n_slot), sl, :], rz.at[s - 1, sl, :], 4 + s, at_z(s))
                for s in range(1, n_slot)
            ]
        elif stage == 4:
            total = pg[py, px, pc, z, sl, :].astype(F32)
            for s in range(1, n_slot):
                total = total + rz[s - 1, sl, :].astype(F32)
            if p == G_DOWN:
                wd_o[...] = total
            elif p == G_UP:
                wo_o[...] = total[0:16, :]
                for j in range(4):
                    wu_o[:, D * j : D * j + D] = total[16 + 16 * j : 32 + 16 * j, :]
            elif p == G_C:
                for i in range(4):
                    wc_o[16 * i : 16 * i + 16, :] = total[:, lanes(i)]
            else:
                {G_V: wv_o, G_Q: wq_o, G_K: wk_o}[p][...] = total

    def scatter_norm(stage):
        p = G_NORM
        if stage > 0:
            for copy in scatters[p]:
                copy.wait_recv()
        put = lambda src, dst, idx, where: send(src, dst, rs_send, rs_recv, p * 8 + idx, where)
        if stage == 0:
            scatters[p] = [put(ngp.at[:, :, 1 - pc], nrc, 0, at_c)]
        elif stage == 1:
            for y in range(2):
                for x in range(2):
                    add_to(ngp.at[y, x, pc], nrc.at[y, x])
            scatters[p] = [put(ngp.at[:, 1 - px, pc], nrx, 1, at_x)]
        elif stage == 2:
            for y in range(2):
                add_to(ngp.at[y, px, pc], nrx.at[y])
            scatters[p] = [put(ngp.at[1 - py, px, pc], nry, 2, at_y)]
        elif stage == 3:
            add_to(ngp.at[py, px, pc], nry)
            scatters[p] = [
                put(ngp.at[py, px, pc, lax.rem(z + s, n_slot)], nrz.at[s - 1], 4 + s, at_z(s)) for s in range(1, n_slot)
            ]
        elif stage == 4:
            total = ngp[py, px, pc, z].astype(F32)
            for s in range(1, n_slot):
                total = total + nrz[s - 1].astype(F32)
            ng_o[...] = total

    for stage in range(5):
        for p in (G_DOWN, G_UP):
            scatter(p, stage)

    dnum_, dz_ = du.at[:, 0:D], du.at[:, D : 2 * D]
    dq_, dk_, dv_, dphi_ = (act.at[:, D * j : D * j + D] for j in range(4))
    cur_a[...] = jnp.zeros_like(cur_a)
    cur_b[...] = jnp.zeros_like(cur_b)
    cur_z[...] = jnp.zeros_like(cur_z)

    def slot_grads(i, _):
        c = n_ch - 1 - i
        at = rows_at(c, CH)
        m2 = two(msk[c])
        gp = g_prev[c]
        gf = g_first[c]
        keep = same(first_of(base + c), first_of(base + c + 1))
        z_r[pl.ds(c, 1), :] = cur_z[0:1, :]
        dzs = []
        for p in range(PAIRS):
            w2 = stack2(wb[at, lanes(p)], left, right)
            v2 = stack2(vv_[at, lanes(p)], left, right)
            do_p = do[at, lanes(p)]
            dmix = mm_t(do_p, v2).astype(BF16) * m2
            dr = mm(dmix, w2) + mm_t(do_p * gp, s_wv[c, p])
            iz, pr, lg = inv_z[at, lanes(p)], prob[at, lanes(p)], num[at, lanes(p)]
            dpr = dr * iz
            dl = pr * (dpr - per_head(jnp.sum, pr * dpr, 0.0))
            dn_p = (dl * iz).astype(BF16)
            dz_p = (-(dpr * pr + dl * lg) * iz).astype(BF16)
            dnum_[at, lanes(p)] = dn_p
            dz_[at, lanes(p)] = dz_p
            dzs.append(dz_p)
            s_r[c, p] = cur_a[p].astype(BF16)
            s_n[c, p] = cur_b[p].astype(BF16)
            cur_a[p] = keep * cur_a[p] + t_mm(rr_[at, lanes(p)] * gf, do_p) * block_diag
            cur_b[p] = keep * cur_b[p] + t_mm(qs[at, lanes(p)] * gf, dn_p) * block_diag
        dz_all = jnp.concatenate(dzs, axis=1)
        firsts = mm(mskt[c][0:16, :], dz_all)
        cur_z[0:1, :] = keep * cur_z[0:1, :] + firsts[0:1, :]
        return 0

    lax.fori_loop(0, n_ch, slot_grads, 0)
    for p in range(PAIRS):
        snd_c[64 * p : 64 * p + 64, :] = compact(cur_b[p]).astype(BF16)
        snd_d[64 * p : 64 * p + 64, :] = compact(cur_a[p]).astype(BF16)
    pack_row(snd_c, cur_z[0:1, :])
    bwd_parts = [(snd_c, rcv_c), (snd_d, rcv_d)]
    exchange_start(bwd_parts, 2, False)
    exchange_wait(bwd_parts, 2, False)
    entering(rcv_c, rcv_d, False)

    def token_grads(c, _):
        at = rows_at(c, CH)
        reach = same(first_of(base + n_ch), first_of(base + c + 1))
        m2, mt = two(msk[c]), mskt[c]
        mt2 = two(mt)
        gp, gn = g_prev[c], g_next[c]
        z_in = z_r[pl.ds(c, 1), :] + reach * e_z[0:1, :]
        dwz = mm(mt, dz_[at, :]) + jnp.concatenate([gn.astype(F32)] * PAIRS, axis=1) * z_in
        for p in range(PAIRS):
            st_n = (s_n[c, p].astype(F32) + reach * e_a[p]).astype(BF16)
            st_r = (s_r[c, p].astype(F32) + reach * e_b[p]).astype(BF16)
            q_p, k_p, v_p, w_p = (ref[at, lanes(p)] for ref in (qs, kk_, vv_, wb))
            r_p, do_p, dn_p = rr_[at, lanes(p)], do[at, lanes(p)], dnum_[at, lanes(p)]
            q2, k2, w2, r2, do2, dn2 = (stack2(a, left, right) for a in (q_p, k_p, w_p, r_p, do_p, dn_p))
            wg, vg, kg = w_p * gn, v_p * gn, k_p * gn
            dsc = mm_t(dn_p, w2).astype(BF16) * m2
            dq = (mm(dsc, k2) + mm_t(dn_p * gp, s_kw[c, p])) * (HEAD_DIM**-0.5)
            dq_[at, lanes(p)] = dq.astype(BF16)
            mix_t = mm_t(w_p, r2).astype(BF16) * mt2
            dv_[at, lanes(p)] = (mm(mix_t, do2) + mm(wg, st_r)).astype(BF16)
            dmix_t = mm_t(v_p, do2).astype(BF16) * mt2
            sc_t = mm_t(k_p, q2).astype(BF16) * mt2
            dw = mm(dmix_t, r2) + mm_t(vg, st_r) + mm(sc_t, dn2) + mm(kg, st_n) + dwz[:, lanes(p)]
            dphi_[at, lanes(p)] = (dw * ew[at, lanes(p)]).astype(BF16)
            dsc_t = mm_t(w_p, dn2).astype(BF16) * mt2
            dk_[at, lanes(p)] = (mm(dsc_t, q2) + mm_t(wg, st_n)).astype(BF16)
        return 0

    lax.fori_loop(0, n_ch, token_grads, 0)

    for y in range(2):
        cols = slice(256 * y, 256 * y + 256)
        put_grad(V0, y, t_mm(n1[:, cols], dv_[...]))
        put_grad(Q0, y, t_mm(n1[:, cols], dq_[...]))
        put_grad(K0, y, t_mm(n1[:, cols], dk_[...]))
    for y in range(2):
        cols = slice(256 * y, 256 * y + 256)
        val = mm_t(t_mm(n1[:, cols], dphi_[...]).astype(BF16), permutation()).astype(BF16)
        for x in range(2):
            for c in range(2):
                for i in range(4):
                    r = ((x * 2 + c) * 4 + i) * 16
                    for j in range(4):
                        pg[y, x, c, j, C0 : C0 + 16, CH * i : CH * i + CH] = val[r : r + 16, lanes(j)]

    def input_grads(i, acc):
        at = rows_at(i)
        dn = mm_t(dq_[at, :], weight(Q0)) + mm_t(dk_[at, :], weight(K0)) + mm_t(dv_[at, :], weight(V0)) + mm_t(dphi_[at, :], wc_s[...])
        nh, rstd = norm_stats(xb[at, :].astype(F32))
        tg_o[at, :] = hid[at, :] + norm_back(dn, nh, rstd, gain1)
        return (acc[0] + jnp.sum(dn * nh, axis=0, keepdims=True), acc[1] + jnp.sum(dn, axis=0, keepdims=True))

    gain1_g, bias1_g = lax.fori_loop(0, n_rb, input_grads, (zero_row, zero_row))
    norm_g = jnp.concatenate([gain1_g, bias1_g, gain2_g, bias2_g, jnp.zeros((12, D), F32)], axis=0)
    if comm:
        for y in range(2):
            for x in range(2):
                for c in range(2):
                    for j in range(4):
                        d = ((y * 2 + x) * 2 + c) * 4 + j
                        ngp[y, x, c, j] = norm_g[:, lanes(d // 8)].astype(BF16)
    else:
        ng_o[...] = norm_g
    for stage in range(5):
        for p in (G_V, G_Q, G_K, G_C, G_NORM):
            scatter(p, stage)

    for copy in pending:
        copy.wait_send()


def vm(shape, dtype):
    return pltpu.VMEM(shape, dtype)


def run_layer(rows, n_slot, seg_rows, comm, operands):
    n_ch = rows // CH
    act_shape = (rows, D)
    hbm, vmem = pl.BlockSpec(memory_space=pl.ANY), pl.BlockSpec(memory_space=pltpu.VMEM)
    sds = jax.ShapeDtypeStruct
    outs = [sds(act_shape, BF16), sds(act_shape, F32)]
    if comm:
        outs += [sds((16, D), F32)] * 4 + [sds((64, CH), F32), sds((16, FF), F32), sds((64, D), F32), sds((16, CH), F32)]
    else:
        outs += [sds((*GRID, END, D), BF16), sds((16, D), F32)]
    b, f = (lambda: vm(act_shape, BF16)), (lambda: vm(act_shape, F32))
    state = lambda dtype: vm((n_ch, PAIRS, CH, CH), dtype)
    scratch = [
        vm((*GRID, END, D), BF16), b(), vm((seg_rows, CH), jnp.int32), b(), b(), b(), b(), b(), b(),
        f(), f(), f(), f(), b(), b(), f(), b(), vm((rows, FF), BF16), vm((rows, FF), BF16), b(), b(),
        state(BF16), state(BF16), vm((max(8, n_ch), D), F32), state(BF16), state(BF16), vm((max(8, n_ch), D), F32),
        vm((PAIRS, CH, CH), F32), vm((PAIRS, CH, CH), F32), vm((8, D), F32),
        vm((PAIRS, CH, CH), F32), vm((PAIRS, CH, CH), F32), vm((8, D), F32),
    ]
    scratch += [vm((n_ch, CH, CH), BF16)] * 6
    long, short = (272, CH), (256, CH)
    scratch += [vm(long, BF16), vm(short, BF16), vm((n_slot, *long), BF16), vm((n_slot, *short), BF16)] * 2
    scratch += [vm((D, D), BF16), pltpu.SemaphoreType.DMA((4 * n_slot,)), pltpu.SemaphoreType.DMA((4 * n_slot,)), pltpu.SemaphoreType.DMA((20,))]
    if comm:
        ny, nx, nc, nz = GRID
        scratch += [
            vm((*GRID, END, D), BF16), vm((*GRID, 16, CH), BF16),
            vm((ny, nx, nz, END, D), BF16), vm((ny, nz, END, D // 2), BF16), vm((nx, nz, END, D // 2), BF16),
            vm((nz, END, D // 2), BF16), vm((nz, END, D // 2), BF16), vm((nz - 1, END, D), BF16),
            vm((ny, nx, nz, 16, CH), BF16), vm((ny, nz, 16, CH), BF16), vm((nz, 16, CH), BF16), vm((nz - 1, 16, CH), BF16),
        ]
        scratch += [pltpu.SemaphoreType.DMA((8 * 6,))] * 2 + [pltpu.SemaphoreType.DMA((8 * 7,))] * 2
    cfg = dict(rows=rows, n_slot=n_slot, comm=comm)
    return pl.pallas_call(
        functools.partial(kernel_body, cfg),
        out_shape=outs,
        in_specs=[hbm] * len(operands),
        out_specs=[vmem] * len(outs),
        scratch_shapes=scratch,
        compiler_params=pltpu.CompilerParams(collective_id=0, has_side_effects=True, vmem_limit_bytes=63 * 2**20),
    )(*operands)


def layer(
    tokens, segment_ids, w_query, w_key, w_value, w_out, w_control, w_up, w_down,
    norm1_gain, norm1_bias, norm2_gain, norm2_bias, out_grad,
):
    n_slot, n_dp = lax.axis_size("slot"), lax.axis_size("dp")
    n_dev = n_slot * n_dp
    rows = tokens.shape[0] // n_slot
    seg = segment_ids.reshape(-1, CH)
    dev = lax.axis_index("dp") * n_slot + lax.axis_index("slot")
    norms = jnp.stack([norm1_gain, norm1_bias, norm2_gain, norm2_bias])
    if n_dev == math.prod(GRID) and n_slot == GRID[3]:
        own = jnp.tile(norms, (1, n_dev))
        place = (lax.broadcasted_iota(jnp.int32, (4, D), 1) // norms.shape[1]) == dev
        block = jnp.pad(jnp.where(place, own, 0), ((0, 12), (0, 0)))
        outs = run_layer(rows, n_slot, seg.shape[0], True, (
            tokens, seg, out_grad, w_query, w_key, w_value, w_out, w_control.reshape(-1, CH), w_up, w_down, block,
        ))
        out, tg, wq, wk, wv, wo, wc, wu, wd, ng = outs
        own = lax.dynamic_slice_in_dim(ng[:4], lax.rem(dev, 8) * norms.shape[1], norms.shape[1], 1)
        return (out, tg, wq, wk, wv, wo, wc.reshape(w_control.shape), wu, wd, own[0], own[1], own[2], own[3])

    both = ("dp", "slot")
    gather = lambda a: lax.all_gather(a, both, axis=0, tiled=True)
    n_blk = math.prod(GRID)
    wc = lax.all_gather(lax.all_gather(w_control, "dp", axis=0, tiled=True), "slot", axis=2, tiled=True)
    gw = SLOTS // GRID[3]
    wc = wc.reshape(8, 4, 16, HEADS, GRID[3], gw).transpose(0, 4, 2, 1, 3, 5).reshape(n_blk, 16, D)
    norm_all = lax.all_gather(norms, both, axis=1, tiled=True)
    norm_blk = jnp.zeros((n_blk, 16, D), BF16).at[0, :4].set(norm_all)
    split = lambda a: gather(a).reshape(n_blk, -1, D)
    up = gather(w_up).reshape(n_blk, 16, 4, D).transpose(0, 2, 1, 3).reshape(n_blk, 64, D)
    packed = jnp.concatenate(
        [split(w_key), norm_blk, wc, split(w_value), split(w_query), split(w_out), up, split(w_down)], axis=1
    ).reshape(*GRID, END, D)
    out, tg, part, ng = run_layer(rows, n_slot, seg.shape[0], False, (tokens, seg, out_grad, packed))
    part = part.reshape(n_blk, END, D).astype(F32)
    scatter = lambda a, dim=0: lax.psum_scatter(a, both, scatter_dimension=dim, tiled=True)
    full = lambda r0, r1: part[:, r0:r1].reshape(-1, D)
    wcg = part[:, C0:V0].reshape(8, GRID[3], 16, 4, HEADS, gw).transpose(0, 3, 2, 4, 1, 5).reshape(D, HEADS, SLOTS)
    wcg = lax.psum_scatter(lax.psum_scatter(wcg, "dp", scatter_dimension=0, tiled=True), "slot", scatter_dimension=2, tiled=True)
    upg = part[:, U0:W0].reshape(n_blk, 4, 16, D).transpose(0, 2, 1, 3).reshape(D, FF)
    ng = scatter(ng[:4], 1)
    return (
        out, tg, scatter(full(Q0, O0)), scatter(full(K0, N0)), scatter(full(V0, Q0)), scatter(full(O0, U0)),
        wcg, scatter(upg), scatter(full(W0, END)), ng[0], ng[1], ng[2], ng[3],
    )


def solution(mesh):
    both = P(("dp", "slot"), None)
    vec = P(("dp", "slot"))
    control = P("dp", None, "slot")
    in_specs = (
        P("dp", None), P("dp"), both, both, both, both, control, both, both, vec, vec, vec, vec, both,
    )
    out_specs = (both, both, both, both, both, both, control, both, both, vec, vec, vec, vec)
    return jax.shard_map(layer, mesh=mesh, in_specs=in_specs, out_specs=out_specs, check_vma=False)
```

```python
import functools
import math

import jax
import jax.numpy as jnp
from jax import lax
from jax.experimental import pallas as pl
from jax.experimental.pallas import tpu as pltpu
from jax.sharding import PartitionSpec as P

D = 512
HEADS = 8
HEAD_DIM = 64
SLOTS = 64
FF = 2048
EPS = 1e-05
CH = 128
PAIRS = HEADS // 2
F32 = jnp.float32
BF16 = jnp.bfloat16
MESH = pl.DeviceIdType.MESH

K0, N0, C0, V0, Q0, O0, U0, W0, END = 0, 16, 32, 48, 64, 80, 96, 160, 224
GRID = (2, 2, 2, 4)
GATHER = ((K0, C0), (C0, V0), (V0, Q0), (Q0, O0), (O0, W0), (W0, END))
SCATTER = ((W0, END), (O0, W0), (V0, Q0), (Q0, O0), (K0, N0), (C0, V0))
G_DOWN, G_UP, G_V, G_Q, G_K, G_C, G_NORM = range(7)


def mm(a, b):
    return jnp.dot(a, b, preferred_element_type=F32)


def mm_t(a, b):
    return lax.dot_general(a, b, (((1,), (1,)), ((), ())), preferred_element_type=F32)


def t_mm(a, b):
    return lax.dot_general(a, b, (((0,), (0,)), ((), ())), preferred_element_type=F32)


def half_lanes(dtype):
    lane = lax.broadcasted_iota(jnp.int32, (1, CH), 1)
    left = jnp.where(lane < HEAD_DIM, 1.0, 0.0)
    return left.astype(dtype), (1.0 - left).astype(dtype)


def stack2(x, left, right):
    return jnp.concatenate([x * left, x * right], axis=0)


def per_head(op, x, fill):
    lane = lax.broadcasted_iota(jnp.int32, x.shape, 1)
    first = lane < HEAD_DIM
    a = op(jnp.where(first, x, fill), axis=1, keepdims=True)
    b = op(jnp.where(first, fill, x), axis=1, keepdims=True)
    return jnp.where(first, a, b)


def norm_stats(x):
    center = x - jnp.mean(x, axis=-1, keepdims=True)
    rstd = lax.rsqrt(jnp.mean(center * center, axis=-1, keepdims=True) + EPS)
    return center * rstd, rstd


def norm_back(dn, nh, rstd, gain):
    e = dn * gain
    return (e - jnp.mean(e, axis=-1, keepdims=True) - nh * jnp.mean(e * nh, axis=-1, keepdims=True)) * rstd


def kernel_body(cfg, *refs):
    refs = list(refs)
    take = lambda n: [refs.pop(0) for _ in range(n)]
    rows, n_slot, comm = cfg["rows"], cfg["n_slot"], cfg["comm"]
    n_ch = rows // CH
    rb = 256 if rows % 256 == 0 else 128
    n_rb = rows // rb
    (tok_in, seg_in, og_in) = take(3)
    if comm:
        (wq_in, wk_in, wv_in, wo_in, wc_in, wu_in, wd_in, *norm_in) = take(11)
        out_h, tg_h, *grad_h = take(10)
    else:
        (g_in,) = take(1)
        (out_h, tg_h, pg, ng_o) = take(4)
    (g, xb, seg, og, n1, qs, kk_, vv_, wb, ew, num, inv_z, prob, rr_, oo_, hid, n2, act, du, da, do) = take(21)
    (n1t, n2t, dq_, dk_, dv_, dphi_, hsum) = take(7)
    (s_kw, s_wv, z_st, s_r, s_n, z_r) = take(6)
    (cur_a, cur_b, cur_z, e_a, e_b, e_z) = take(6)
    (msk, mskt, g_prev, g_last, g_next, g_first) = take(6)
    (snd_a, snd_b, rcv_a, rcv_b, snd_c, snd_d, rcv_c, rcv_d) = take(8)
    (wc_s, st_send, st_recv, in_sem, out_sem) = take(5)
    if comm:
        (pg, ngp, rc, rx1, ry1, ry2, rx2, rz, nrc, nrx, nry, nrz) = take(12)
        (ag_send, ag_recv, rs_send, rs_recv) = take(4)
        (wct, nv) = take(2)
        grad_s = take(8)
        (wq_o, wk_o, wv_o, wo_o, wc_o, wu_o, wd_o, ng_o) = grad_s
    assert not refs
    tg_o, out_o = prob, oo_
    dnum_, dz_ = du.at[:, 0:D], du.at[:, D : 2 * D]

    dp = lax.axis_index("dp")
    z = lax.axis_index("slot")
    left, right = half_lanes(BF16)
    leftf, rightf = half_lanes(F32)
    ri = lax.broadcasted_iota(jnp.int32, (CH, CH), 0)
    ci = lax.broadcasted_iota(jnp.int32, (CH, CH), 1)
    block_diag = jnp.where((ri < HEAD_DIM) == (ci < HEAD_DIM), 1.0, 0.0).astype(F32)
    ones_diag = block_diag.astype(BF16)
    pairs = range(PAIRS)

    if comm:
        ny, nx, nc, nz = GRID
        py, px, pc = dp // (nx * nc), lax.rem(dp // nc, nx), lax.rem(dp, nc)
        at_x = ((py * nx + (1 - px)) * nc + pc, z)
        at_y = (((1 - py) * nx + px) * nc + pc, z)
        at_c = ((py * nx + px) * nc + (1 - pc), z)

    def at_z(s):
        return (dp, lax.rem(z + s, n_slot))

    def remote(src, dst, send_sem, recv_sem, idx, where):
        return pltpu.make_async_remote_copy(
            src_ref=src, dst_ref=dst, send_sem=send_sem.at[idx], recv_sem=recv_sem.at[idx],
            device_id=where, device_id_type=MESH,
        )

    loads = {}

    def load(name, src, dst):
        copy = pltpu.make_async_copy(src, dst, in_sem.at[sum(map(len, loads.values()))])
        copy.start()
        loads.setdefault(name, []).append(copy)

    def loaded(name):
        for copy in loads.get(name, ()):
            copy.wait()

    if comm:
        my = g.at[py, px, pc, z]
        for i, ref in enumerate(norm_in):
            load("norm", ref, nv.at[i])
        load(0, wk_in, my.at[K0 : K0 + 16])
        load(1, wc_in, wct)
        load(2, wv_in, my.at[V0 : V0 + 16])
        load(3, wq_in, my.at[Q0 : Q0 + 16])
    else:
        load(0, g_in, g)
    load("tok", tok_in.at[pl.ds(pl.multiple_of(z * rows, CH), rows)], xb)
    load("seg", seg_in, seg)
    if comm:
        load(4, wo_in, my.at[O0 : O0 + 16])
        for i in range(4):
            load(4, wu_in.at[:, D * i : D * i + D], my.at[U0 + 16 * i : U0 + 16 * i + 16])
        load(5, wd_in, my.at[W0:END])
    load("og", og_in, og)

    for ref in (rcv_a, rcv_b, rcv_c, rcv_d):
        ref[...] = jnp.zeros_like(ref)
    bar = pltpu.get_barrier_semaphore()
    peers = [at_z(s) for s in range(1, n_slot)]
    if comm:
        peers += [at_x, at_y, at_c]
    for peer in peers:
        pl.semaphore_signal(bar, inc=1, device_id=peer, device_id_type=MESH)
    pl.semaphore_wait(bar, len(peers))

    la, lb = pl.ds(0, D // 2), pl.ds(D // 2, D // 2)

    def gather_copies(p, stage):
        r0, r1 = GATHER[p]
        sl = pl.ds(r0, r1 - r0)
        put = lambda ref, idx, where: remote(ref, ref, ag_send, ag_recv, p * 8 + idx, where)
        if stage == 0:
            return [put(g.at[py, px, pc, z, sl], s - 1, at_z(s)) for s in range(1, n_slot)]
        if stage == 1:
            return [put(g.at[py, px, pc, :, sl, la], 3, at_x), put(g.at[py, px, pc, :, sl, lb], 4, at_y)]
        if stage == 2:
            return [put(g.at[py, :, pc, :, sl, la], 5, at_y), put(g.at[:, px, pc, :, sl, lb], 6, at_x)]
        return [put(g.at[:, :, pc, :, sl, :], 7, at_c)]

    def gather(p, stage):
        if not comm:
            return
        if stage == 0:
            if p != 1:
                loaded(p)
        else:
            for copy in gather_copies(p, stage - 1):
                copy.wait_recv()
        if stage < 4:
            for copy in gather_copies(p, stage):
                copy.start()

    def weight(r0):
        return g[:, :, :, :, r0 : r0 + 16, :].reshape(D, D)

    if comm:
        loaded("norm")
        each = nv.shape[2]
        vals = [nv[i].astype(F32) for i in range(4)] + [jnp.zeros((12, each), F32)]
        a = lax.broadcasted_iota(jnp.int32, (each, D), 0)
        b = lax.broadcasted_iota(jnp.int32, (each, D), 1)
        place = jnp.where(b == a + each * (dp * n_slot + z), 1.0, 0.0).astype(BF16)
        my[N0 : N0 + 16, :] = mm(jnp.concatenate(vals, axis=0).astype(BF16), place).astype(BF16)
    gather(0, 0)
    if comm:
        loaded(1)
        a = lax.broadcasted_iota(jnp.int32, (wct.shape[1], wct.shape[1]), 0)
        b = lax.broadcasted_iota(jnp.int32, (wct.shape[1], wct.shape[1]), 1)
        flat = mm_t(jnp.where(a == b, 1.0, 0.0).astype(BF16), wct[...]).astype(BF16)
        for i in range(4):
            my[C0 : C0 + 16, CH * i : CH * i + CH] = flat[16 * i : 16 * i + 16, :]
    else:
        loaded(0)
    for p in range(1, 4):
        gather(p, 0)

    seg_rows = seg.shape[0]

    def seg_row(i):
        return seg[pl.ds(jnp.clip(i, 0, seg_rows - 1), 1), :].astype(F32)

    def first_of(i):
        return seg_row(i)[:, 0:1]

    def last_of(i):
        return seg_row(i)[:, CH - 1 : CH]

    base = z * n_ch

    def same(a, b):
        return jnp.where(a == b, 1.0, 0.0).astype(F32)

    def make_masks(c, _):
        row = jnp.broadcast_to(seg_row(base + c), (CH, CH))
        col = row.T
        eq = row == col
        msk[c] = jnp.where(eq & (ci <= ri), 1.0, 0.0).astype(BF16)
        mskt[c] = jnp.where(eq & (ri <= ci), 1.0, 0.0).astype(BF16)
        g_prev[c] = same(col, last_of(base + c - 1)).astype(BF16)
        g_last[c] = same(col, last_of(base + c)).astype(BF16)
        g_next[c] = same(col, first_of(base + c + 1)).astype(BF16)
        g_first[c] = same(col, first_of(base + c)).astype(BF16)
        return 0

    def rows_at(i, n=rb):
        return pl.ds(pl.multiple_of(i * n, n), n)

    def center(i, _):
        at = rows_at(i)
        nh, _r = norm_stats(xb[at, :].astype(F32))
        hid[at, :] = nh
        return 0

    loaded("seg")
    lax.fori_loop(0, n_ch, make_masks, 0)
    gather(0, 1)
    loaded("tok")
    lax.fori_loop(0, n_rb, center, 0)
    gather(1, 1)
    gather(0, 2)
    gather(2, 1)
    gather(1, 2)
    gather(3, 1)
    gather(0, 3)
    gather(2, 2)
    gather(4, 0)
    gather(5, 0)
    gather(1, 3)
    gather(0, 4)

    norms = jnp.sum(g[:, :, :, :, N0 : N0 + 16, :].astype(F32).reshape(32, 16, D), axis=0)
    gain1, bias1, gain2, bias2 = (norms[i : i + 1, :] for i in range(4))

    def project_k(i, _):
        at = rows_at(i)
        n = (hid[at, :] * gain1 + bias1).astype(BF16)
        n1[at, :] = n
        n1t[:, at] = n.T
        kk_[at, :] = mm(n, weight(K0)).astype(BF16)
        return 0

    lax.fori_loop(0, n_rb, project_k, 0)
    gather(3, 2)
    gather(2, 3)
    gather(1, 4)

    def permutation():
        gw = SLOTS // GRID[3]
        a = lax.broadcasted_iota(jnp.int32, (D, D), 0)
        b = lax.broadcasted_iota(jnp.int32, (D, D), 1)
        h, s = b // SLOTS, lax.rem(b, SLOTS)
        src = (s // gw) * (HEADS * gw) + h * gw + lax.rem(s, gw)
        return jnp.where(a == src, 1.0, 0.0).astype(BF16)

    def control_weight():
        parts = []
        for y in range(2):
            for x in range(2):
                for c in range(2):
                    for i in range(4):
                        tiles = [g[y, x, c, j, C0 : C0 + 16, CH * i : CH * i + CH] for j in range(4)]
                        parts.append(jnp.concatenate(tiles, axis=1))
        return jnp.concatenate(parts, axis=0)

    wc_s[...] = mm(control_weight(), permutation()).astype(BF16)

    def project_c(i, _):
        at = rows_at(i)
        e = jnp.exp(mm(n1[at, :], wc_s[...]))
        ew[at, :] = e
        wb[at, :] = e.astype(BF16)
        return 0

    def project_v(i, _):
        at = rows_at(i)
        vv_[at, :] = mm(n1[at, :], weight(V0)).astype(BF16)
        return 0

    def project_q(i, _):
        at = rows_at(i)
        qs[at, :] = (mm(n1[at, :], weight(Q0)).astype(BF16) * (HEAD_DIM**-0.5)).astype(BF16)
        return 0

    def lanes(p):
        return slice(CH * p, CH * p + CH)

    def split(x):
        return [x[:, lanes(p)] for p in pairs]

    def compact(x):
        return x[0:HEAD_DIM, :] + x[HEAD_DIM:CH, :]

    def expand(x):
        return jnp.concatenate([x * leftf, x * rightf], axis=0)

    def pack_row(ref, row):
        hi = row.astype(BF16).astype(F32)
        lo = row - hi
        parts = [a[:, lanes(p)] for a in (hi, lo) for p in pairs]
        parts.append(jnp.zeros((8, CH), F32))
        ref[256:272, :] = jnp.concatenate(parts, axis=0).astype(BF16)

    def unpack_row(x):
        x = x.astype(F32)
        x = x[0:PAIRS, :] + x[PAIRS : 2 * PAIRS, :]
        return jnp.concatenate([x[p : p + 1, :] for p in pairs], axis=1)

    def wide(x):
        return jnp.concatenate([x] * PAIRS, axis=1)

    def scan_step(cur, saved, c, keep, rows_a, rows_b):
        new = [t_mm(a, b) * block_diag for a, b in zip(split(rows_a), split(rows_b))]
        old = [cur[p] for p in pairs]
        for p in pairs:
            saved[c, p] = old[p].astype(BF16)
        for p in pairs:
            cur[p] = keep * old[p] + new[p]

    def exchange_copies(idx, src, dst, up, s):
        k = idx * n_slot + s
        ahead, behind = (z + s, z - s) if up else (z - s, z + s)
        out = lambda: remote(src, dst.at[z], st_send, st_recv, k, (dp, ahead))
        come = lambda: remote(src, dst.at[behind], st_send, st_recv, k, (dp, ahead))
        return out, come, (ahead >= 0) & (ahead < n_slot), (behind >= 0) & (behind < n_slot)

    def exchange_start(idx, src, dst, up):
        for s in range(1, n_slot):
            out, _c, has, _h = exchange_copies(idx, src, dst, up, s)
            pl.when(has)(lambda: out().start())

    def exchange_wait(idx, src, dst, up):
        for s in range(1, n_slot):
            out, come, has, gets = exchange_copies(idx, src, dst, up, s)
            pl.when(has)(lambda: out().wait_send())
            pl.when(gets)(lambda: come().wait_recv())

    def pack_state(snd, cur):
        for p in pairs:
            snd[64 * p : 64 * p + 64, :] = compact(cur[p]).astype(BF16)

    def entering(buf, e, up):
        edge = last_of(base - 1) if up else first_of(base + n_ch)
        gate = [same(last_of((a + 1) * n_ch - 1) if up else first_of(a * n_ch), edge) for a in range(n_slot)]
        total = sum(gate[a] * buf[a].astype(F32) for a in range(n_slot))
        for p in pairs:
            e[p] = expand(total[64 * p : 64 * p + 64, :])
        if total.shape[0] > 256:
            e_z[0:1, :] = unpack_row(total[256:272, :])

    cur_a[...] = jnp.zeros_like(cur_a)
    cur_b[...] = jnp.zeros_like(cur_b)
    cur_z[...] = jnp.zeros_like(cur_z)

    def key_states(c, _):
        at = rows_at(c, CH)
        keep = same(last_of(base + c - 1), last_of(base + c))
        w = wb[at, :]
        zi = mm(msk[c], w)
        scan_step(cur_a, s_kw, c, keep, kk_[at, :] * wide(g_last[c]), w)
        z_old = cur_z[0:1, :]
        z_st[pl.ds(c, 1), :] = z_old
        inv_z[at, :] = zi
        cur_z[0:1, :] = keep * z_old + zi[CH - 1 : CH, :]
        return 0

    def value_states(c, _):
        at = rows_at(c, CH)
        keep = same(last_of(base + c - 1), last_of(base + c))
        scan_step(cur_b, s_wv, c, keep, wb[at, :] * wide(g_last[c]), vv_[at, :])
        return 0

    lax.fori_loop(0, n_rb, project_c, 0)
    lax.fori_loop(0, n_ch, key_states, 0)
    pack_state(snd_a, cur_a)
    pack_row(snd_a, cur_z[0:1, :])
    exchange_start(0, snd_a, rcv_a, True)
    gather(3, 3)
    gather(2, 4)
    lax.fori_loop(0, n_rb, project_v, 0)
    gather(3, 4)
    lax.fori_loop(0, n_ch, value_states, 0)
    pack_state(snd_b, cur_b)
    exchange_start(1, snd_b, rcv_b, True)
    gather(4, 1)
    lax.fori_loop(0, n_rb, project_q, 0)

    def two(x):
        return jnp.concatenate([x, x], axis=1)

    def stacks(x):
        return [stack2(a, left, right) for a in split(x)]

    def numerators(c, _):
        at = rows_at(c, CH)
        m2 = two(msk[c])
        q, k2, w2 = split(qs[at, :]), stacks(kk_[at, :]), stacks(wb[at, :])
        sc = [mm_t(q[p], k2[p]).astype(BF16) * m2 for p in pairs]
        num[at, :] = jnp.concatenate([mm(sc[p], w2[p]) for p in pairs], axis=1)
        return 0

    lax.fori_loop(0, n_ch, numerators, 0)
    gather(5, 1)
    gather(4, 2)
    exchange_wait(0, snd_a, rcv_a, True)
    entering(rcv_a, e_a, True)
    exchange_wait(1, snd_b, rcv_b, True)
    entering(rcv_b, e_b, True)

    def mixture(c, _):
        at = rows_at(c, CH)
        reach = same(last_of(base - 1), last_of(base + c - 1))
        m2 = two(msk[c])
        gp = g_prev[c]
        gpw = wide(gp)
        z_in = z_st[pl.ds(c, 1), :] + reach * e_z[0:1, :]
        skw = [(s_kw[c, p].astype(F32) + reach * e_a[p]).astype(BF16) for p in pairs]
        swv = [(s_wv[c, p].astype(F32) + reach * e_b[p]).astype(BF16) for p in pairs]
        q = split(qs[at, :] * gpw)
        w2, v2 = stacks(wb[at, :]), stacks(vv_[at, :])
        iz = 1.0 / (inv_z[at, :] + gpw.astype(F32) * z_in)
        from_state = jnp.concatenate([mm(q[p], skw[p]) for p in pairs], axis=1)
        lg = (num[at, :] + from_state) * iz
        top = jnp.concatenate([per_head(jnp.max, a, -jnp.inf) for a in split(lg)], axis=1)
        ex = jnp.exp(lg - top)
        tot = jnp.concatenate([mm(a.astype(BF16), ones_diag) for a in split(ex)], axis=1)
        pr = ex / tot
        r = (pr * iz).astype(BF16)
        rs, rg = split(r), split(r * gpw)
        mix = [mm_t(rs[p], w2[p]).astype(BF16) * m2 for p in pairs]
        o = jnp.concatenate([mm(mix[p], v2[p]) + mm(rg[p], swv[p]) for p in pairs], axis=1)
        for p in pairs:
            s_kw[c, p] = skw[p]
            s_wv[c, p] = swv[p]
        num[at, :] = lg
        inv_z[at, :] = iz
        prob[at, :] = pr
        rr_[at, :] = r
        oo_[at, :] = o.astype(BF16)

        @pl.when(c == n_ch // 2)
        def _():
            gather(5, 2)
            gather(4, 3)

        return 0

    lax.fori_loop(0, n_ch, mixture, 0)
    gather(5, 3)
    gather(4, 4)

    def up_w(j):
        return weight(U0 + 16 * j)

    def down_w(j):
        return g[j // 2, j % 2, :, :, W0:END, :].reshape(D, D)

    c0, c1 = math.sqrt(2.0 / math.pi), 0.044715

    def hidden(i, _):
        at = rows_at(i)
        h = xb[at, :].astype(F32) + mm(oo_[at, :], weight(O0))
        hsum[at, :] = h
        nh, _r = norm_stats(h)
        n = (nh * gain2 + bias2).astype(BF16)
        n2[at, :] = n
        n2t[:, at] = n.T
        return 0

    def feed(i, _):
        at = rows_at(i)
        n, gr = n2[at, :], og[at, :]
        for j in range(4):
            u = mm(n, up_w(j))
            dg = mm_t(gr, down_w(j)).astype(BF16).astype(F32)
            sq = u * u
            t = jnp.tanh(c0 * u * (1.0 + c1 * sq))
            half = 0.5 * (1.0 + t)
            slope = half + 0.5 * u * (1.0 - t * t) * (c0 * (1.0 + 3.0 * c1 * sq))
            act[at, D * j : D * j + D] = (u * half).astype(BF16)
            du[at, D * j : D * j + D] = (dg * slope).astype(BF16)
        return 0

    lax.fori_loop(0, n_rb, hidden, 0)
    loaded("og")
    gather(5, 4)
    lax.fori_loop(0, n_rb, feed, 0)

    def put_grad(r0, y, val):
        pg[y, :, :, :, r0 : r0 + 16, :] = val.astype(BF16).reshape(2, 2, 4, 16, D)

    def down_grads(m, _):
        val = t_mm(act[:, pl.ds(pl.multiple_of(m * 256, 256), 256)], og[...])
        pg[m // 4, lax.rem(m // 2, 2), lax.rem(m, 2), :, W0:END, :] = val.astype(BF16).reshape(4, 64, D)
        return 0

    def up_grads(j, _):
        for y in range(2):
            val = mm(n2t[256 * y : 256 * y + 256, :], du[:, pl.ds(pl.multiple_of(j * D, D), D)])
            pg[y, :, :, :, pl.ds(pl.multiple_of(U0 + 16 * j, 16), 16), :] = val.astype(BF16).reshape(2, 2, 4, 16, D)
        return 0

    def out_copy(ref):
        i = [ref is a for a in grad_s].index(True)
        return pltpu.make_async_copy(ref, grad_h[i], out_sem.at[i])

    def store(ref):
        out_copy(ref).start()

    def add_to(dst, src):
        dst[...] = (dst[...].astype(F32) + src[...].astype(F32)).astype(BF16)

    def scatter_copies(p, stage):
        put = lambda src, dst, idx, where: remote(src, dst, rs_send, rs_recv, p * 8 + idx, where)
        if p == G_NORM:
            if stage == 0:
                return [put(ngp.at[:, :, 1 - pc], nrc, 0, at_c)]
            if stage == 1:
                return [put(ngp.at[:, 1 - px, pc], nrx, 1, at_x)]
            if stage == 2:
                return [put(ngp.at[1 - py, px, pc], nry, 2, at_y)]
            return [put(ngp.at[py, px, pc, lax.rem(z + s, n_slot)], nrz.at[s - 1], 4 + s, at_z(s)) for s in range(1, n_slot)]
        r0, r1 = SCATTER[p]
        sl = pl.ds(r0, r1 - r0)
        if stage == 0:
            return [put(pg.at[:, :, 1 - pc, :, sl, :], rc.at[:, :, :, sl, :], 0, at_c)]
        if stage == 1:
            return [
                put(pg.at[:, 1 - px, pc, :, sl, la], rx1.at[:, :, sl, :], 1, at_x),
                put(pg.at[1 - py, :, pc, :, sl, lb], ry1.at[:, :, sl, :], 2, at_y),
            ]
        if stage == 2:
            return [
                put(pg.at[1 - py, px, pc, :, sl, la], ry2.at[:, sl, :], 3, at_y),
                put(pg.at[py, 1 - px, pc, :, sl, lb], rx2.at[:, sl, :], 4, at_x),
            ]
        return [
            put(pg.at[py, px, pc, lax.rem(z + s, n_slot), sl, :], rz.at[s - 1, sl, :], 4 + s, at_z(s))
            for s in range(1, n_slot)
        ]

    def scatter_add(p, stage):
        if p == G_NORM:
            if stage == 1:
                for y in range(2):
                    for x in range(2):
                        add_to(ngp.at[y, x, pc], nrc.at[y, x])
            elif stage == 2:
                for y in range(2):
                    add_to(ngp.at[y, px, pc], nrx.at[y])
            elif stage == 3:
                add_to(ngp.at[py, px, pc], nry)
            else:
                total = ngp[py, px, pc, z].astype(F32)
                for s in range(1, n_slot):
                    total = total + nrz[s - 1].astype(F32)
                ng_o[...] = total
                store(ng_o)
            return
        r0, r1 = SCATTER[p]
        sl = pl.ds(r0, r1 - r0)
        if stage == 1:
            def body(i, _):
                y, x = i // 2, lax.rem(i, 2)
                add_to(pg.at[y, x, pc, :, sl, :], rc.at[y, x, :, sl, :])
                return 0
            lax.fori_loop(0, 4, body, 0)
        elif stage == 2:
            def body(i, _):
                add_to(pg.at[i, px, pc, :, sl, la], rx1.at[i, :, sl, :])
                add_to(pg.at[py, i, pc, :, sl, lb], ry1.at[i, :, sl, :])
                return 0
            lax.fori_loop(0, 2, body, 0)
        elif stage == 3:
            add_to(pg.at[py, px, pc, :, sl, la], ry2.at[:, sl, :])
            add_to(pg.at[py, px, pc, :, sl, lb], rx2.at[:, sl, :])
        else:
            total = pg[py, px, pc, z, sl, :].astype(F32)
            for s in range(1, n_slot):
                total = total + rz[s - 1, sl, :].astype(F32)
            if p == G_DOWN:
                wd_o[...] = total
                store(wd_o)
            elif p == G_UP:
                wo_o[...] = total[0:16, :]
                for j in range(4):
                    wu_o[:, D * j : D * j + D] = total[16 + 16 * j : 32 + 16 * j, :]
                store(wo_o)
                store(wu_o)
            elif p == G_C:
                for i in range(4):
                    wc_o[16 * i : 16 * i + 16, :] = total[:, lanes(i)]
                store(wc_o)
            else:
                dst = {G_V: wv_o, G_Q: wq_o, G_K: wk_o}[p]
                dst[...] = total
                store(dst)

    def scatter(p, stage):
        if not comm:
            return
        if stage > 0:
            for copy in scatter_copies(p, stage - 1):
                copy.wait_recv()
            scatter_add(p, stage)
        if stage < 4:
            for copy in scatter_copies(p, stage):
                copy.start()

    lax.fori_loop(0, 8, down_grads, 0)
    scatter(G_DOWN, 0)
    lax.fori_loop(0, 4, up_grads, 0)
    scatter(G_DOWN, 1)

    def feed_back(i, acc):
        at = rows_at(i)
        dn = jnp.zeros((rb, D), F32)
        for j in range(4):
            dn = dn + mm_t(du[at, D * j : D * j + D], up_w(j))
        nh, rstd = norm_stats(hsum[at, :])
        dh = og[at, :].astype(F32) + norm_back(dn, nh, rstd, gain2)
        hid[at, :] = dh
        a = dh.astype(BF16)
        da[at, :] = a
        do[at, :] = mm_t(a, weight(O0)).astype(BF16)
        return (acc[0] + jnp.sum(dn * nh, axis=0, keepdims=True), acc[1] + jnp.sum(dn, axis=0, keepdims=True))

    zero_row = jnp.zeros((1, D), F32)
    gain2_g, bias2_g = lax.fori_loop(0, n_rb, feed_back, (zero_row, zero_row))
    for y in range(2):
        put_grad(O0, y, t_mm(oo_[:, 256 * y : 256 * y + 256], da[...]))
    scatter(G_UP, 0)

    cur_a[...] = jnp.zeros_like(cur_a)
    cur_b[...] = jnp.zeros_like(cur_b)
    cur_z[...] = jnp.zeros_like(cur_z)

    def slot_states(i, _):
        c = n_ch - 1 - i
        at = rows_at(c, CH)
        keep = same(first_of(base + c), first_of(base + c + 1))
        scan_step(cur_a, s_r, c, keep, rr_[at, :] * wide(g_first[c]), do[at, :])
        return 0

    lax.fori_loop(0, n_ch, slot_states, 0)
    pack_state(snd_d, cur_a)
    exchange_start(2, snd_d, rcv_d, False)
    scatter(G_UP, 1)

    def slot_grads(i, _):
        c = n_ch - 1 - i
        at = rows_at(c, CH)
        m2 = two(msk[c])
        gpw = wide(g_prev[c])
        keep = same(first_of(base + c), first_of(base + c + 1))
        w2, v2 = stacks(wb[at, :]), stacks(vv_[at, :])
        do_c = do[at, :]
        ds, dg = split(do_c), split(do_c * gpw)
        dmix = [mm_t(ds[p], v2[p]).astype(BF16) * m2 for p in pairs]
        dr = jnp.concatenate([mm(dmix[p], w2[p]) + mm_t(dg[p], s_wv[c, p]) for p in pairs], axis=1)
        iz, pr, lg = inv_z[at, :], prob[at, :], num[at, :]
        dpr = dr * iz
        inner = jnp.concatenate([mm(a.astype(BF16), ones_diag) for a in split(pr * dpr)], axis=1)
        dl = pr * (dpr - inner)
        dn_c = (dl * iz).astype(BF16)
        dz_c = (-(dpr * pr + dl * lg) * iz).astype(BF16)
        firsts = mm(mskt[c][0:16, :], dz_c)
        scan_step(cur_b, s_n, c, keep, qs[at, :] * wide(g_first[c]), dn_c)
        z_old = cur_z[0:1, :]
        z_r[pl.ds(c, 1), :] = z_old
        cur_z[0:1, :] = keep * z_old + firsts[0:1, :]
        dnum_[at, :] = dn_c
        dz_[at, :] = dz_c

        @pl.when(i == n_ch // 2)
        def _():
            scatter(G_DOWN, 2)

        return 0

    lax.fori_loop(0, n_ch, slot_grads, 0)
    pack_state(snd_c, cur_b)
    pack_row(snd_c, cur_z[0:1, :])
    exchange_start(3, snd_c, rcv_c, False)
    exchange_wait(2, snd_d, rcv_d, False)
    entering(rcv_d, e_b, False)
    scatter(G_UP, 2)

    def query_value_grads(c, _):
        at = rows_at(c, CH)
        reach = same(first_of(base + n_ch), first_of(base + c + 1))
        m2, mt2 = two(msk[c]), two(mskt[c])
        gpw, gnw = wide(g_prev[c]), wide(g_next[c])
        w_c, dn_c, do_c = wb[at, :], dnum_[at, :], do[at, :]
        w, wg, dn, dg = split(w_c), split(w_c * gnw), split(dn_c), split(dn_c * gpw)
        w2, k2, r2, do2 = stacks(w_c), stacks(kk_[at, :]), stacks(rr_[at, :]), stacks(do_c)
        st_r = [(s_r[c, p].astype(F32) + reach * e_b[p]).astype(BF16) for p in pairs]
        dsc = [mm_t(dn[p], w2[p]).astype(BF16) * m2 for p in pairs]
        mix_t = [mm_t(w[p], r2[p]).astype(BF16) * mt2 for p in pairs]
        dq = jnp.concatenate([mm(dsc[p], k2[p]) + mm_t(dg[p], s_kw[c, p]) for p in pairs], axis=1)
        dv = jnp.concatenate([mm(mix_t[p], do2[p]) + mm(wg[p], st_r[p]) for p in pairs], axis=1)
        for p in pairs:
            s_r[c, p] = st_r[p]
        dq_[at, :] = (dq * (HEAD_DIM**-0.5)).astype(BF16)
        dv_[at, :] = dv.astype(BF16)

        @pl.when(c == n_ch // 2)
        def _():
            scatter(G_DOWN, 3)

        return 0

    lax.fori_loop(0, n_ch, query_value_grads, 0)
    for y in range(2):
        cols = slice(256 * y, 256 * y + 256)
        put_grad(V0, y, mm(n1t[cols, :], dv_[...]))
        put_grad(Q0, y, mm(n1t[cols, :], dq_[...]))
    scatter(G_V, 0)
    scatter(G_Q, 0)
    scatter(G_UP, 3)
    exchange_wait(3, snd_c, rcv_c, False)
    entering(rcv_c, e_a, False)
    scatter(G_V, 1)
    scatter(G_Q, 1)

    def key_slot_grads(c, _):
        at = rows_at(c, CH)
        reach = same(first_of(base + n_ch), first_of(base + c + 1))
        mt = mskt[c]
        mt2 = two(mt)
        gnw = wide(g_next[c])
        z_in = z_r[pl.ds(c, 1), :] + reach * e_z[0:1, :]
        w_c, v_c, k_c = wb[at, :], vv_[at, :], kk_[at, :]
        w, v, k, wg, vg, kg = (split(a) for a in (w_c, v_c, k_c, w_c * gnw, v_c * gnw, k_c * gnw))
        q2, dn2, r2, do2 = (stacks(ref[at, :]) for ref in (qs, dnum_, rr_, do))
        st_n = [(s_n[c, p].astype(F32) + reach * e_a[p]).astype(BF16) for p in pairs]
        st_r = [s_r[c, p] for p in pairs]
        dsc_t = [mm_t(w[p], dn2[p]).astype(BF16) * mt2 for p in pairs]
        dmix_t = [mm_t(v[p], do2[p]).astype(BF16) * mt2 for p in pairs]
        sc_t = [mm_t(k[p], q2[p]).astype(BF16) * mt2 for p in pairs]
        dk = jnp.concatenate([mm(dsc_t[p], q2[p]) + mm_t(wg[p], st_n[p]) for p in pairs], axis=1)
        dw = mm(mt, dz_[at, :]) + gnw.astype(F32) * z_in
        dw = dw + jnp.concatenate(
            [mm(dmix_t[p], r2[p]) + mm_t(vg[p], st_r[p]) + mm(sc_t[p], dn2[p]) + mm(kg[p], st_n[p]) for p in pairs], axis=1
        )
        dk_[at, :] = dk.astype(BF16)
        dphi_[at, :] = (dw * ew[at, :]).astype(BF16)

        @pl.when(c == n_ch // 2)
        def _():
            scatter(G_DOWN, 4)
            scatter(G_V, 2)
            scatter(G_Q, 2)

        return 0

    lax.fori_loop(0, n_ch, key_slot_grads, 0)
    scatter(G_UP, 4)

    for y in range(2):
        cols = slice(256 * y, 256 * y + 256)
        val = mm_t(mm(n1t[cols, :], dphi_[...]).astype(BF16), permutation()).astype(BF16)
        for x in range(2):
            for c in range(2):
                for i in range(4):
                    r = ((x * 2 + c) * 4 + i) * 16
                    for j in range(4):
                        pg[y, x, c, j, C0 : C0 + 16, CH * i : CH * i + CH] = val[r : r + 16, lanes(j)]
    scatter(G_C, 0)
    for y in range(2):
        put_grad(K0, y, mm(n1t[256 * y : 256 * y + 256, :], dk_[...]))
    scatter(G_K, 0)
    scatter(G_C, 1)
    scatter(G_V, 3)
    scatter(G_K, 1)
    scatter(G_Q, 3)

    def input_grads(i, acc):
        at = rows_at(i)
        dn = mm_t(dq_[at, :], weight(Q0)) + mm_t(dk_[at, :], weight(K0)) + mm_t(dv_[at, :], weight(V0)) + mm_t(dphi_[at, :], wc_s[...])
        nh, rstd = norm_stats(xb[at, :].astype(F32))
        tg_o[at, :] = hid[at, :] + norm_back(dn, nh, rstd, gain1)
        return (acc[0] + jnp.sum(dn * nh, axis=0, keepdims=True), acc[1] + jnp.sum(dn, axis=0, keepdims=True))

    def outputs(i, _):
        at = rows_at(i)
        out = hsum[at, :]
        for j in range(4):
            out = out + mm(act[at, D * j : D * j + D], down_w(j))
        out_o[at, :] = out.astype(BF16)
        return 0

    gain1_g, bias1_g = lax.fori_loop(0, n_rb, input_grads, (zero_row, zero_row))
    tg_copy = pltpu.make_async_copy(tg_o, tg_h, out_sem.at[8])
    tg_copy.start()
    norm_g = jnp.concatenate([gain1_g, bias1_g, gain2_g, bias2_g, jnp.zeros((12, D), F32)], axis=0)
    if comm:
        for y in range(2):
            for x in range(2):
                for c in range(2):
                    for j in range(4):
                        d = ((y * 2 + x) * 2 + c) * 4 + j
                        ngp[y, x, c, j] = norm_g[:, lanes(d // 8)].astype(BF16)
    else:
        ng_o[...] = norm_g
    scatter(G_NORM, 0)
    scatter(G_C, 2)
    scatter(G_K, 2)
    scatter(G_NORM, 1)
    lax.fori_loop(0, n_rb, outputs, 0)
    out_done = pltpu.make_async_copy(out_o, out_h, out_sem.at[9])
    out_done.start()
    scatter(G_NORM, 2)
    scatter(G_C, 3)
    scatter(G_K, 3)
    scatter(G_NORM, 3)
    for p in (G_V, G_Q, G_C, G_K, G_NORM):
        scatter(p, 4)

    tg_copy.wait()
    out_done.wait()
    if comm:
        for ref in grad_s:
            out_copy(ref).wait()
        for stage in range(4):
            for p in range(len(GATHER)):
                for copy in gather_copies(p, stage):
                    copy.wait_send()
            for p in range(len(SCATTER) + 1):
                for copy in scatter_copies(p, stage):
                    copy.wait_send()


def vm(shape, dtype):
    return pltpu.VMEM(shape, dtype)


def run_layer(rows, n_slot, seg_rows, comm, operands):
    n_ch = rows // CH
    act_shape = (rows, D)
    hbm, vmem = pl.BlockSpec(memory_space=pl.ANY), pl.BlockSpec(memory_space=pltpu.VMEM)
    sds = jax.ShapeDtypeStruct
    outs = [sds(act_shape, BF16), sds(act_shape, F32)]
    grads = [(16, D)] * 4 + [(64, CH), (16, FF), (64, D), (16, CH)]
    if comm:
        outs += [sds(shape, F32) for shape in grads]
        out_specs = [hbm] * len(outs)
    else:
        outs += [sds((*GRID, END, D), BF16), sds((16, D), F32)]
        out_specs = [hbm, hbm, vmem, vmem]
    b, f = (lambda: vm(act_shape, BF16)), (lambda: vm(act_shape, F32))
    state = lambda dtype: vm((n_ch, PAIRS, CH, CH), dtype)
    sems = lambda n: pltpu.SemaphoreType.DMA((n,))
    scratch = [
        vm((*GRID, END, D), BF16), b(), vm((seg_rows, CH), jnp.int32), b(), b(), b(), b(), b(), b(),
        f(), f(), f(), f(), b(), b(), f(), b(), vm((rows, FF), BF16), vm((rows, FF), BF16), b(), b(),
        vm((D, rows), BF16), vm((D, rows), BF16), b(), b(), b(), b(), f(),
        state(BF16), state(BF16), vm((max(8, n_ch), D), F32), state(BF16), state(BF16), vm((max(8, n_ch), D), F32),
        vm((PAIRS, CH, CH), F32), vm((PAIRS, CH, CH), F32), vm((8, D), F32),
        vm((PAIRS, CH, CH), F32), vm((PAIRS, CH, CH), F32), vm((8, D), F32),
    ]
    scratch += [vm((n_ch, CH, CH), BF16)] * 6
    long, short = (272, CH), (256, CH)
    scratch += [vm(long, BF16), vm(short, BF16), vm((n_slot, *long), BF16), vm((n_slot, *short), BF16)] * 2
    scratch += [vm((D, D), BF16), sems(4 * n_slot), sems(4 * n_slot), sems(20), sems(10)]
    if comm:
        ny, nx, nc, nz = GRID
        scratch += [
            vm((*GRID, END, D), BF16), vm((*GRID, 16, CH), BF16),
            vm((ny, nx, nz, END, D), BF16), vm((ny, nz, END, D // 2), BF16), vm((nx, nz, END, D // 2), BF16),
            vm((nz, END, D // 2), BF16), vm((nz, END, D // 2), BF16), vm((nz - 1, END, D), BF16),
            vm((ny, nx, nz, 16, CH), BF16), vm((ny, nz, 16, CH), BF16), vm((nz, 16, CH), BF16), vm((nz - 1, 16, CH), BF16),
        ]
        scratch += [sems(8 * 6)] * 2 + [sems(8 * 7)] * 2
        scratch += [vm(operands[7].shape, BF16), vm((4, 1, operands[-1].shape[1]), BF16)] + [vm(shape, F32) for shape in grads]
    cfg = dict(rows=rows, n_slot=n_slot, comm=comm)
    return pl.pallas_call(
        functools.partial(kernel_body, cfg),
        out_shape=outs,
        in_specs=[hbm] * len(operands),
        out_specs=out_specs,
        scratch_shapes=scratch,
        compiler_params=pltpu.CompilerParams(collective_id=0, has_side_effects=True, vmem_limit_bytes=63 * 2**20),
    )(*operands)


def finish_body(*refs):
    src, dst, rest = refs[:10], refs[10:23], refs[23:]
    *held, sem_in, sem_out = rest
    jobs = [(1, 0), (1, 1), (0, 0), (0, 1)] + [(i, None) for i in (2, 3, 4, 5, 7, 8)]

    def copy(k, come):
        i, part = jobs[k]
        buf = held[(0, 1, 2, 3, 4, 5, None, 6, 7)[i]]
        cut = lambda ref: ref if part is None else ref.at[pl.ds(part * (ref.shape[0] // 2), ref.shape[0] // 2)]
        if come:
            return pltpu.make_async_copy(cut(src[i]), cut(buf), sem_in.at[k])
        return pltpu.make_async_copy(cut(buf), cut(dst[i]), sem_out.at[k])

    for k in range(len(jobs)):
        copy(k, True).start()
    dst[6][...] = src[6][...].T
    wide = dst[9].shape[1]
    dev = lax.axis_index("dp") * lax.axis_size("slot") + lax.axis_index("slot")
    vals = pltpu.roll(src[9][...], lax.rem(CH - wide * lax.rem(dev, CH // wide), CH), 1)
    for i in range(4):
        dst[9 + i][...] = vals[i : i + 1, 0:wide]
    for k in range(len(jobs)):
        copy(k, True).wait()
        copy(k, False).start()
    for k in range(len(jobs)):
        copy(k, False).wait()


def finish(outs, wide):
    hbm, vmem = pl.BlockSpec(memory_space=pl.ANY), pl.BlockSpec(memory_space=pltpu.VMEM)
    sds = jax.ShapeDtypeStruct
    shapes = [sds(a.shape, a.dtype) for a in outs[:9]] + [sds((1, wide), F32)] * 4
    shapes[6] = sds(outs[6].shape[::-1], F32)
    return pl.pallas_call(
        finish_body,
        out_shape=shapes,
        in_specs=[vmem if i in (6, 9) else hbm for i in range(10)],
        out_specs=[vmem if i == 6 or i > 8 else hbm for i in range(13)],
        scratch_shapes=[vm(outs[i].shape, outs[i].dtype) for i in (0, 1, 2, 3, 4, 5, 7, 8)] + [pltpu.SemaphoreType.DMA((10,))] * 2,
        compiler_params=pltpu.CompilerParams(vmem_limit_bytes=63 * 2**20),
    )(*outs)


def layer(
    tokens, segment_ids, w_query, w_key, w_value, w_out, w_control, w_up, w_down,
    norm1_gain, norm1_bias, norm2_gain, norm2_bias, out_grad,
):
    n_slot, n_dp = lax.axis_size("slot"), lax.axis_size("dp")
    n_dev = n_slot * n_dp
    rows = tokens.shape[0] // n_slot
    seg = segment_ids.reshape(-1, CH)
    norms = (norm1_gain, norm1_bias, norm2_gain, norm2_bias)
    if n_dev == math.prod(GRID) and n_slot == GRID[3]:
        outs = run_layer(rows, n_slot, seg.shape[0], True, (
            tokens, seg, out_grad, w_query, w_key, w_value, w_out,
            w_control.transpose(1, 2, 0).reshape(CH, -1), w_up, w_down, *(a.reshape(1, -1) for a in norms),
        ))
        outs = finish(outs, norm1_gain.shape[0])
        control = outs[6].reshape(*w_control.shape[1:], -1).transpose(2, 0, 1)
        return (*outs[:6], control, *outs[7:9], *(a.reshape(-1) for a in outs[9:]))

    norms = jnp.stack(norms)
    both = ("dp", "slot")
    gather = lambda a: lax.all_gather(a, both, axis=0, tiled=True)
    n_blk = math.prod(GRID)
    wc = lax.all_gather(lax.all_gather(w_control, "dp", axis=0, tiled=True), "slot", axis=2, tiled=True)
    gw = SLOTS // GRID[3]
    wc = wc.reshape(8, 4, 16, HEADS, GRID[3], gw).transpose(0, 4, 2, 1, 3, 5).reshape(n_blk, 16, D)
    norm_all = lax.all_gather(norms, both, axis=1, tiled=True)
    norm_blk = jnp.zeros((n_blk, 16, D), BF16).at[0, :4].set(norm_all)
    split = lambda a: gather(a).reshape(n_blk, -1, D)
    up = gather(w_up).reshape(n_blk, 16, 4, D).transpose(0, 2, 1, 3).reshape(n_blk, 64, D)
    packed = jnp.concatenate(
        [split(w_key), norm_blk, wc, split(w_value), split(w_query), split(w_out), up, split(w_down)], axis=1
    ).reshape(*GRID, END, D)
    out, tg, part, ng = run_layer(rows, n_slot, seg.shape[0], False, (tokens, seg, out_grad, packed))
    part = part.reshape(n_blk, END, D).astype(F32)
    scatter = lambda a, dim=0: lax.psum_scatter(a, both, scatter_dimension=dim, tiled=True)
    full = lambda r0, r1: part[:, r0:r1].reshape(-1, D)
    wcg = part[:, C0:V0].reshape(8, GRID[3], 16, 4, HEADS, gw).transpose(0, 3, 2, 4, 1, 5).reshape(D, HEADS, SLOTS)
    wcg = lax.psum_scatter(lax.psum_scatter(wcg, "dp", scatter_dimension=0, tiled=True), "slot", scatter_dimension=2, tiled=True)
    upg = part[:, U0:W0].reshape(n_blk, 4, 16, D).transpose(0, 2, 1, 3).reshape(D, FF)
    ng = scatter(ng[:4], 1)
    return (
        out, tg, scatter(full(Q0, O0)), scatter(full(K0, N0)), scatter(full(V0, Q0)), scatter(full(O0, U0)),
        wcg, scatter(upg), scatter(full(W0, END)), ng[0], ng[1], ng[2], ng[3],
    )


def solution(mesh):
    both = P(("dp", "slot"), None)
    vec = P(("dp", "slot"))
    control = P("dp", None, "slot")
    in_specs = (
        P("dp", None), P("dp"), both, both, both, both, control, both, both, vec, vec, vec, vec, both,
    )
    out_specs = (both, both, both, both, both, both, control, both, both, vec, vec, vec, vec)
    return jax.shard_map(layer, mesh=mesh, in_specs=in_specs, out_specs=out_specs, check_vma=False)
```

```python
import functools
import math

import jax
import jax.numpy as jnp
from jax import lax
from jax.experimental import pallas as pl
from jax.experimental.pallas import tpu as pltpu
from jax.sharding import PartitionSpec as P

D = 512
HEADS = 8
HEAD_DIM = 64
SLOTS = 64
FF = 2048
EPS = 1e-05
CH = 128
PAIRS = HEADS // 2
F32 = jnp.float32
BF16 = jnp.bfloat16
MESH = pl.DeviceIdType.MESH

K0, C0, V0, Q0, O0, U0, W0, END = 0, 16, 32, 48, 64, 80, 144, 208
GRID = (2, 2, 2, 4)
ROWS = ((K0, C0), (C0, V0), (V0, Q0), (Q0, O0), (O0, U0), (U0, U0 + 32), (U0 + 32, W0), (W0, END))
PK, PC, PV, PQ, PO, PU, PU2, PW, PN = range(9)


def mm(a, b):
    return jnp.dot(a, b, preferred_element_type=F32)


def mm_t(a, b):
    return lax.dot_general(a, b, (((1,), (1,)), ((), ())), preferred_element_type=F32)


def t_mm(a, b):
    return lax.dot_general(a, b, (((0,), (0,)), ((), ())), preferred_element_type=F32)


def half_lanes(dtype):
    lane = lax.broadcasted_iota(jnp.int32, (1, CH), 1)
    left = jnp.where(lane < HEAD_DIM, 1.0, 0.0)
    return left.astype(dtype), (1.0 - left).astype(dtype)


def stack2(x, left, right):
    return jnp.concatenate([x * left, x * right], axis=0)


def per_head(op, x, fill):
    lane = lax.broadcasted_iota(jnp.int32, x.shape, 1)
    first = lane < HEAD_DIM
    a = op(jnp.where(first, x, fill), axis=1, keepdims=True)
    b = op(jnp.where(first, fill, x), axis=1, keepdims=True)
    return jnp.where(first, a, b)


def norm_stats(x):
    center = x - jnp.mean(x, axis=-1, keepdims=True)
    rstd = lax.rsqrt(jnp.mean(center * center, axis=-1, keepdims=True) + EPS)
    return center * rstd, rstd


def norm_back(dn, nh, rstd, gain):
    e = dn * gain
    return (e - jnp.mean(e, axis=-1, keepdims=True) - nh * jnp.mean(e * nh, axis=-1, keepdims=True)) * rstd


def kernel_body(cfg, *refs):
    refs = list(refs)
    take = lambda n: [refs.pop(0) for _ in range(n)]
    rows, n_slot, comm = cfg["rows"], cfg["n_slot"], cfg["comm"]
    n_ch = rows // CH
    rb = rows if rows <= 768 else 256
    n_rb = rows // rb
    (tok_in, seg_in, og_in) = take(3)
    if comm:
        (wq_in, wk_in, wv_in, wo_in, wc_in, wu_in, wd_in, *norm_in) = take(11)
        out_h, tg_h, *grad_h = take(10)
    else:
        (g_in, gn_in) = take(2)
        (out_h, tg_h, pg, ng_o) = take(4)
    (g, gn, xb, seg, og, n1, qs, kk_, vv_, wb, ew, num, inv_z, prob, rr_, oo_, hid, n2, act, du, da, do) = take(22)
    (n1t, n2t, dq_, dk_, dv_, dphi_, hsum) = take(7)
    (s_kw, s_wv, z_st, s_r, s_n, z_r) = take(6)
    (cur_a, cur_b, cur_z, e_a, e_b, e_z) = take(6)
    (msk, mskt, g_prev, g_last, g_next, g_first) = take(6)
    (snd_a, snd_b, rcv_a, rcv_b, snd_c, snd_d, rcv_c, rcv_d) = take(8)
    (wc_s, st_send, st_recv, in_sem, out_sem) = take(5)
    if comm:
        (pg, ngp, rc, rx1, ry1, ry2, rx2, rz, nrc, nrx, nry, nrz) = take(12)
        (ag_send, ag_recv, rs_send, rs_recv) = take(4)
        (wct, nv) = take(2)
        grad_s = take(8)
        (wq_o, wk_o, wv_o, wo_o, wc_o, wu_o, wd_o, ng_o) = grad_s
    assert not refs
    tg_o, out_o = prob, oo_
    dnum_, dz_ = du.at[:, 0:D], du.at[:, D : 2 * D]

    dp = lax.axis_index("dp")
    z = lax.axis_index("slot")
    left, right = half_lanes(BF16)
    leftf, rightf = half_lanes(F32)
    ri = lax.broadcasted_iota(jnp.int32, (CH, CH), 0)
    ci = lax.broadcasted_iota(jnp.int32, (CH, CH), 1)
    block_diag = jnp.where((ri < HEAD_DIM) == (ci < HEAD_DIM), 1.0, 0.0).astype(F32)
    ones_diag = block_diag.astype(BF16)
    pairs = range(PAIRS)

    if comm:
        ny, nx, nc, nz = GRID
        py, px, pc = dp // (nx * nc), lax.rem(dp // nc, nx), lax.rem(dp, nc)
        at_x = ((py * nx + (1 - px)) * nc + pc, z)
        at_y = (((1 - py) * nx + px) * nc + pc, z)
        at_c = ((py * nx + px) * nc + (1 - pc), z)

    def at_z(s):
        return (dp, lax.rem(z + s, n_slot))

    def remote(src, dst, send_sem, recv_sem, idx, where):
        return pltpu.make_async_remote_copy(
            src_ref=src, dst_ref=dst, send_sem=send_sem.at[idx], recv_sem=recv_sem.at[idx],
            device_id=where, device_id_type=MESH,
        )

    loads = {}

    def load(name, src, dst):
        copy = pltpu.make_async_copy(src, dst, in_sem.at[sum(map(len, loads.values()))])
        copy.start()
        loads.setdefault(name, []).append(copy)

    def loaded(name):
        for copy in loads.get(name, ()):
            copy.wait()

    if comm:
        my = g.at[py, px, pc, z]
        load(PK, wk_in, my.at[K0:C0])
        for i, ref in enumerate(norm_in):
            load(PN, ref, nv.at[i])
        load(PC, wc_in, wct)
        load(PV, wv_in, my.at[V0:Q0])
        load(PQ, wq_in, my.at[Q0:O0])
    else:
        load(PK, g_in, g)
        load(PK, gn_in, gn)
    load("tok", tok_in.at[pl.ds(pl.multiple_of(z * rows, CH), rows)], xb)
    load("seg", seg_in, seg)
    if comm:
        load(PO, wo_in, my.at[O0:U0])
        load(PW, wd_in, my.at[W0:END])
        for i in range(4):
            load(PU if i < 2 else PU2, wu_in.at[:, D * i : D * i + D], my.at[U0 + 16 * i : U0 + 16 * i + 16])
    load("og", og_in, og)

    for ref in (rcv_a, rcv_b, rcv_c, rcv_d):
        ref[...] = jnp.zeros_like(ref)
    bar = pltpu.get_barrier_semaphore()
    peers = [at_z(s) for s in range(1, n_slot)]
    if comm:
        peers += [at_x, at_y, at_c]
    for peer in peers:
        pl.semaphore_signal(bar, inc=1, device_id=peer, device_id_type=MESH)
    pl.semaphore_wait(bar, len(peers))

    la, lb = pl.ds(0, D // 2), pl.ds(D // 2, D // 2)

    def gather_copies(p, stage):
        put = lambda ref, idx, where, src=None: remote(ref if src is None else src, ref, ag_send, ag_recv, p * 8 + idx, where)
        if p == PN:
            if stage == 0:
                return [put(gn.at[py, px, pc, z], s - 1, at_z(s)) for s in range(1, n_slot)]
            return [put(*((gn.at[py, px, pc], 3, at_x), (gn.at[py, :, pc], 5, at_y), (gn.at[:, :, pc], 7, at_c))[stage - 1])]
        r0, r1 = ROWS[p]
        sl = pl.ds(r0, r1 - r0)
        if stage == 0:
            src = wk_in if p == PK else None
            return [put(g.at[py, px, pc, z, sl], s - 1, at_z(s), src) for s in range(1, n_slot)]
        if stage == 1:
            return [put(g.at[py, px, pc, :, sl, la], 3, at_x), put(g.at[py, px, pc, :, sl, lb], 4, at_y)]
        if stage == 2:
            return [put(g.at[py, :, pc, :, sl, la], 5, at_y), put(g.at[:, px, pc, :, sl, lb], 6, at_x)]
        return [put(g.at[:, :, pc, :, sl, :], 7, at_c)]

    def gather(p, stage):
        if not comm:
            return
        if stage == 0:
            if p not in (PK, PC, PN):
                loaded(p)
        else:
            for copy in gather_copies(p, stage - 1):
                copy.wait_recv()
        if stage < 4:
            for copy in gather_copies(p, stage):
                copy.start()

    def weight(r0):
        return g[:, :, :, :, r0 : r0 + 16, :].reshape(D, D)

    gather(PK, 0)
    if comm:
        loaded(PN)
        each = nv.shape[2]
        dev = dp * n_slot + z
        vals = [nv[i].astype(F32) for i in range(4)] + [jnp.zeros((12, each), F32)]
        a = lax.broadcasted_iota(jnp.int32, (each, CH), 0)
        b = lax.broadcasted_iota(jnp.int32, (each, CH), 1)
        place = jnp.where(b == a + each * lax.rem(dev, CH // each), 1.0, 0.0).astype(BF16)
        a = lax.broadcasted_iota(jnp.int32, (16, 16), 0)
        b = lax.broadcasted_iota(jnp.int32, (16, 16), 1)
        down = jnp.where(a == b + 4 * (dev // (CH // each)), 1.0, 0.0).astype(BF16)
        vals = mm(jnp.concatenate(vals, axis=0).astype(BF16), place).astype(BF16)
        gn[py, px, pc, z] = mm(down, vals).astype(BF16)
        gather(PN, 0)
        loaded(PC)
        a = lax.broadcasted_iota(jnp.int32, (wct.shape[1], wct.shape[1]), 0)
        b = lax.broadcasted_iota(jnp.int32, (wct.shape[1], wct.shape[1]), 1)
        flat = mm_t(jnp.where(a == b, 1.0, 0.0).astype(BF16), wct[...]).astype(BF16)
        for i in range(4):
            my[C0:V0, CH * i : CH * i + CH] = flat[16 * i : 16 * i + 16, :]
        gather(PC, 0)
        loaded(PK)
    else:
        loaded(PK)

    seg_rows = seg.shape[0]

    def seg_row(i):
        return seg[pl.ds(jnp.clip(i, 0, seg_rows - 1), 1), :].astype(F32)

    def first_of(i):
        return seg_row(i)[:, 0:1]

    def last_of(i):
        return seg_row(i)[:, CH - 1 : CH]

    base = z * n_ch

    def same(a, b):
        return jnp.where(a == b, 1.0, 0.0).astype(F32)

    def rows_at(i, n=rb):
        return pl.ds(i * n if isinstance(i, int) else pl.multiple_of(i * n, n), n)

    def chunks(step):
        for i in range(n_ch):
            step(i)

    def make_masks(c):
        row = jnp.broadcast_to(seg_row(base + c), (CH, CH))
        col = row.T
        eq = row == col
        msk[c] = jnp.where(eq & (ci <= ri), 1.0, 0.0).astype(BF16)
        mskt[c] = jnp.where(eq & (ri <= ci), 1.0, 0.0).astype(BF16)
        g_prev[c] = same(col, last_of(base + c - 1)).astype(BF16)
        g_last[c] = same(col, last_of(base + c)).astype(BF16)
        g_next[c] = same(col, first_of(base + c + 1)).astype(BF16)
        g_first[c] = same(col, first_of(base + c)).astype(BF16)

    def center(i, _):
        at = rows_at(i)
        nh, _r = norm_stats(xb[at, :].astype(F32))
        hid[at, :] = nh
        return 0

    loaded("seg")
    chunks(make_masks)
    loaded("tok")
    lax.fori_loop(0, n_rb, center, 0)
    for p in (PN, PK, PC):
        gather(p, 1)
    for p in (PV, PQ):
        gather(p, 0)
    for p in (PN, PK, PC):
        gather(p, 2)
    for p in (PV, PQ):
        gather(p, 1)
    for p in (PO, PW, PU):
        gather(p, 0)
    for p in (PN, PK, PC):
        gather(p, 3)
    for p in (PV, PQ):
        gather(p, 2)
    for p in (PN, PK):
        gather(p, 4)

    norms = jnp.sum(gn[...].astype(F32).reshape(math.prod(GRID), 16, CH), axis=0)
    gain1, bias1, gain2, bias2 = (
        jnp.concatenate([norms[4 * q + i : 4 * q + i + 1, :] for q in range(4)], axis=1) for i in range(4)
    )

    def project_k(i, _):
        at = rows_at(i)
        n = (hid[at, :] * gain1 + bias1).astype(BF16)
        n1[at, :] = n
        n1t[:, at] = n.T
        kk_[at, :] = mm(n, weight(K0)).astype(BF16)
        return 0

    lax.fori_loop(0, n_rb, project_k, 0)
    gather(PC, 4)

    def permutation():
        gw = SLOTS // GRID[3]
        a = lax.broadcasted_iota(jnp.int32, (D, D), 0)
        b = lax.broadcasted_iota(jnp.int32, (D, D), 1)
        h, s = b // SLOTS, lax.rem(b, SLOTS)
        src = (s // gw) * (HEADS * gw) + h * gw + lax.rem(s, gw)
        return jnp.where(a == src, 1.0, 0.0).astype(BF16)

    def control_weight():
        parts = []
        for y in range(2):
            for x in range(2):
                for c in range(2):
                    for i in range(4):
                        tiles = [g[y, x, c, j, C0 : C0 + 16, CH * i : CH * i + CH] for j in range(4)]
                        parts.append(jnp.concatenate(tiles, axis=1))
        return jnp.concatenate(parts, axis=0)

    wc_s[...] = mm(control_weight(), permutation()).astype(BF16)

    def project_c(i, _):
        at = rows_at(i)
        e = jnp.exp(mm(n1[at, :], wc_s[...]))
        ew[at, :] = e
        wb[at, :] = e.astype(BF16)
        return 0

    def project_v(i, _):
        at = rows_at(i)
        vv_[at, :] = mm(n1[at, :], weight(V0)).astype(BF16)
        return 0

    def project_q(i, _):
        at = rows_at(i)
        qs[at, :] = (mm(n1[at, :], weight(Q0)).astype(BF16) * (HEAD_DIM**-0.5)).astype(BF16)
        return 0

    def lanes(p):
        return slice(CH * p, CH * p + CH)

    def split(x):
        return [x[:, lanes(p)] for p in pairs]

    def compact(x):
        return x[0:HEAD_DIM, :] + x[HEAD_DIM:CH, :]

    def expand(x):
        return jnp.concatenate([x * leftf, x * rightf], axis=0)

    def pack_row(ref, row):
        hi = row.astype(BF16).astype(F32)
        lo = row - hi
        parts = [a[:, lanes(p)] for a in (hi, lo) for p in pairs]
        parts.append(jnp.zeros((8, CH), F32))
        ref[256:272, :] = jnp.concatenate(parts, axis=0).astype(BF16)

    def unpack_row(x):
        x = x.astype(F32)
        x = x[0:PAIRS, :] + x[PAIRS : 2 * PAIRS, :]
        return jnp.concatenate([x[p : p + 1, :] for p in pairs], axis=1)

    def wide(x):
        return jnp.concatenate([x] * PAIRS, axis=1)

    def scan_step(cur, saved, c, keep, rows_a, rows_b):
        new = [t_mm(a, b) * block_diag for a, b in zip(split(rows_a), split(rows_b))]
        old = [cur[p] for p in pairs]
        for p in pairs:
            saved[c, p] = old[p].astype(BF16)
        for p in pairs:
            cur[p] = keep * old[p] + new[p]

    def place(up):
        return z if up else n_slot - 1 - z

    def toward(up, s):
        return (dp, z + s if up else z - s)

    def edge_gate(up, far):
        if up:
            return same(last_of(base - (far - 1) * n_ch - 1), last_of(base - (far - 2) * n_ch - 1))
        return same(first_of(base + far * n_ch), first_of(base + (far - 1) * n_ch))

    def exchange_copy(idx, src, dst, up, step):
        k = idx * max(n_slot, 4) + step
        if n_slot == 4:
            return remote(src, dst.at[0 if step == 0 else 1], st_send, st_recv, k, toward(up, max(step, 1)))
        return remote(src, dst.at[step], st_send, st_recv, k, toward(up, step))

    def exchange_start(idx, src, dst, up):
        if n_slot == 4:
            @pl.when(lax.rem(place(up), 2) == 0)
            def _():
                exchange_copy(idx, src, dst, up, 0).start()
            return
        for s in range(1, n_slot):
            @pl.when(place(up) + s < n_slot)
            def _():
                exchange_copy(idx, src, dst, up, s).start()

    def exchange_pass(idx, src, dst, up):
        if n_slot == 4:
            @pl.when(place(up) == 1)
            def _():
                exchange_copy(idx, src, dst, up, 0).wait_recv()
                src[...] = (src[...].astype(F32) + edge_gate(up, 1) * dst[0].astype(F32)).astype(BF16)
                for s in (1, 2):
                    exchange_copy(idx, src, dst, up, s).start()

    def exchange_wait(idx, src, dst, up):
        if n_slot == 4:
            @pl.when(place(up) == 3)
            def _():
                exchange_copy(idx, src, dst, up, 0).wait_recv()
                exchange_copy(idx, src, dst, up, 2).wait_recv()
            @pl.when(place(up) == 2)
            def _():
                exchange_copy(idx, src, dst, up, 1).wait_recv()
            gate = jnp.where(place(up) == 3, edge_gate(up, 2), 1.0)
            return dst[0].astype(F32) + gate * dst[1].astype(F32)
        total = 0.0
        for s in range(1, n_slot):
            @pl.when(place(up) >= s)
            def _():
                exchange_copy(idx, src, dst, up, s).wait_recv()
            gate = 1.0
            for far in range(2, s + 1):
                gate = gate * edge_gate(up, far)
            total = total + gate * dst[s].astype(F32)
        return total

    def exchange_end(idx, src, dst, up):
        if n_slot == 4:
            @pl.when(lax.rem(place(up), 2) == 0)
            def _():
                exchange_copy(idx, src, dst, up, 0).wait_send()
            @pl.when(place(up) == 1)
            def _():
                for s in (1, 2):
                    exchange_copy(idx, src, dst, up, s).wait_send()
            return
        for s in range(1, n_slot):
            @pl.when(place(up) + s < n_slot)
            def _():
                exchange_copy(idx, src, dst, up, s).wait_send()

    def pack_state(snd, cur):
        for p in pairs:
            snd[64 * p : 64 * p + 64, :] = compact(cur[p]).astype(BF16)

    def entering(total, e):
        for p in pairs:
            e[p] = expand(total[64 * p : 64 * p + 64, :])
        if total.shape[0] > 256:
            e_z[0:1, :] = unpack_row(total[256:272, :])

    cur_a[...] = jnp.zeros_like(cur_a)
    cur_b[...] = jnp.zeros_like(cur_b)
    cur_z[...] = jnp.zeros_like(cur_z)

    def key_states(c):
        at = rows_at(c, CH)
        keep = same(last_of(base + c - 1), last_of(base + c))
        w = wb[at, :]
        zi = mm(msk[c], w)
        scan_step(cur_a, s_kw, c, keep, kk_[at, :] * wide(g_last[c]), w)
        z_old = cur_z[0:1, :]
        z_st[pl.ds(c, 1), :] = z_old
        inv_z[at, :] = zi
        cur_z[0:1, :] = keep * z_old + zi[CH - 1 : CH, :]

    def value_states(c):
        at = rows_at(c, CH)
        keep = same(last_of(base + c - 1), last_of(base + c))
        scan_step(cur_b, s_wv, c, keep, wb[at, :] * wide(g_last[c]), vv_[at, :])

    lax.fori_loop(0, n_rb, project_c, 0)
    gather(PV, 3)
    gather(PQ, 3)
    chunks(key_states)
    pack_state(snd_a, cur_a)
    pack_row(snd_a, cur_z[0:1, :])
    exchange_start(0, snd_a, rcv_a, True)
    gather(PO, 1)
    gather(PW, 1)
    gather(PV, 4)
    lax.fori_loop(0, n_rb, project_v, 0)
    chunks(value_states)
    pack_state(snd_b, cur_b)
    exchange_start(1, snd_b, rcv_b, True)
    exchange_pass(0, snd_a, rcv_a, True)
    gather(PU, 1)
    gather(PU2, 0)
    gather(PQ, 4)
    lax.fori_loop(0, n_rb, project_q, 0)
    gather(PO, 2)
    gather(PW, 2)

    def two(x):
        return jnp.concatenate([x, x], axis=1)

    def stacks(x):
        return [stack2(a, left, right) for a in split(x)]

    def numerators(c):
        at = rows_at(c, CH)
        m2 = two(msk[c])
        q, k2, w2 = split(qs[at, :]), stacks(kk_[at, :]), stacks(wb[at, :])
        sc = [mm_t(q[p], k2[p]).astype(BF16) * m2 for p in pairs]
        num[at, :] = jnp.concatenate([mm(sc[p], w2[p]) for p in pairs], axis=1)

    chunks(numerators)
    exchange_pass(1, snd_b, rcv_b, True)
    gather(PU, 2)
    entering(exchange_wait(0, snd_a, rcv_a, True), e_a)

    def softmax(c):
        at = rows_at(c, CH)
        reach = same(last_of(base - 1), last_of(base + c - 1))
        gpw = wide(g_prev[c])
        z_in = z_st[pl.ds(c, 1), :] + reach * e_z[0:1, :]
        skw = [(s_kw[c, p].astype(F32) + reach * e_a[p]).astype(BF16) for p in pairs]
        q = split(qs[at, :] * gpw)
        iz = 1.0 / (inv_z[at, :] + gpw.astype(F32) * z_in)
        from_state = jnp.concatenate([mm(q[p], skw[p]) for p in pairs], axis=1)
        lg = (num[at, :] + from_state) * iz
        top = jnp.concatenate([per_head(jnp.max, a, -jnp.inf) for a in split(lg)], axis=1)
        ex = jnp.exp(lg - top)
        tot = jnp.concatenate([mm(a.astype(BF16), ones_diag) for a in split(ex)], axis=1)
        pr = ex / tot
        for p in pairs:
            s_kw[c, p] = skw[p]
        num[at, :] = lg
        inv_z[at, :] = iz
        prob[at, :] = pr
        rr_[at, :] = (pr * iz).astype(BF16)

        if c == n_ch // 2:
            gather(PU2, 1)

    def mixture(c):
        at = rows_at(c, CH)
        reach = same(last_of(base - 1), last_of(base + c - 1))
        m2 = two(msk[c])
        swv = [(s_wv[c, p].astype(F32) + reach * e_b[p]).astype(BF16) for p in pairs]
        w2, v2 = stacks(wb[at, :]), stacks(vv_[at, :])
        r = rr_[at, :]
        rs, rg = split(r), split(r * wide(g_prev[c]))
        mix = [mm_t(rs[p], w2[p]).astype(BF16) * m2 for p in pairs]
        o = jnp.concatenate([mm(mix[p], v2[p]) + mm(rg[p], swv[p]) for p in pairs], axis=1)
        for p in pairs:
            s_wv[c, p] = swv[p]
        oo_[at, :] = o.astype(BF16)

    chunks(softmax)
    gather(PO, 3)
    entering(exchange_wait(1, snd_b, rcv_b, True), e_b)
    gather(PW, 3)
    chunks(mixture)
    gather(PO, 4)
    gather(PU2, 2)

    def up_w(j):
        at = U0 + 16 * j if isinstance(j, int) else pl.multiple_of(U0 + 16 * j, 16)
        return g[:, :, :, :, pl.ds(at, 16), :].reshape(D, D)

    def down_w(j):
        return g[j // 2, lax.rem(j, 2), :, :, W0:END, :].reshape(D, D)

    c0, c1 = math.sqrt(2.0 / math.pi), 0.044715

    def hidden(i, _):
        at = rows_at(i)
        h = xb[at, :].astype(F32) + mm(oo_[at, :], weight(O0))
        hsum[at, :] = h
        nh, _r = norm_stats(h)
        n = (nh * gain2 + bias2).astype(BF16)
        n2[at, :] = n
        n2t[:, at] = n.T
        return 0

    def feed(j, _):
        def rows_of(i, _):
            at = rows_at(i)
            u = mm(n2[at, :], up_w(j)).astype(BF16)
            dg = mm_t(og[at, :], down_w(j)).astype(BF16)
            sq = u * u
            t = jnp.tanh(u * (c0 + c0 * c1 * sq))
            half = 0.5 + 0.5 * t
            slope = half + u * (1.0 - t * t) * (0.5 * c0 + 1.5 * c0 * c1 * sq)
            cols = pl.ds(pl.multiple_of(j * D, D), D)
            act[at, cols] = u * half
            du[at, cols] = dg * slope
            return 0

        return lax.fori_loop(0, n_rb, rows_of, 0)

    lax.fori_loop(0, n_rb, hidden, 0)
    loaded("og")
    gather(PU, 3)
    gather(PW, 4)
    gather(PU, 4)

    def put_grad(r0, y, val):
        pg[y, :, :, :, r0 : r0 + 16, :] = val.astype(BF16).reshape(2, 2, 4, 16, D)

    def down_grads(j, _):
        val = t_mm(act[:, pl.ds(pl.multiple_of(j * D, D), D)], og[...])
        pg[j // 2, lax.rem(j, 2), :, :, W0:END, :] = val.astype(BF16).reshape(2, 4, 64, D)
        return 0

    def up_grads(j, _):
        for y in range(2):
            val = mm(n2t[256 * y : 256 * y + 256, :], du[:, pl.ds(pl.multiple_of(j * D, D), D)])
            pg[y, :, :, :, pl.ds(pl.multiple_of(U0 + 16 * j, 16), 16), :] = val.astype(BF16).reshape(2, 2, 4, 16, D)
        return 0

    def out_copy(ref):
        i = [ref is a for a in grad_s].index(True)
        return pltpu.make_async_copy(ref, grad_h[i], out_sem.at[i])

    def store(ref):
        out_copy(ref).start()

    def add_to(dst, src):
        dst[...] = dst[...] + src[...]

    def scatter_copies(p, stage):
        put = lambda src, dst, idx, where: remote(src, dst, rs_send, rs_recv, p * 8 + idx, where)
        if p == PN:
            if stage == 0:
                return [put(ngp.at[:, :, 1 - pc], nrc, 0, at_c)]
            if stage == 1:
                return [put(ngp.at[:, 1 - px, pc], nrx, 1, at_x)]
            if stage == 2:
                return [put(ngp.at[1 - py, px, pc], nry, 2, at_y)]
            return [put(ngp.at[py, px, pc, lax.rem(z + s, n_slot)], nrz.at[s - 1], 4 + s, at_z(s)) for s in range(1, n_slot)]
        r0, r1 = ROWS[p]
        sl = pl.ds(r0, r1 - r0)
        if stage == 0:
            return [put(pg.at[:, :, 1 - pc, :, sl, :], rc.at[:, :, :, sl, :], 0, at_c)]
        if stage == 1:
            return [
                put(pg.at[:, 1 - px, pc, :, sl, la], rx1.at[:, :, sl, :], 1, at_x),
                put(pg.at[1 - py, :, pc, :, sl, lb], ry1.at[:, :, sl, :], 2, at_y),
            ]
        if stage == 2:
            return [
                put(pg.at[1 - py, px, pc, :, sl, la], ry2.at[:, sl, :], 3, at_y),
                put(pg.at[py, 1 - px, pc, :, sl, lb], rx2.at[:, sl, :], 4, at_x),
            ]
        return [
            put(pg.at[py, px, pc, lax.rem(z + s, n_slot), sl, :], rz.at[s - 1, sl, :], 4 + s, at_z(s))
            for s in range(1, n_slot)
        ]

    def scatter_add(p, stage):
        if p == PN:
            if stage == 1:
                for y in range(2):
                    for x in range(2):
                        add_to(ngp.at[y, x, pc], nrc.at[y, x])
            elif stage == 2:
                for y in range(2):
                    add_to(ngp.at[y, px, pc], nrx.at[y])
            elif stage == 3:
                add_to(ngp.at[py, px, pc], nry)
            else:
                total = ngp[py, px, pc, z].astype(F32)
                for s in range(1, n_slot):
                    total = total + nrz[s - 1].astype(F32)
                ng_o[...] = total
                store(ng_o)
            return
        r0, r1 = ROWS[p]
        sl = pl.ds(r0, r1 - r0)
        if stage == 1:
            def body(i, _):
                y, x = i // 2, lax.rem(i, 2)
                add_to(pg.at[y, x, pc, :, sl, :], rc.at[y, x, :, sl, :])
                return 0
            lax.fori_loop(0, 4, body, 0)
        elif stage == 2:
            def body(i, _):
                add_to(pg.at[i, px, pc, :, sl, la], rx1.at[i, :, sl, :])
                add_to(pg.at[py, i, pc, :, sl, lb], ry1.at[i, :, sl, :])
                return 0
            lax.fori_loop(0, 2, body, 0)
        elif stage == 3:
            add_to(pg.at[py, px, pc, :, sl, la], ry2.at[:, sl, :])
            add_to(pg.at[py, px, pc, :, sl, lb], rx2.at[:, sl, :])
        else:
            total = pg[py, px, pc, z, sl, :].astype(F32)
            for s in range(1, n_slot):
                total = total + rz[s - 1, sl, :].astype(F32)
            if p in (PU, PU2):
                for j in range(2):
                    at = 2 * D * (p - PU) + D * j
                    wu_o[:, at : at + D] = total[16 * j : 16 * j + 16, :]
                if p == PU2:
                    store(wu_o)
            elif p == PC:
                for i in range(4):
                    wc_o[16 * i : 16 * i + 16, :] = total[:, lanes(i)]
                store(wc_o)
            else:
                dst = {PV: wv_o, PQ: wq_o, PK: wk_o, PO: wo_o, PW: wd_o}[p]
                dst[...] = total
                store(dst)

    def scatter(p, stage):
        if not comm:
            return
        if stage > 0:
            for copy in scatter_copies(p, stage - 1):
                copy.wait_recv()
            scatter_add(p, stage)
        if stage < 4:
            for copy in scatter_copies(p, stage):
                copy.start()

    for j in range(2):
        feed(j, 0)
    lax.fori_loop(0, 2, up_grads, 0)
    scatter(PU, 0)
    gather(PU2, 3)
    gather(PU2, 4)
    for j in range(2, 4):
        feed(j, 0)
    lax.fori_loop(2, 4, up_grads, 0)
    scatter(PU, 1)
    scatter(PU2, 0)
    lax.fori_loop(0, 4, down_grads, 0)
    scatter(PW, 0)
    scatter(PU2, 1)

    def feed_back(i, acc):
        at = rows_at(i)
        dn = jnp.zeros((rb, D), F32)
        for j in range(4):
            dn = dn + mm_t(du[at, D * j : D * j + D], up_w(j))
        nh, rstd = norm_stats(hsum[at, :])
        dh = og[at, :].astype(F32) + norm_back(dn, nh, rstd, gain2)
        hid[at, :] = dh
        a = dh.astype(BF16)
        da[at, :] = a
        do[at, :] = mm_t(a, weight(O0)).astype(BF16)
        return (acc[0] + jnp.sum(dn * nh, axis=0, keepdims=True), acc[1] + jnp.sum(dn, axis=0, keepdims=True))

    zero_row = jnp.zeros((1, D), F32)
    gain2_g, bias2_g = lax.fori_loop(0, n_rb, feed_back, (zero_row, zero_row))
    for y in range(2):
        put_grad(O0, y, t_mm(oo_[:, 256 * y : 256 * y + 256], da[...]))
    scatter(PO, 0)
    scatter(PW, 1)

    cur_a[...] = jnp.zeros_like(cur_a)
    cur_b[...] = jnp.zeros_like(cur_b)
    cur_z[...] = jnp.zeros_like(cur_z)

    def slot_states(i):
        c = n_ch - 1 - i
        at = rows_at(c, CH)
        keep = same(first_of(base + c), first_of(base + c + 1))
        scan_step(cur_a, s_r, c, keep, rr_[at, :] * wide(g_first[c]), do[at, :])

    def slot_grads(i):
        c = n_ch - 1 - i
        at = rows_at(c, CH)
        m2 = two(msk[c])
        gpw = wide(g_prev[c])
        keep = same(first_of(base + c), first_of(base + c + 1))
        w2, v2 = stacks(wb[at, :]), stacks(vv_[at, :])
        do_c = do[at, :]
        ds, dg = split(do_c), split(do_c * gpw)
        dmix = [mm_t(ds[p], v2[p]).astype(BF16) * m2 for p in pairs]
        dr = jnp.concatenate([mm(dmix[p], w2[p]) + mm_t(dg[p], s_wv[c, p]) for p in pairs], axis=1)
        iz, pr, lg = inv_z[at, :], prob[at, :], num[at, :]
        dpr = dr * iz
        inner = jnp.concatenate([mm(a.astype(BF16), ones_diag) for a in split(pr * dpr)], axis=1)
        dl = pr * (dpr - inner)
        dn_c = (dl * iz).astype(BF16)
        dz_c = (-(dpr * pr + dl * lg) * iz).astype(BF16)
        firsts = mm(mskt[c][0:16, :], dz_c)
        scan_step(cur_b, s_n, c, keep, qs[at, :] * wide(g_first[c]), dn_c)
        z_old = cur_z[0:1, :]
        z_r[pl.ds(c, 1), :] = z_old
        cur_z[0:1, :] = keep * z_old + firsts[0:1, :]
        dnum_[at, :] = dn_c
        dz_[at, :] = dz_c

        if i == n_ch // 2:
            scatter(PU, 2)

    chunks(slot_grads)
    pack_state(snd_c, cur_b)
    pack_row(snd_c, cur_z[0:1, :])
    exchange_start(2, snd_c, rcv_c, False)
    chunks(slot_states)
    pack_state(snd_d, cur_a)
    exchange_start(3, snd_d, rcv_d, False)
    exchange_pass(2, snd_c, rcv_c, False)
    scatter(PU2, 2)
    scatter(PO, 1)

    def query_grads(c):
        at = rows_at(c, CH)
        m2 = two(msk[c])
        dn_c = dnum_[at, :]
        dn, dg = split(dn_c), split(dn_c * wide(g_prev[c]))
        w2, k2 = stacks(wb[at, :]), stacks(kk_[at, :])
        dsc = [mm_t(dn[p], w2[p]).astype(BF16) * m2 for p in pairs]
        dq = jnp.concatenate([mm(dsc[p], k2[p]) + mm_t(dg[p], s_kw[c, p]) for p in pairs], axis=1)
        dq_[at, :] = (dq * (HEAD_DIM**-0.5)).astype(BF16)

    chunks(query_grads)
    for y in range(2):
        put_grad(Q0, y, mm(n1t[256 * y : 256 * y + 256, :], dq_[...]))
    scatter(PQ, 0)
    exchange_pass(3, snd_d, rcv_d, False)

    def near_grads(c):
        at = rows_at(c, CH)
        mt = mskt[c]
        mt2 = two(mt)
        w, v, k = split(wb[at, :]), split(vv_[at, :]), split(kk_[at, :])
        q2, dn2, r2, do2 = (stacks(ref[at, :]) for ref in (qs, dnum_, rr_, do))
        dsc_t = [mm_t(w[p], dn2[p]).astype(BF16) * mt2 for p in pairs]
        dmix_t = [mm_t(v[p], do2[p]).astype(BF16) * mt2 for p in pairs]
        sc_t = [mm_t(k[p], q2[p]).astype(BF16) * mt2 for p in pairs]
        dk = jnp.concatenate([mm(dsc_t[p], q2[p]) for p in pairs], axis=1)
        dw = jnp.concatenate([mm(dmix_t[p], r2[p]) + mm(sc_t[p], dn2[p]) for p in pairs], axis=1)
        num[at, :] = dk
        inv_z[at, :] = dw + mm(mt, dz_[at, :])

        if c == n_ch // 2:
            scatter(PQ, 1)
            scatter(PW, 2)

    chunks(near_grads)
    scatter(PO, 2)
    entering(exchange_wait(2, snd_c, rcv_c, False), e_a)
    entering(exchange_wait(3, snd_d, rcv_d, False), e_b)
    scatter(PU, 3)
    scatter(PU2, 3)

    def far_grads(c):
        at = rows_at(c, CH)
        reach = same(first_of(base + n_ch), first_of(base + c + 1))
        gnw = wide(g_next[c])
        z_in = z_r[pl.ds(c, 1), :] + reach * e_z[0:1, :]
        wg, vg, kg = (split(ref[at, :] * gnw) for ref in (wb, vv_, kk_))
        st_n = [(s_n[c, p].astype(F32) + reach * e_a[p]).astype(BF16) for p in pairs]
        st_r = [(s_r[c, p].astype(F32) + reach * e_b[p]).astype(BF16) for p in pairs]
        dk = num[at, :] + jnp.concatenate([mm_t(wg[p], st_n[p]) for p in pairs], axis=1)
        dw = inv_z[at, :] + gnw.astype(F32) * z_in
        dw = dw + jnp.concatenate([mm_t(vg[p], st_r[p]) + mm(kg[p], st_n[p]) for p in pairs], axis=1)
        for p in pairs:
            s_r[c, p] = st_r[p]
        dk_[at, :] = dk.astype(BF16)
        dphi_[at, :] = (dw * ew[at, :]).astype(BF16)

    chunks(far_grads)

    for y in range(2):
        cols = slice(256 * y, 256 * y + 256)
        val = mm_t(mm(n1t[cols, :], dphi_[...]).astype(BF16), permutation()).astype(BF16)
        for x in range(2):
            for c in range(2):
                for i in range(4):
                    r = ((x * 2 + c) * 4 + i) * 16
                    for j in range(4):
                        pg[y, x, c, j, C0 : C0 + 16, CH * i : CH * i + CH] = val[r : r + 16, lanes(j)]
    scatter(PC, 0)
    for y in range(2):
        put_grad(K0, y, mm(n1t[256 * y : 256 * y + 256, :], dk_[...]))
    scatter(PK, 0)
    scatter(PQ, 2)
    scatter(PW, 3)

    def value_grads(c):
        at = rows_at(c, CH)
        mt2 = two(mskt[c])
        w_c = wb[at, :]
        w, wg = split(w_c), split(w_c * wide(g_next[c]))
        r2, do2 = stacks(rr_[at, :]), stacks(do[at, :])
        mix_t = [mm_t(w[p], r2[p]).astype(BF16) * mt2 for p in pairs]
        dv = jnp.concatenate([mm(mix_t[p], do2[p]) + mm(wg[p], s_r[c, p]) for p in pairs], axis=1)
        dv_[at, :] = dv.astype(BF16)

    chunks(value_grads)
    for y in range(2):
        put_grad(V0, y, mm(n1t[256 * y : 256 * y + 256, :], dv_[...]))
    scatter(PV, 0)
    scatter(PC, 1)
    scatter(PK, 1)
    scatter(PO, 3)

    def input_grads(i, acc):
        at = rows_at(i)
        dn = mm_t(dq_[at, :], weight(Q0)) + mm_t(dk_[at, :], weight(K0)) + mm_t(dv_[at, :], weight(V0)) + mm_t(dphi_[at, :], wc_s[...])
        nh, rstd = norm_stats(xb[at, :].astype(F32))
        tg_o[at, :] = hid[at, :] + norm_back(dn, nh, rstd, gain1)
        return (acc[0] + jnp.sum(dn * nh, axis=0, keepdims=True), acc[1] + jnp.sum(dn, axis=0, keepdims=True))

    def outputs(i, _):
        at = rows_at(i)
        out = hsum[at, :]
        for j in range(4):
            out = out + mm(act[at, D * j : D * j + D], down_w(j))
        out_o[at, :] = out.astype(BF16)
        return 0

    gain1_g, bias1_g = lax.fori_loop(0, n_rb, input_grads, (zero_row, zero_row))
    tg_copy = pltpu.make_async_copy(tg_o, tg_h, out_sem.at[8])
    tg_copy.start()
    norm_g = jnp.concatenate([gain1_g, bias1_g, gain2_g, bias2_g, jnp.zeros((12, D), F32)], axis=0)
    if comm:
        for y in range(2):
            for x in range(2):
                for c in range(2):
                    for j in range(4):
                        d = ((y * 2 + x) * 2 + c) * 4 + j
                        ngp[y, x, c, j] = norm_g[:, lanes(d // 8)].astype(BF16)
    else:
        ng_o[...] = norm_g
    scatter(PN, 0)
    scatter(PV, 1)
    scatter(PC, 2)
    scatter(PK, 2)
    scatter(PQ, 3)
    scatter(PN, 1)
    lax.fori_loop(0, n_rb, outputs, 0)
    out_done = pltpu.make_async_copy(out_o, out_h, out_sem.at[9])
    out_done.start()
    scatter(PV, 2)
    scatter(PC, 3)
    scatter(PK, 3)
    scatter(PN, 2)
    scatter(PV, 3)
    scatter(PN, 3)
    for p in (PU, PU2, PW, PO, PQ, PC, PK, PV, PN):
        scatter(p, 4)

    tg_copy.wait()
    out_done.wait()
    for args in ((0, snd_a, rcv_a, True), (1, snd_b, rcv_b, True), (2, snd_c, rcv_c, False), (3, snd_d, rcv_d, False)):
        exchange_end(*args)
    if comm:
        for ref in grad_s:
            out_copy(ref).wait()
        for stage in range(4):
            for p in range(len(ROWS) + 1):
                for copy in gather_copies(p, stage) + scatter_copies(p, stage):
                    copy.wait_send()


def vm(shape, dtype):
    return pltpu.VMEM(shape, dtype)


def run_layer(rows, n_slot, seg_rows, comm, operands):
    n_ch = rows // CH
    act_shape = (rows, D)
    hbm, vmem = pl.BlockSpec(memory_space=pl.ANY), pl.BlockSpec(memory_space=pltpu.VMEM)
    sds = jax.ShapeDtypeStruct
    outs = [sds(act_shape, BF16), sds(act_shape, F32)]
    grads = [(16, D)] * 4 + [(64, CH), (16, FF), (64, D), (16, CH)]
    if comm:
        outs += [sds(shape, F32) for shape in grads]
        out_specs = [hbm] * len(outs)
    else:
        outs += [sds((*GRID, END, D), BF16), sds((16, D), F32)]
        out_specs = [hbm, hbm, vmem, vmem]
    b, f = (lambda: vm(act_shape, BF16)), (lambda: vm(act_shape, F32))
    state = lambda dtype: vm((n_ch, PAIRS, CH, CH), dtype)
    sems = lambda n: pltpu.SemaphoreType.DMA((n,))
    scratch = [
        vm((*GRID, END, D), BF16), vm((*GRID, 16, CH), BF16), b(), vm((seg_rows, CH), jnp.int32), b(), b(), b(), b(), b(), b(),
        f(), f(), f(), f(), b(), b(), f(), b(), vm((rows, FF), BF16), vm((rows, FF), BF16), b(), b(),
        vm((D, rows), BF16), vm((D, rows), BF16), b(), b(), b(), b(), f(),
        state(BF16), state(BF16), vm((max(8, n_ch), D), F32), state(BF16), state(BF16), vm((max(8, n_ch), D), F32),
        vm((PAIRS, CH, CH), F32), vm((PAIRS, CH, CH), F32), vm((8, D), F32),
        vm((PAIRS, CH, CH), F32), vm((PAIRS, CH, CH), F32), vm((8, D), F32),
    ]
    scratch += [vm((n_ch, CH, CH), BF16)] * 6
    long, short = (272, CH), (256, CH)
    scratch += [vm(long, BF16), vm(short, BF16), vm((n_slot, *long), BF16), vm((n_slot, *short), BF16)] * 2
    scratch += [vm((D, D), BF16), sems(4 * max(n_slot, 4)), sems(4 * max(n_slot, 4)), sems(20), sems(10)]
    if comm:
        ny, nx, nc, nz = GRID
        scratch += [
            vm((*GRID, END, D), BF16), vm((*GRID, 16, CH), BF16),
            vm((ny, nx, nz, END, D), BF16), vm((ny, nz, END, D // 2), BF16), vm((nx, nz, END, D // 2), BF16),
            vm((nz, END, D // 2), BF16), vm((nz, END, D // 2), BF16), vm((nz - 1, END, D), BF16),
            vm((ny, nx, nz, 16, CH), BF16), vm((ny, nz, 16, CH), BF16), vm((nz, 16, CH), BF16), vm((nz - 1, 16, CH), BF16),
        ]
        scratch += [sems(8 * (len(ROWS) + 1))] * 4
        scratch += [vm(operands[7].shape, BF16), vm((4, 1, operands[-1].shape[1]), BF16)] + [vm(shape, F32) for shape in grads]
    cfg = dict(rows=rows, n_slot=n_slot, comm=comm)
    return pl.pallas_call(
        functools.partial(kernel_body, cfg),
        out_shape=outs,
        in_specs=[hbm] * len(operands),
        out_specs=out_specs,
        scratch_shapes=scratch,
        compiler_params=pltpu.CompilerParams(collective_id=0, has_side_effects=True, vmem_limit_bytes=63 * 2**20),
    )(*operands)


def finish_body(*refs):
    src, dst, rest = refs[:10], refs[10:23], refs[23:]
    *held, sem_in, sem_out = rest
    jobs = [(1, 0), (1, 1), (0, 0), (0, 1)] + [(i, None) for i in (2, 3, 4, 5, 7, 8)]

    def copy(k, come):
        i, part = jobs[k]
        buf = held[(0, 1, 2, 3, 4, 5, None, 6, 7)[i]]
        cut = lambda ref: ref if part is None else ref.at[pl.ds(part * (ref.shape[0] // 2), ref.shape[0] // 2)]
        if come:
            return pltpu.make_async_copy(cut(src[i]), cut(buf), sem_in.at[k])
        return pltpu.make_async_copy(cut(buf), cut(dst[i]), sem_out.at[k])

    for k in range(len(jobs)):
        copy(k, True).start()
    dst[6][...] = src[6][...].T
    wide = dst[9].shape[1]
    dev = lax.axis_index("dp") * lax.axis_size("slot") + lax.axis_index("slot")
    vals = pltpu.roll(src[9][...], lax.rem(CH - wide * lax.rem(dev, CH // wide), CH), 1)
    for i in range(4):
        dst[9 + i][...] = vals[i : i + 1, 0:wide]
    for k in range(len(jobs)):
        copy(k, True).wait()
        copy(k, False).start()
    for k in range(len(jobs)):
        copy(k, False).wait()


def finish(outs, wide):
    hbm, vmem = pl.BlockSpec(memory_space=pl.ANY), pl.BlockSpec(memory_space=pltpu.VMEM)
    sds = jax.ShapeDtypeStruct
    shapes = [sds(a.shape, a.dtype) for a in outs[:9]] + [sds((1, wide), F32)] * 4
    shapes[6] = sds(outs[6].shape[::-1], F32)
    return pl.pallas_call(
        finish_body,
        out_shape=shapes,
        in_specs=[vmem if i in (6, 9) else hbm for i in range(10)],
        out_specs=[vmem if i == 6 or i > 8 else hbm for i in range(13)],
        scratch_shapes=[vm(outs[i].shape, outs[i].dtype) for i in (0, 1, 2, 3, 4, 5, 7, 8)] + [pltpu.SemaphoreType.DMA((10,))] * 2,
        compiler_params=pltpu.CompilerParams(vmem_limit_bytes=63 * 2**20),
    )(*outs)


def layer(
    tokens, segment_ids, w_query, w_key, w_value, w_out, w_control, w_up, w_down,
    norm1_gain, norm1_bias, norm2_gain, norm2_bias, out_grad,
):
    n_slot, n_dp = lax.axis_size("slot"), lax.axis_size("dp")
    n_dev = n_slot * n_dp
    rows = tokens.shape[0] // n_slot
    seg = segment_ids.reshape(-1, CH)
    norms = (norm1_gain, norm1_bias, norm2_gain, norm2_bias)
    if n_dev == math.prod(GRID) and n_slot == GRID[3]:
        outs = run_layer(rows, n_slot, seg.shape[0], True, (
            tokens, seg, out_grad, w_query, w_key, w_value, w_out,
            w_control.transpose(1, 2, 0).reshape(CH, -1), w_up, w_down, *(a.reshape(1, -1) for a in norms),
        ))
        outs = finish(outs, norm1_gain.shape[0])
        control = outs[6].reshape(*w_control.shape[1:], -1).transpose(2, 0, 1)
        return (*outs[:6], control, *outs[7:9], *(a.reshape(-1) for a in outs[9:]))

    norms = jnp.stack(norms)
    both = ("dp", "slot")
    gather = lambda a: lax.all_gather(a, both, axis=0, tiled=True)
    n_blk = math.prod(GRID)
    wc = lax.all_gather(lax.all_gather(w_control, "dp", axis=0, tiled=True), "slot", axis=2, tiled=True)
    gw = SLOTS // GRID[3]
    wc = wc.reshape(8, 4, 16, HEADS, GRID[3], gw).transpose(0, 4, 2, 1, 3, 5).reshape(n_blk, 16, D)
    norm_all = lax.all_gather(norms, both, axis=1, tiled=True)
    norm_all = norm_all.reshape(4, 4, CH).transpose(1, 0, 2).reshape(16, CH)
    norm_blk = jnp.zeros((n_blk, 16, CH), BF16).at[0].set(norm_all).reshape(*GRID, 16, CH)
    split = lambda a: gather(a).reshape(n_blk, -1, D)
    up = gather(w_up).reshape(n_blk, 16, 4, D).transpose(0, 2, 1, 3).reshape(n_blk, 64, D)
    packed = jnp.concatenate(
        [split(w_key), wc, split(w_value), split(w_query), split(w_out), up, split(w_down)], axis=1
    ).reshape(*GRID, END, D)
    out, tg, part, ng = run_layer(rows, n_slot, seg.shape[0], False, (tokens, seg, out_grad, packed, norm_blk))
    part = part.reshape(n_blk, END, D).astype(F32)
    scatter = lambda a, dim=0: lax.psum_scatter(a, both, scatter_dimension=dim, tiled=True)
    full = lambda r0, r1: part[:, r0:r1].reshape(-1, D)
    wcg = part[:, C0:V0].reshape(8, GRID[3], 16, 4, HEADS, gw).transpose(0, 3, 2, 4, 1, 5).reshape(D, HEADS, SLOTS)
    wcg = lax.psum_scatter(lax.psum_scatter(wcg, "dp", scatter_dimension=0, tiled=True), "slot", scatter_dimension=2, tiled=True)
    upg = part[:, U0:W0].reshape(n_blk, 4, 16, D).transpose(0, 2, 1, 3).reshape(D, FF)
    ng = scatter(ng[:4], 1)
    return (
        out, tg, scatter(full(Q0, O0)), scatter(full(K0, C0)), scatter(full(V0, Q0)), scatter(full(O0, U0)),
        wcg, scatter(upg), scatter(full(W0, END)), ng[0], ng[1], ng[2], ng[3],
    )


def solution(mesh):
    both = P(("dp", "slot"), None)
    vec = P(("dp", "slot"))
    control = P("dp", None, "slot")
    in_specs = (
        P("dp", None), P("dp"), both, both, both, both, control, both, both, vec, vec, vec, vec, both,
    )
    out_specs = (both, both, both, both, both, both, control, both, both, vec, vec, vec, vec)
    return jax.shard_map(layer, mesh=mesh, in_specs=in_specs, out_specs=out_specs, check_vma=False)
```

```python
import functools
import math

import jax
import jax.numpy as jnp
from jax import lax
from jax.experimental import pallas as pl
from jax.experimental.pallas import tpu as pltpu
from jax.sharding import PartitionSpec as P

D = 512
HEADS = 8
HEAD_DIM = 64
SLOTS = 64
FF = 2048
EPS = 1e-05
CH = 128
PAIRS = HEADS // 2
F32 = jnp.float32
BF16 = jnp.bfloat16
MESH = pl.DeviceIdType.MESH

K0, C0, V0, Q0, O0, U0, W0, END = 0, 16, 32, 48, 64, 80, 144, 208
GRID = (2, 2, 2, 4)
ROWS = ((K0, C0), (C0, V0), (V0, Q0), (Q0, O0), (O0, U0), (U0, U0 + 32), (U0 + 32, W0), (W0, END))
PK, PC, PV, PQ, PO, PU, PU2, PW, PN = range(9)


def mm(a, b):
    return jnp.dot(a, b, preferred_element_type=F32)


def mm_t(a, b):
    return lax.dot_general(a, b, (((1,), (1,)), ((), ())), preferred_element_type=F32)


def t_mm(a, b):
    return lax.dot_general(a, b, (((0,), (0,)), ((), ())), preferred_element_type=F32)


def half_lanes(dtype):
    lane = lax.broadcasted_iota(jnp.int32, (1, CH), 1)
    left = jnp.where(lane < HEAD_DIM, 1.0, 0.0)
    return left.astype(dtype), (1.0 - left).astype(dtype)


def stack2(x, left, right):
    return jnp.concatenate([x * left, x * right], axis=0)


def per_head(op, x, fill):
    lane = lax.broadcasted_iota(jnp.int32, x.shape, 1)
    first = lane < HEAD_DIM
    a = op(jnp.where(first, x, fill), axis=1, keepdims=True)
    b = op(jnp.where(first, fill, x), axis=1, keepdims=True)
    return jnp.where(first, a, b)


def norm_stats(x):
    center = x - jnp.mean(x, axis=-1, keepdims=True)
    rstd = lax.rsqrt(jnp.mean(center * center, axis=-1, keepdims=True) + EPS)
    return center * rstd, rstd


def norm_back(dn, nh, rstd, gain):
    e = dn * gain
    return (e - jnp.mean(e, axis=-1, keepdims=True) - nh * jnp.mean(e * nh, axis=-1, keepdims=True)) * rstd


def kernel_body(cfg, *refs):
    refs = list(refs)
    take = lambda n: [refs.pop(0) for _ in range(n)]
    rows, n_slot, comm = cfg["rows"], cfg["n_slot"], cfg["comm"]
    n_ch = rows // CH
    rb = rows if rows <= 768 else 256
    n_rb = rows // rb
    (tok_in, seg_in, og_in) = take(3)
    if comm:
        (wq_in, wk_in, wv_in, wo_in, wc_in, wu_in, wd_in, *norm_in) = take(11)
        out_h, tg_h, *grad_h = take(10)
    else:
        (g_in, gn_in) = take(2)
        (out_h, tg_h, pg, ng_o) = take(4)
    (g, gn, xb, seg, og, n1, qs, kk_, vv_, wb, ew, num, inv_z, prob, rr_, oo_, hid, n2, act, du, da, do) = take(22)
    (n1t, n2t, dq_, dk_, dv_, dphi_, hsum) = take(7)
    (s_kw, s_wv, z_st, s_r, s_n, z_r) = take(6)
    (cur_a, cur_b, cur_z, e_a, e_b, e_z) = take(6)
    (msk, mskt, g_prev, g_last, g_next, g_first) = take(6)
    (snd_a, snd_b, rcv_a, rcv_b, snd_c, snd_d, rcv_c, rcv_d) = take(8)
    (wc_s, st_send, st_recv, in_sem, out_sem) = take(5)
    if comm:
        (pg, ngp, rc, rx1, ry1, ry2, rx2, rz, nrc, nrx, nry, nrz) = take(12)
        (ag_send, ag_recv, rs_send, rs_recv) = take(4)
        (wct, nv) = take(2)
        grad_s = take(8)
        (wq_o, wk_o, wv_o, wo_o, wc_o, wu_o, wd_o, ng_o) = grad_s
    assert not refs
    tg_o, out_o = prob, oo_
    dnum_, dz_ = du.at[:, 0:D], du.at[:, D : 2 * D]

    dp = lax.axis_index("dp")
    z = lax.axis_index("slot")
    left, right = half_lanes(BF16)
    leftf, rightf = half_lanes(F32)
    ri = lax.broadcasted_iota(jnp.int32, (CH, CH), 0)
    ci = lax.broadcasted_iota(jnp.int32, (CH, CH), 1)
    block_diag = jnp.where((ri < HEAD_DIM) == (ci < HEAD_DIM), 1.0, 0.0).astype(F32)
    ones_diag = block_diag.astype(BF16)
    pairs = range(PAIRS)

    if comm:
        ny, nx, nc, nz = GRID
        py, px, pc = dp // (nx * nc), lax.rem(dp // nc, nx), lax.rem(dp, nc)
        at_x = ((py * nx + (1 - px)) * nc + pc, z)
        at_y = (((1 - py) * nx + px) * nc + pc, z)
        at_c = ((py * nx + px) * nc + (1 - pc), z)

    def at_z(s):
        return (dp, lax.rem(z + s, n_slot))

    def remote(src, dst, send_sem, recv_sem, idx, where):
        return pltpu.make_async_remote_copy(
            src_ref=src, dst_ref=dst, send_sem=send_sem.at[idx], recv_sem=recv_sem.at[idx],
            device_id=where, device_id_type=MESH,
        )

    loads = {}

    def load(name, src, dst):
        copy = pltpu.make_async_copy(src, dst, in_sem.at[sum(map(len, loads.values()))])
        copy.start()
        loads.setdefault(name, []).append(copy)

    def loaded(name):
        for copy in loads.get(name, ()):
            copy.wait()

    if comm:
        my = g.at[py, px, pc, z]
        load(PK, wk_in, my.at[K0:C0])
        for i, ref in enumerate(norm_in):
            load(PN, ref, nv.at[i])
        load(PC, wc_in, wct)
        load(PV, wv_in, my.at[V0:Q0])
        load(PQ, wq_in, my.at[Q0:O0])
    else:
        load(PK, g_in, g)
        load(PK, gn_in, gn)
    load("tok", tok_in.at[pl.ds(pl.multiple_of(z * rows, CH), rows)], xb)
    load("seg", seg_in, seg)
    if comm:
        load(PO, wo_in, my.at[O0:U0])
        load(PW, wd_in, my.at[W0:END])
        for i in range(4):
            load(PU if i < 2 else PU2, wu_in.at[:, D * i : D * i + D], my.at[U0 + 16 * i : U0 + 16 * i + 16])
    load("og", og_in, og)

    for ref in (rcv_a, rcv_b, rcv_c, rcv_d):
        ref[...] = jnp.zeros_like(ref)
    bar = pltpu.get_barrier_semaphore()
    peers = [at_z(s) for s in range(1, n_slot)]
    if comm:
        peers += [at_x, at_y, at_c]
    for peer in peers:
        pl.semaphore_signal(bar, inc=1, device_id=peer, device_id_type=MESH)
    pl.semaphore_wait(bar, len(peers))

    la, lb = pl.ds(0, D // 2), pl.ds(D // 2, D // 2)

    EARLY = (PU, PU2, PW)

    def gather_copies(p, stage):
        put = lambda ref, idx, where, src=None: remote(ref if src is None else src, ref, ag_send, ag_recv, p * 24 + idx, where)
        if p == PN:
            if stage == 0:
                return [put(gn.at[py, px, pc, z], s - 1, at_z(s)) for s in range(1, n_slot)]
            return [put(*((gn.at[py, px, pc], 3, at_x), (gn.at[py, :, pc], 5, at_y), (gn.at[:, :, pc], 7, at_c))[stage - 1])]
        r0, r1 = ROWS[p]
        sl = pl.ds(r0, r1 - r0)
        if stage == 0:
            src = wk_in if p == PK else None
            return [put(g.at[py, px, pc, z, sl], s - 1, at_z(s), src) for s in range(1, n_slot)]
        if stage == 3:
            return [put(g.at[:, :, pc, :, sl, :], 7, at_c)]
        if p not in EARLY:
            which, base_idx = [slice(None)], 3
        elif stage > 3:
            which, base_idx = [z], 8
        else:
            which, base_idx = [lax.rem(z + s, n_slot) for s in range(1, n_slot)], 12
        copies = []
        for k, zz in enumerate(which):
            if stage in (1, 4):
                copies += [
                    put(g.at[py, px, pc, zz, sl, la], base_idx + 4 * k, at_x),
                    put(g.at[py, px, pc, zz, sl, lb], base_idx + 4 * k + 1, at_y),
                ]
            else:
                copies += [
                    put(g.at[py, :, pc, zz, sl, la], base_idx + 4 * k + 2, at_y),
                    put(g.at[:, px, pc, zz, sl, lb], base_idx + 4 * k + 3, at_x),
                ]
        return copies

    def gather(p, stage):
        if not comm:
            return
        if stage == 0:
            if p not in (PK, PC, PN, *EARLY):
                loaded(p)
        else:
            for copy in gather_copies(p, stage - 1):
                copy.wait_recv()
        if stage == 3 and p in EARLY:
            for copy in gather_copies(p, 5):
                copy.wait_recv()
        if stage < 4:
            for copy in gather_copies(p, stage):
                copy.start()

    def gather_own(p, stage):
        if not comm:
            return
        if stage == 4:
            loaded(p)
        else:
            for copy in gather_copies(p, 4):
                copy.wait_recv()
        for copy in gather_copies(p, stage):
            copy.start()

    def weight(r0):
        return g[:, :, :, :, r0 : r0 + 16, :].reshape(D, D)

    gather(PK, 0)
    if comm:
        loaded(PN)
        each = nv.shape[2]
        dev = dp * n_slot + z
        vals = [nv[i].astype(F32) for i in range(4)] + [jnp.zeros((12, each), F32)]
        a = lax.broadcasted_iota(jnp.int32, (each, CH), 0)
        b = lax.broadcasted_iota(jnp.int32, (each, CH), 1)
        place = jnp.where(b == a + each * lax.rem(dev, CH // each), 1.0, 0.0).astype(BF16)
        a = lax.broadcasted_iota(jnp.int32, (16, 16), 0)
        b = lax.broadcasted_iota(jnp.int32, (16, 16), 1)
        down = jnp.where(a == b + 4 * (dev // (CH // each)), 1.0, 0.0).astype(BF16)
        vals = mm(jnp.concatenate(vals, axis=0).astype(BF16), place).astype(BF16)
        gn[py, px, pc, z] = mm(down, vals).astype(BF16)
        gather(PN, 0)
        loaded(PC)
        a = lax.broadcasted_iota(jnp.int32, (wct.shape[1], wct.shape[1]), 0)
        b = lax.broadcasted_iota(jnp.int32, (wct.shape[1], wct.shape[1]), 1)
        flat = mm_t(jnp.where(a == b, 1.0, 0.0).astype(BF16), wct[...]).astype(BF16)
        for i in range(4):
            my[C0:V0, CH * i : CH * i + CH] = flat[16 * i : 16 * i + 16, :]
        gather(PC, 0)
        loaded(PK)
        for p in EARLY:
            gather_own(p, 4)
    else:
        loaded(PK)

    seg_rows = seg.shape[0]

    def seg_row(i):
        return seg[pl.ds(jnp.clip(i, 0, seg_rows - 1), 1), :].astype(F32)

    def first_of(i):
        return seg_row(i)[:, 0:1]

    def last_of(i):
        return seg_row(i)[:, CH - 1 : CH]

    base = z * n_ch

    def same(a, b):
        return jnp.where(a == b, 1.0, 0.0).astype(F32)

    def rows_at(i, n=rb):
        return pl.ds(i * n if isinstance(i, int) else pl.multiple_of(i * n, n), n)

    def chunks(step):
        for i in range(n_ch):
            step(i)

    def make_masks(c):
        row = jnp.broadcast_to(seg_row(base + c), (CH, CH))
        col = row.T
        eq = row == col
        msk[c] = jnp.where(eq & (ci <= ri), 1.0, 0.0).astype(BF16)
        mskt[c] = jnp.where(eq & (ri <= ci), 1.0, 0.0).astype(BF16)
        g_prev[c] = same(col, last_of(base + c - 1)).astype(BF16)
        g_last[c] = same(col, last_of(base + c)).astype(BF16)
        g_next[c] = same(col, first_of(base + c + 1)).astype(BF16)
        g_first[c] = same(col, first_of(base + c)).astype(BF16)

    def center(i, _):
        at = rows_at(i)
        nh, _r = norm_stats(xb[at, :].astype(F32))
        hid[at, :] = nh
        return 0

    loaded("seg")
    chunks(make_masks)
    loaded("tok")
    lax.fori_loop(0, n_rb, center, 0)
    for p in (PN, PK, PC):
        gather(p, 1)
    for p in (PV, PQ):
        gather(p, 0)
    for p in (PN, PK, PC):
        gather(p, 2)
    for p in (PV, PQ):
        gather(p, 1)
    for p in (PO, PW, PU, PU2):
        gather(p, 0)
    for p in (PN, PK, PC):
        gather(p, 3)
    for p in (PV, PQ):
        gather(p, 2)
    for p in (PN, PK):
        gather(p, 4)
    for p in EARLY:
        gather_own(p, 5)

    norms = jnp.sum(gn[...].astype(F32).reshape(math.prod(GRID), 16, CH), axis=0)
    gain1, bias1, gain2, bias2 = (
        jnp.concatenate([norms[4 * q + i : 4 * q + i + 1, :] for q in range(4)], axis=1) for i in range(4)
    )

    def project_k(i, _):
        at = rows_at(i)
        n = (hid[at, :] * gain1 + bias1).astype(BF16)
        n1[at, :] = n
        n1t[:, at] = n.T
        kk_[at, :] = mm(n, weight(K0)).astype(BF16)
        return 0

    lax.fori_loop(0, n_rb, project_k, 0)
    gather(PC, 4)

    def permutation():
        gw = SLOTS // GRID[3]
        a = lax.broadcasted_iota(jnp.int32, (D, D), 0)
        b = lax.broadcasted_iota(jnp.int32, (D, D), 1)
        h, s = b // SLOTS, lax.rem(b, SLOTS)
        src = (s // gw) * (HEADS * gw) + h * gw + lax.rem(s, gw)
        return jnp.where(a == src, 1.0, 0.0).astype(BF16)

    def control_weight():
        parts = []
        for y in range(2):
            for x in range(2):
                for c in range(2):
                    for i in range(4):
                        tiles = [g[y, x, c, j, C0 : C0 + 16, CH * i : CH * i + CH] for j in range(4)]
                        parts.append(jnp.concatenate(tiles, axis=1))
        return jnp.concatenate(parts, axis=0)

    wc_s[...] = mm(control_weight(), permutation()).astype(BF16)

    def project_c(i, _):
        at = rows_at(i)
        e = jnp.exp(mm(n1[at, :], wc_s[...]))
        ew[at, :] = e
        wb[at, :] = e.astype(BF16)
        return 0

    def project_v(i, _):
        at = rows_at(i)
        vv_[at, :] = mm(n1[at, :], weight(V0)).astype(BF16)
        return 0

    def project_q(i, _):
        at = rows_at(i)
        qs[at, :] = (mm(n1[at, :], weight(Q0)).astype(BF16) * (HEAD_DIM**-0.5)).astype(BF16)
        return 0

    def lanes(p):
        return slice(CH * p, CH * p + CH)

    def split(x):
        return [x[:, lanes(p)] for p in pairs]

    def compact(x):
        return x[0:HEAD_DIM, :] + x[HEAD_DIM:CH, :]

    def expand(x):
        return jnp.concatenate([x * leftf, x * rightf], axis=0)

    def pack_row(ref, row):
        hi = row.astype(BF16).astype(F32)
        lo = row - hi
        parts = [a[:, lanes(p)] for a in (hi, lo) for p in pairs]
        parts.append(jnp.zeros((8, CH), F32))
        ref[256:272, :] = jnp.concatenate(parts, axis=0).astype(BF16)

    def unpack_row(x):
        x = x.astype(F32)
        x = x[0:PAIRS, :] + x[PAIRS : 2 * PAIRS, :]
        return jnp.concatenate([x[p : p + 1, :] for p in pairs], axis=1)

    def wide(x):
        return jnp.concatenate([x] * PAIRS, axis=1)

    def scan_step(cur, saved, c, keep, rows_a, rows_b):
        new = [t_mm(a, b) * block_diag for a, b in zip(split(rows_a), split(rows_b))]
        old = [cur[p] for p in pairs]
        for p in pairs:
            saved[c, p] = old[p].astype(BF16)
        for p in pairs:
            cur[p] = keep * old[p] + new[p]

    def place(up):
        return z if up else n_slot - 1 - z

    def toward(up, s):
        return (dp, z + s if up else z - s)

    def edge_gate(up, far):
        if up:
            return same(last_of(base - (far - 1) * n_ch - 1), last_of(base - (far - 2) * n_ch - 1))
        return same(first_of(base + far * n_ch), first_of(base + (far - 1) * n_ch))

    def exchange_copy(idx, src, dst, up, step):
        k = idx * max(n_slot, 4) + step
        if n_slot == 4:
            return remote(src, dst.at[0 if step == 0 else 1], st_send, st_recv, k, toward(up, max(step, 1)))
        return remote(src, dst.at[step], st_send, st_recv, k, toward(up, step))

    def exchange_start(idx, src, dst, up):
        if n_slot == 4:
            @pl.when(lax.rem(place(up), 2) == 0)
            def _():
                exchange_copy(idx, src, dst, up, 0).start()
            return
        for s in range(1, n_slot):
            @pl.when(place(up) + s < n_slot)
            def _():
                exchange_copy(idx, src, dst, up, s).start()

    def exchange_pass(idx, src, dst, up):
        if n_slot == 4:
            @pl.when(place(up) == 1)
            def _():
                exchange_copy(idx, src, dst, up, 0).wait_recv()
                src[...] = (src[...].astype(F32) + edge_gate(up, 1) * dst[0].astype(F32)).astype(BF16)
                for s in (1, 2):
                    exchange_copy(idx, src, dst, up, s).start()

    def exchange_wait(idx, src, dst, up):
        if n_slot == 4:
            @pl.when(place(up) == 3)
            def _():
                exchange_copy(idx, src, dst, up, 0).wait_recv()
                exchange_copy(idx, src, dst, up, 2).wait_recv()
            @pl.when(place(up) == 2)
            def _():
                exchange_copy(idx, src, dst, up, 1).wait_recv()
            gate = jnp.where(place(up) == 3, edge_gate(up, 2), 1.0)
            return dst[0].astype(F32) + gate * dst[1].astype(F32)
        total = 0.0
        for s in range(1, n_slot):
            @pl.when(place(up) >= s)
            def _():
                exchange_copy(idx, src, dst, up, s).wait_recv()
            gate = 1.0
            for far in range(2, s + 1):
                gate = gate * edge_gate(up, far)
            total = total + gate * dst[s].astype(F32)
        return total

    def exchange_end(idx, src, dst, up):
        if n_slot == 4:
            @pl.when(lax.rem(place(up), 2) == 0)
            def _():
                exchange_copy(idx, src, dst, up, 0).wait_send()
            @pl.when(place(up) == 1)
            def _():
                for s in (1, 2):
                    exchange_copy(idx, src, dst, up, s).wait_send()
            return
        for s in range(1, n_slot):
            @pl.when(place(up) + s < n_slot)
            def _():
                exchange_copy(idx, src, dst, up, s).wait_send()

    def pack_state(snd, cur):
        for p in pairs:
            snd[64 * p : 64 * p + 64, :] = compact(cur[p]).astype(BF16)

    def entering(total, e):
        for p in pairs:
            e[p] = expand(total[64 * p : 64 * p + 64, :])
        if total.shape[0] > 256:
            e_z[0:1, :] = unpack_row(total[256:272, :])

    cur_a[...] = jnp.zeros_like(cur_a)
    cur_b[...] = jnp.zeros_like(cur_b)
    cur_z[...] = jnp.zeros_like(cur_z)

    def key_states(c):
        at = rows_at(c, CH)
        keep = same(last_of(base + c - 1), last_of(base + c))
        w = wb[at, :]
        zi = mm(msk[c], w)
        scan_step(cur_a, s_kw, c, keep, kk_[at, :] * wide(g_last[c]), w)
        z_old = cur_z[0:1, :]
        z_st[pl.ds(c, 1), :] = z_old
        inv_z[at, :] = zi
        cur_z[0:1, :] = keep * z_old + zi[CH - 1 : CH, :]

    def value_states(c):
        at = rows_at(c, CH)
        keep = same(last_of(base + c - 1), last_of(base + c))
        scan_step(cur_b, s_wv, c, keep, wb[at, :] * wide(g_last[c]), vv_[at, :])

    lax.fori_loop(0, n_rb, project_c, 0)
    gather(PV, 3)
    gather(PQ, 3)
    chunks(key_states)
    pack_state(snd_a, cur_a)
    pack_row(snd_a, cur_z[0:1, :])
    exchange_start(0, snd_a, rcv_a, True)
    gather(PO, 1)
    gather(PW, 1)
    gather(PV, 4)
    lax.fori_loop(0, n_rb, project_v, 0)
    chunks(value_states)
    pack_state(snd_b, cur_b)
    exchange_start(1, snd_b, rcv_b, True)
    exchange_pass(0, snd_a, rcv_a, True)
    gather(PU, 1)
    gather(PQ, 4)
    lax.fori_loop(0, n_rb, project_q, 0)
    gather(PO, 2)
    gather(PW, 2)

    def two(x):
        return jnp.concatenate([x, x], axis=1)

    def stacks(x):
        return [stack2(a, left, right) for a in split(x)]

    def numerators(c):
        at = rows_at(c, CH)
        m2 = two(msk[c])
        q, k2, w2 = split(qs[at, :]), stacks(kk_[at, :]), stacks(wb[at, :])
        sc = [mm_t(q[p], k2[p]).astype(BF16) * m2 for p in pairs]
        num[at, :] = jnp.concatenate([mm(sc[p], w2[p]) for p in pairs], axis=1)

    chunks(numerators)
    exchange_pass(1, snd_b, rcv_b, True)
    gather(PU, 2)
    gather(PU2, 1)
    gather(PO, 3)
    entering(exchange_wait(0, snd_a, rcv_a, True), e_a)

    def softmax(c):
        at = rows_at(c, CH)
        reach = same(last_of(base - 1), last_of(base + c - 1))
        gpw = wide(g_prev[c])
        z_in = z_st[pl.ds(c, 1), :] + reach * e_z[0:1, :]
        skw = [(s_kw[c, p].astype(F32) + reach * e_a[p]).astype(BF16) for p in pairs]
        q = split(qs[at, :] * gpw)
        iz = 1.0 / (inv_z[at, :] + gpw.astype(F32) * z_in)
        from_state = jnp.concatenate([mm(q[p], skw[p]) for p in pairs], axis=1)
        lg = (num[at, :] + from_state) * iz
        top = jnp.concatenate([per_head(jnp.max, a, -jnp.inf) for a in split(lg)], axis=1)
        ex = jnp.exp(lg - top)
        tot = jnp.concatenate([mm(a.astype(BF16), ones_diag) for a in split(ex)], axis=1)
        pr = ex / tot
        for p in pairs:
            s_kw[c, p] = skw[p]
        num[at, :] = lg
        inv_z[at, :] = iz
        prob[at, :] = pr
        rr_[at, :] = (pr * iz).astype(BF16)

    def mixture(c):
        at = rows_at(c, CH)
        reach = same(last_of(base - 1), last_of(base + c - 1))
        m2 = two(msk[c])
        swv = [(s_wv[c, p].astype(F32) + reach * e_b[p]).astype(BF16) for p in pairs]
        w2, v2 = stacks(wb[at, :]), stacks(vv_[at, :])
        r = rr_[at, :]
        rs, rg = split(r), split(r * wide(g_prev[c]))
        mix = [mm_t(rs[p], w2[p]).astype(BF16) * m2 for p in pairs]
        o = jnp.concatenate([mm(mix[p], v2[p]) + mm(rg[p], swv[p]) for p in pairs], axis=1)
        for p in pairs:
            s_wv[c, p] = swv[p]
        oo_[at, :] = o.astype(BF16)

    chunks(softmax)
    gather(PW, 3)
    entering(exchange_wait(1, snd_b, rcv_b, True), e_b)
    chunks(mixture)
    gather(PU, 3)
    gather(PO, 4)
    gather(PU2, 2)

    def up_w(j):
        at = U0 + 16 * j if isinstance(j, int) else pl.multiple_of(U0 + 16 * j, 16)
        return g[:, :, :, :, pl.ds(at, 16), :].reshape(D, D)

    def down_w(j):
        return g[j // 2, lax.rem(j, 2), :, :, W0:END, :].reshape(D, D)

    c0, c1 = math.sqrt(2.0 / math.pi), 0.044715

    def hidden(i, _):
        at = rows_at(i)
        h = xb[at, :].astype(F32) + mm(oo_[at, :], weight(O0))
        hsum[at, :] = h
        nh, _r = norm_stats(h)
        n = (nh * gain2 + bias2).astype(BF16)
        n2[at, :] = n
        n2t[:, at] = n.T
        return 0

    def feed(j, _):
        def rows_of(i, _):
            at = rows_at(i)
            u = mm(n2[at, :], up_w(j)).astype(BF16)
            dg = mm_t(og[at, :], down_w(j)).astype(BF16)
            sq = u * u
            t = jnp.tanh(u * (c0 + c0 * c1 * sq))
            half = 0.5 + 0.5 * t
            slope = half + u * (1.0 - t * t) * (0.5 * c0 + 1.5 * c0 * c1 * sq)
            cols = pl.ds(pl.multiple_of(j * D, D), D)
            act[at, cols] = u * half
            du[at, cols] = dg * slope
            return 0

        return lax.fori_loop(0, n_rb, rows_of, 0)

    lax.fori_loop(0, n_rb, hidden, 0)
    loaded("og")
    gather(PW, 4)
    gather(PU, 4)

    def put_grad(r0, y, val):
        pg[y, :, :, :, r0 : r0 + 16, :] = val.astype(BF16).reshape(2, 2, 4, 16, D)

    def down_grads(j, _):
        val = t_mm(act[:, pl.ds(pl.multiple_of(j * D, D), D)], og[...])
        pg[j // 2, lax.rem(j, 2), :, :, W0:END, :] = val.astype(BF16).reshape(2, 4, 64, D)
        return 0

    def up_grads(j, _):
        for y in range(2):
            val = mm(n2t[256 * y : 256 * y + 256, :], du[:, pl.ds(pl.multiple_of(j * D, D), D)])
            pg[y, :, :, :, pl.ds(pl.multiple_of(U0 + 16 * j, 16), 16), :] = val.astype(BF16).reshape(2, 2, 4, 16, D)
        return 0

    def out_copy(ref):
        i = [ref is a for a in grad_s].index(True)
        return pltpu.make_async_copy(ref, grad_h[i], out_sem.at[i])

    def store(ref):
        out_copy(ref).start()

    def add_to(dst, src):
        dst[...] = dst[...] + src[...]

    def scatter_copies(p, stage):
        put = lambda src, dst, idx, where: remote(src, dst, rs_send, rs_recv, p * 8 + idx, where)
        if p == PN:
            if stage == 0:
                return [put(ngp.at[:, :, 1 - pc], nrc, 0, at_c)]
            if stage == 1:
                return [put(ngp.at[:, 1 - px, pc], nrx, 1, at_x)]
            if stage == 2:
                return [put(ngp.at[1 - py, px, pc], nry, 2, at_y)]
            return [put(ngp.at[py, px, pc, lax.rem(z + s, n_slot)], nrz.at[s - 1], 4 + s, at_z(s)) for s in range(1, n_slot)]
        r0, r1 = ROWS[p]
        sl = pl.ds(r0, r1 - r0)
        if stage == 0:
            return [put(pg.at[:, :, 1 - pc, :, sl, :], rc.at[:, :, :, sl, :], 0, at_c)]
        if stage == 1:
            return [
                put(pg.at[:, 1 - px, pc, :, sl, la], rx1.at[:, :, sl, :], 1, at_x),
                put(pg.at[1 - py, :, pc, :, sl, lb], ry1.at[:, :, sl, :], 2, at_y),
            ]
        if stage == 2:
            return [
                put(pg.at[1 - py, px, pc, :, sl, la], ry2.at[:, sl, :], 3, at_y),
                put(pg.at[py, 1 - px, pc, :, sl, lb], rx2.at[:, sl, :], 4, at_x),
            ]
        return [
            put(pg.at[py, px, pc, lax.rem(z + s, n_slot), sl, :], rz.at[s - 1, sl, :], 4 + s, at_z(s))
            for s in range(1, n_slot)
        ]

    def scatter_add(p, stage):
        if p == PN:
            if stage == 1:
                for y in range(2):
                    for x in range(2):
                        add_to(ngp.at[y, x, pc], nrc.at[y, x])
            elif stage == 2:
                for y in range(2):
                    add_to(ngp.at[y, px, pc], nrx.at[y])
            elif stage == 3:
                add_to(ngp.at[py, px, pc], nry)
            else:
                total = ngp[py, px, pc, z].astype(F32)
                for s in range(1, n_slot):
                    total = total + nrz[s - 1].astype(F32)
                ng_o[...] = total
                store(ng_o)
            return
        r0, r1 = ROWS[p]
        sl = pl.ds(r0, r1 - r0)
        if stage == 1:
            def body(i, _):
                y, x = i // 2, lax.rem(i, 2)
                add_to(pg.at[y, x, pc, :, sl, :], rc.at[y, x, :, sl, :])
                return 0
            lax.fori_loop(0, 4, body, 0)
        elif stage == 2:
            def body(i, _):
                add_to(pg.at[i, px, pc, :, sl, la], rx1.at[i, :, sl, :])
                add_to(pg.at[py, i, pc, :, sl, lb], ry1.at[i, :, sl, :])
                return 0
            lax.fori_loop(0, 2, body, 0)
        elif stage == 3:
            add_to(pg.at[py, px, pc, :, sl, la], ry2.at[:, sl, :])
            add_to(pg.at[py, px, pc, :, sl, lb], rx2.at[:, sl, :])
        else:
            total = pg[py, px, pc, z, sl, :].astype(F32)
            for s in range(1, n_slot):
                total = total + rz[s - 1, sl, :].astype(F32)
            if p in (PU, PU2):
                for j in range(2):
                    at = 2 * D * (p - PU) + D * j
                    wu_o[:, at : at + D] = total[16 * j : 16 * j + 16, :]
                if p == PU2:
                    store(wu_o)
            elif p == PC:
                for i in range(4):
                    wc_o[16 * i : 16 * i + 16, :] = total[:, lanes(i)]
                store(wc_o)
            else:
                dst = {PV: wv_o, PQ: wq_o, PK: wk_o, PO: wo_o, PW: wd_o}[p]
                dst[...] = total
                store(dst)

    def scatter(p, stage):
        if not comm:
            return
        if stage > 0:
            for copy in scatter_copies(p, stage - 1):
                copy.wait_recv()
            scatter_add(p, stage)
        if stage < 4:
            for copy in scatter_copies(p, stage):
                copy.start()

    for j in range(2):
        feed(j, 0)
        if j == 0:
            gather(PU2, 3)
    lax.fori_loop(0, 2, up_grads, 0)
    scatter(PU, 0)
    gather(PU2, 4)
    for j in range(2, 4):
        feed(j, 0)
    lax.fori_loop(2, 4, up_grads, 0)
    scatter(PU, 1)
    scatter(PU2, 0)
    lax.fori_loop(0, 4, down_grads, 0)
    scatter(PW, 0)
    scatter(PU2, 1)

    def feed_back(i, acc):
        at = rows_at(i)
        dn = jnp.zeros((rb, D), F32)
        for j in range(4):
            dn = dn + mm_t(du[at, D * j : D * j + D], up_w(j))
        nh, rstd = norm_stats(hsum[at, :])
        dh = og[at, :].astype(F32) + norm_back(dn, nh, rstd, gain2)
        hid[at, :] = dh
        a = dh.astype(BF16)
        da[at, :] = a
        do[at, :] = mm_t(a, weight(O0)).astype(BF16)
        return (acc[0] + jnp.sum(dn * nh, axis=0, keepdims=True), acc[1] + jnp.sum(dn, axis=0, keepdims=True))

    zero_row = jnp.zeros((1, D), F32)
    gain2_g, bias2_g = lax.fori_loop(0, n_rb, feed_back, (zero_row, zero_row))
    for y in range(2):
        put_grad(O0, y, t_mm(oo_[:, 256 * y : 256 * y + 256], da[...]))
    scatter(PO, 0)
    scatter(PW, 1)

    cur_a[...] = jnp.zeros_like(cur_a)
    cur_b[...] = jnp.zeros_like(cur_b)
    cur_z[...] = jnp.zeros_like(cur_z)

    def slot_states(i):
        c = n_ch - 1 - i
        at = rows_at(c, CH)
        keep = same(first_of(base + c), first_of(base + c + 1))
        scan_step(cur_a, s_r, c, keep, rr_[at, :] * wide(g_first[c]), do[at, :])

    chunks(slot_states)
    pack_state(snd_d, cur_a)
    exchange_start(3, snd_d, rcv_d, False)
    scatter(PU, 2)

    def slot_grads(i):
        c = n_ch - 1 - i
        at = rows_at(c, CH)
        m2 = two(msk[c])
        gpw = wide(g_prev[c])
        keep = same(first_of(base + c), first_of(base + c + 1))
        w2, v2 = stacks(wb[at, :]), stacks(vv_[at, :])
        do_c = do[at, :]
        ds, dg = split(do_c), split(do_c * gpw)
        dmix = [mm_t(ds[p], v2[p]).astype(BF16) * m2 for p in pairs]
        dr = jnp.concatenate([mm(dmix[p], w2[p]) + mm_t(dg[p], s_wv[c, p]) for p in pairs], axis=1)
        iz, pr, lg = inv_z[at, :], prob[at, :], num[at, :]
        dpr = dr * iz
        inner = jnp.concatenate([mm(a.astype(BF16), ones_diag) for a in split(pr * dpr)], axis=1)
        dl = pr * (dpr - inner)
        dn_c = (dl * iz).astype(BF16)
        dz_c = (-(dpr * pr + dl * lg) * iz).astype(BF16)
        firsts = mm(mskt[c][0:16, :], dz_c)
        scan_step(cur_b, s_n, c, keep, qs[at, :] * wide(g_first[c]), dn_c)
        z_old = cur_z[0:1, :]
        z_r[pl.ds(c, 1), :] = z_old
        cur_z[0:1, :] = keep * z_old + firsts[0:1, :]
        dnum_[at, :] = dn_c
        dz_[at, :] = dz_c

    chunks(slot_grads)
    pack_state(snd_c, cur_b)
    pack_row(snd_c, cur_z[0:1, :])
    exchange_start(2, snd_c, rcv_c, False)
    exchange_pass(3, snd_d, rcv_d, False)
    scatter(PU2, 2)
    scatter(PO, 1)

    def query_grads(c):
        at = rows_at(c, CH)
        m2 = two(msk[c])
        dn_c = dnum_[at, :]
        dn, dg = split(dn_c), split(dn_c * wide(g_prev[c]))
        w2, k2 = stacks(wb[at, :]), stacks(kk_[at, :])
        dsc = [mm_t(dn[p], w2[p]).astype(BF16) * m2 for p in pairs]
        dq = jnp.concatenate([mm(dsc[p], k2[p]) + mm_t(dg[p], s_kw[c, p]) for p in pairs], axis=1)
        dq_[at, :] = (dq * (HEAD_DIM**-0.5)).astype(BF16)

    chunks(query_grads)
    for y in range(2):
        put_grad(Q0, y, mm(n1t[256 * y : 256 * y + 256, :], dq_[...]))
    scatter(PQ, 0)
    exchange_pass(2, snd_c, rcv_c, False)

    def near_grads(c):
        at = rows_at(c, CH)
        mt = mskt[c]
        mt2 = two(mt)
        w, v, k = split(wb[at, :]), split(vv_[at, :]), split(kk_[at, :])
        q2, dn2, r2, do2 = (stacks(ref[at, :]) for ref in (qs, dnum_, rr_, do))
        dsc_t = [mm_t(w[p], dn2[p]).astype(BF16) * mt2 for p in pairs]
        dmix_t = [mm_t(v[p], do2[p]).astype(BF16) * mt2 for p in pairs]
        sc_t = [mm_t(k[p], q2[p]).astype(BF16) * mt2 for p in pairs]
        dk = jnp.concatenate([mm(dsc_t[p], q2[p]) for p in pairs], axis=1)
        dw = jnp.concatenate([mm(dmix_t[p], r2[p]) + mm(sc_t[p], dn2[p]) for p in pairs], axis=1)
        num[at, :] = dk
        inv_z[at, :] = dw + mm(mt, dz_[at, :])

    chunks(near_grads)
    scatter(PQ, 1)
    scatter(PU, 3)
    scatter(PO, 2)
    entering(exchange_wait(3, snd_d, rcv_d, False), e_b)

    def value_grads(c):
        at = rows_at(c, CH)
        mt2 = two(mskt[c])
        w_c = wb[at, :]
        w, wg = split(w_c), split(w_c * wide(g_next[c]))
        reach = same(first_of(base + n_ch), first_of(base + c + 1))
        r2, do2 = stacks(rr_[at, :]), stacks(do[at, :])
        st_r = [(s_r[c, p].astype(F32) + reach * e_b[p]).astype(BF16) for p in pairs]
        mix_t = [mm_t(w[p], r2[p]).astype(BF16) * mt2 for p in pairs]
        dv = jnp.concatenate([mm(mix_t[p], do2[p]) + mm(wg[p], st_r[p]) for p in pairs], axis=1)
        for p in pairs:
            s_r[c, p] = st_r[p]
        dv_[at, :] = dv.astype(BF16)

    chunks(value_grads)
    for y in range(2):
        put_grad(V0, y, mm(n1t[256 * y : 256 * y + 256, :], dv_[...]))
    scatter(PV, 0)
    scatter(PW, 2)
    scatter(PU2, 3)
    scatter(PQ, 2)
    entering(exchange_wait(2, snd_c, rcv_c, False), e_a)

    def far_grads(c):
        at = rows_at(c, CH)
        reach = same(first_of(base + n_ch), first_of(base + c + 1))
        gnw = wide(g_next[c])
        z_in = z_r[pl.ds(c, 1), :] + reach * e_z[0:1, :]
        wg, vg, kg = (split(ref[at, :] * gnw) for ref in (wb, vv_, kk_))
        st_n = [(s_n[c, p].astype(F32) + reach * e_a[p]).astype(BF16) for p in pairs]
        st_r = [s_r[c, p] for p in pairs]
        dk = num[at, :] + jnp.concatenate([mm_t(wg[p], st_n[p]) for p in pairs], axis=1)
        dw = inv_z[at, :] + gnw.astype(F32) * z_in
        dw = dw + jnp.concatenate([mm_t(vg[p], st_r[p]) + mm(kg[p], st_n[p]) for p in pairs], axis=1)
        dk_[at, :] = dk.astype(BF16)
        dphi_[at, :] = (dw * ew[at, :]).astype(BF16)

    chunks(far_grads)

    for y in range(2):
        cols = slice(256 * y, 256 * y + 256)
        val = mm_t(mm(n1t[cols, :], dphi_[...]).astype(BF16), permutation()).astype(BF16)
        for x in range(2):
            for c in range(2):
                for i in range(4):
                    r = ((x * 2 + c) * 4 + i) * 16
                    for j in range(4):
                        pg[y, x, c, j, C0 : C0 + 16, CH * i : CH * i + CH] = val[r : r + 16, lanes(j)]
    scatter(PC, 0)
    for y in range(2):
        put_grad(K0, y, mm(n1t[256 * y : 256 * y + 256, :], dk_[...]))
    scatter(PK, 0)
    scatter(PV, 1)
    scatter(PO, 3)
    scatter(PQ, 3)

    def input_grads(i, acc):
        at = rows_at(i)
        dn = mm_t(dq_[at, :], weight(Q0)) + mm_t(dk_[at, :], weight(K0)) + mm_t(dv_[at, :], weight(V0)) + mm_t(dphi_[at, :], wc_s[...])
        nh, rstd = norm_stats(xb[at, :].astype(F32))
        tg_o[at, :] = hid[at, :] + norm_back(dn, nh, rstd, gain1)
        return (acc[0] + jnp.sum(dn * nh, axis=0, keepdims=True), acc[1] + jnp.sum(dn, axis=0, keepdims=True))

    def outputs(i, _):
        at = rows_at(i)
        out = hsum[at, :]
        for j in range(4):
            out = out + mm(act[at, D * j : D * j + D], down_w(j))
        out_o[at, :] = out.astype(BF16)
        return 0

    gain1_g, bias1_g = lax.fori_loop(0, n_rb, input_grads, (zero_row, zero_row))
    tg_copy = pltpu.make_async_copy(tg_o, tg_h, out_sem.at[8])
    tg_copy.start()
    norm_g = jnp.concatenate([gain1_g, bias1_g, gain2_g, bias2_g, jnp.zeros((12, D), F32)], axis=0)
    if comm:
        for y in range(2):
            for x in range(2):
                for c in range(2):
                    for j in range(4):
                        d = ((y * 2 + x) * 2 + c) * 4 + j
                        ngp[y, x, c, j] = norm_g[:, lanes(d // 8)].astype(BF16)
    else:
        ng_o[...] = norm_g
    scatter(PN, 0)
    scatter(PC, 1)
    scatter(PK, 1)
    scatter(PV, 2)
    scatter(PW, 3)
    scatter(PN, 1)
    lax.fori_loop(0, n_rb, outputs, 0)
    out_done = pltpu.make_async_copy(out_o, out_h, out_sem.at[9])
    out_done.start()
    scatter(PC, 2)
    scatter(PK, 2)
    scatter(PN, 2)
    for args in ((0, snd_a, rcv_a, True), (1, snd_b, rcv_b, True), (2, snd_c, rcv_c, False), (3, snd_d, rcv_d, False)):
        exchange_end(*args)
    if comm:
        for p in range(len(ROWS) + 1):
            for stage in (*range(4), 4, 5) if p in EARLY else range(4):
                for copy in gather_copies(p, stage):
                    copy.wait_send()
    scatter(PV, 3)
    scatter(PU, 4)
    scatter(PU2, 4)
    scatter(PC, 3)
    scatter(PK, 3)
    scatter(PN, 3)
    if comm:
        for p in range(len(ROWS) + 1):
            for stage in range(3):
                for copy in scatter_copies(p, stage):
                    copy.wait_send()
    for p in (PO, PW, PQ, PV, PC, PK, PN):
        scatter(p, 4)
    tg_copy.wait()
    out_done.wait()
    if comm:
        for ref in grad_s:
            out_copy(ref).wait()
        for p in range(len(ROWS) + 1):
            for copy in scatter_copies(p, 3):
                copy.wait_send()


def vm(shape, dtype):
    return pltpu.VMEM(shape, dtype)


def run_layer(rows, n_slot, seg_rows, comm, operands):
    n_ch = rows // CH
    act_shape = (rows, D)
    hbm, vmem = pl.BlockSpec(memory_space=pl.ANY), pl.BlockSpec(memory_space=pltpu.VMEM)
    sds = jax.ShapeDtypeStruct
    outs = [sds(act_shape, BF16), sds(act_shape, F32)]
    grads = [(16, D)] * 4 + [(64, CH), (16, FF), (64, D), (16, CH)]
    if comm:
        outs += [sds(shape, F32) for shape in grads]
        out_specs = [hbm] * len(outs)
    else:
        outs += [sds((*GRID, END, D), BF16), sds((16, D), F32)]
        out_specs = [hbm, hbm, vmem, vmem]
    b, f = (lambda: vm(act_shape, BF16)), (lambda: vm(act_shape, F32))
    state = lambda dtype: vm((n_ch, PAIRS, CH, CH), dtype)
    sems = lambda n: pltpu.SemaphoreType.DMA((n,))
    scratch = [
        vm((*GRID, END, D), BF16), vm((*GRID, 16, CH), BF16), b(), vm((seg_rows, CH), jnp.int32), b(), b(), b(), b(), b(), b(),
        f(), f(), f(), f(), b(), b(), f(), b(), vm((rows, FF), BF16), vm((rows, FF), BF16), b(), b(),
        vm((D, rows), BF16), vm((D, rows), BF16), b(), b(), b(), b(), f(),
        state(BF16), state(BF16), vm((max(8, n_ch), D), F32), state(BF16), state(BF16), vm((max(8, n_ch), D), F32),
        vm((PAIRS, CH, CH), F32), vm((PAIRS, CH, CH), F32), vm((8, D), F32),
        vm((PAIRS, CH, CH), F32), vm((PAIRS, CH, CH), F32), vm((8, D), F32),
    ]
    scratch += [vm((n_ch, CH, CH), BF16)] * 6
    long, short = (272, CH), (256, CH)
    scratch += [vm(long, BF16), vm(short, BF16), vm((n_slot, *long), BF16), vm((n_slot, *short), BF16)] * 2
    scratch += [vm((D, D), BF16), sems(4 * max(n_slot, 4)), sems(4 * max(n_slot, 4)), sems(20), sems(10)]
    if comm:
        ny, nx, nc, nz = GRID
        scratch += [
            vm((*GRID, END, D), BF16), vm((*GRID, 16, CH), BF16),
            vm((ny, nx, nz, END, D), BF16), vm((ny, nz, END, D // 2), BF16), vm((nx, nz, END, D // 2), BF16),
            vm((nz, END, D // 2), BF16), vm((nz, END, D // 2), BF16), vm((nz - 1, END, D), BF16),
            vm((ny, nx, nz, 16, CH), BF16), vm((ny, nz, 16, CH), BF16), vm((nz, 16, CH), BF16), vm((nz - 1, 16, CH), BF16),
        ]
        scratch += [sems(24 * (len(ROWS) + 1))] * 2 + [sems(8 * (len(ROWS) + 1))] * 2
        scratch += [vm(operands[7].shape, BF16), vm((4, 1, operands[-1].shape[1]), BF16)] + [vm(shape, F32) for shape in grads]
    cfg = dict(rows=rows, n_slot=n_slot, comm=comm)
    return pl.pallas_call(
        functools.partial(kernel_body, cfg),
        out_shape=outs,
        in_specs=[hbm] * len(operands),
        out_specs=out_specs,
        scratch_shapes=scratch,
        compiler_params=pltpu.CompilerParams(collective_id=0, has_side_effects=True, vmem_limit_bytes=63 * 2**20),
    )(*operands)


def finish_body(*refs):
    src, dst, rest = refs[:10], refs[10:23], refs[23:]
    *held, sem_in, sem_out = rest
    jobs = [(1, 0), (1, 1), (0, 0), (0, 1)] + [(i, None) for i in (2, 3, 4, 5, 7, 8)]

    def copy(k, come):
        i, part = jobs[k]
        buf = held[(0, 1, 2, 3, 4, 5, None, 6, 7)[i]]
        cut = lambda ref: ref if part is None else ref.at[pl.ds(part * (ref.shape[0] // 2), ref.shape[0] // 2)]
        if come:
            return pltpu.make_async_copy(cut(src[i]), cut(buf), sem_in.at[k])
        return pltpu.make_async_copy(cut(buf), cut(dst[i]), sem_out.at[k])

    for k in range(len(jobs)):
        copy(k, True).start()
    dst[6][...] = src[6][...].T
    wide = dst[9].shape[1]
    dev = lax.axis_index("dp") * lax.axis_size("slot") + lax.axis_index("slot")
    vals = pltpu.roll(src[9][...], lax.rem(CH - wide * lax.rem(dev, CH // wide), CH), 1)
    for i in range(4):
        dst[9 + i][...] = vals[i : i + 1, 0:wide]
    for k in range(len(jobs)):
        copy(k, True).wait()
        copy(k, False).start()
    for k in range(len(jobs)):
        copy(k, False).wait()


def finish(outs, wide):
    hbm, vmem = pl.BlockSpec(memory_space=pl.ANY), pl.BlockSpec(memory_space=pltpu.VMEM)
    sds = jax.ShapeDtypeStruct
    shapes = [sds(a.shape, a.dtype) for a in outs[:9]] + [sds((1, wide), F32)] * 4
    shapes[6] = sds(outs[6].shape[::-1], F32)
    return pl.pallas_call(
        finish_body,
        out_shape=shapes,
        in_specs=[vmem if i in (6, 9) else hbm for i in range(10)],
        out_specs=[vmem if i == 6 or i > 8 else hbm for i in range(13)],
        scratch_shapes=[vm(outs[i].shape, outs[i].dtype) for i in (0, 1, 2, 3, 4, 5, 7, 8)] + [pltpu.SemaphoreType.DMA((10,))] * 2,
        compiler_params=pltpu.CompilerParams(vmem_limit_bytes=63 * 2**20),
    )(*outs)


def layer(
    tokens, segment_ids, w_query, w_key, w_value, w_out, w_control, w_up, w_down,
    norm1_gain, norm1_bias, norm2_gain, norm2_bias, out_grad,
):
    n_slot, n_dp = lax.axis_size("slot"), lax.axis_size("dp")
    n_dev = n_slot * n_dp
    rows = tokens.shape[0] // n_slot
    seg = segment_ids.reshape(-1, CH)
    norms = (norm1_gain, norm1_bias, norm2_gain, norm2_bias)
    if n_dev == math.prod(GRID) and n_slot == GRID[3]:
        outs = run_layer(rows, n_slot, seg.shape[0], True, (
            tokens, seg, out_grad, w_query, w_key, w_value, w_out,
            w_control.transpose(1, 2, 0).reshape(CH, -1), w_up, w_down, *(a.reshape(1, -1) for a in norms),
        ))
        outs = finish(outs, norm1_gain.shape[0])
        control = outs[6].reshape(*w_control.shape[1:], -1).transpose(2, 0, 1)
        return (*outs[:6], control, *outs[7:9], *(a.reshape(-1) for a in outs[9:]))

    norms = jnp.stack(norms)
    both = ("dp", "slot")
    gather = lambda a: lax.all_gather(a, both, axis=0, tiled=True)
    n_blk = math.prod(GRID)
    wc = lax.all_gather(lax.all_gather(w_control, "dp", axis=0, tiled=True), "slot", axis=2, tiled=True)
    gw = SLOTS // GRID[3]
    wc = wc.reshape(8, 4, 16, HEADS, GRID[3], gw).transpose(0, 4, 2, 1, 3, 5).reshape(n_blk, 16, D)
    norm_all = lax.all_gather(norms, both, axis=1, tiled=True)
    norm_all = norm_all.reshape(4, 4, CH).transpose(1, 0, 2).reshape(16, CH)
    norm_blk = jnp.zeros((n_blk, 16, CH), BF16).at[0].set(norm_all).reshape(*GRID, 16, CH)
    split = lambda a: gather(a).reshape(n_blk, -1, D)
    up = gather(w_up).reshape(n_blk, 16, 4, D).transpose(0, 2, 1, 3).reshape(n_blk, 64, D)
    packed = jnp.concatenate(
        [split(w_key), wc, split(w_value), split(w_query), split(w_out), up, split(w_down)], axis=1
    ).reshape(*GRID, END, D)
    out, tg, part, ng = run_layer(rows, n_slot, seg.shape[0], False, (tokens, seg, out_grad, packed, norm_blk))
    part = part.reshape(n_blk, END, D).astype(F32)
    scatter = lambda a, dim=0: lax.psum_scatter(a, both, scatter_dimension=dim, tiled=True)
    full = lambda r0, r1: part[:, r0:r1].reshape(-1, D)
    wcg = part[:, C0:V0].reshape(8, GRID[3], 16, 4, HEADS, gw).transpose(0, 3, 2, 4, 1, 5).reshape(D, HEADS, SLOTS)
    wcg = lax.psum_scatter(lax.psum_scatter(wcg, "dp", scatter_dimension=0, tiled=True), "slot", scatter_dimension=2, tiled=True)
    upg = part[:, U0:W0].reshape(n_blk, 4, 16, D).transpose(0, 2, 1, 3).reshape(D, FF)
    ng = scatter(ng[:4], 1)
    return (
        out, tg, scatter(full(Q0, O0)), scatter(full(K0, C0)), scatter(full(V0, Q0)), scatter(full(O0, U0)),
        wcg, scatter(upg), scatter(full(W0, END)), ng[0], ng[1], ng[2], ng[3],
    )


def solution(mesh):
    both = P(("dp", "slot"), None)
    vec = P(("dp", "slot"))
    control = P("dp", None, "slot")
    in_specs = (
        P("dp", None), P("dp"), both, both, both, both, control, both, both, vec, vec, vec, vec, both,
    )
    out_specs = (both, both, both, both, both, both, control, both, both, vec, vec, vec, vec)
    return jax.shard_map(layer, mesh=mesh, in_specs=in_specs, out_specs=out_specs, check_vma=False)
```

```python
import functools
import math

import jax
import jax.numpy as jnp
from jax import lax
from jax.experimental import pallas as pl
from jax.experimental.pallas import tpu as pltpu
from jax.sharding import PartitionSpec as P

D = 512
HEADS = 8
HEAD_DIM = 64
SLOTS = 64
FF = 2048
EPS = 1e-05
CH = 128
PAIRS = HEADS // 2
F32 = jnp.float32
BF16 = jnp.bfloat16
MESH = pl.DeviceIdType.MESH

K0, C0, V0, Q0, O0, U0, END = 0, 16, 32, 48, 64, 80, 208
GRID = (2, 2, 2, 4)
ROWS = ((K0, C0), (C0, V0), (V0, Q0), (Q0, O0), (O0, U0), *((U0 + 32 * j, U0 + 32 * j + 32) for j in range(4)))
PK, PC, PV, PQ, PO, PF, PN = 0, 1, 2, 3, 4, 5, 9


def mm(a, b):
    return jnp.dot(a, b, preferred_element_type=F32)


def mm_t(a, b):
    return lax.dot_general(a, b, (((1,), (1,)), ((), ())), preferred_element_type=F32)


def t_mm(a, b):
    return lax.dot_general(a, b, (((0,), (0,)), ((), ())), preferred_element_type=F32)


def half_lanes(dtype):
    lane = lax.broadcasted_iota(jnp.int32, (1, CH), 1)
    left = jnp.where(lane < HEAD_DIM, 1.0, 0.0)
    return left.astype(dtype), (1.0 - left).astype(dtype)


def stack2(x, left, right):
    return jnp.concatenate([x * left, x * right], axis=0)


def per_head(op, x, fill):
    lane = lax.broadcasted_iota(jnp.int32, x.shape, 1)
    first = lane < HEAD_DIM
    a = op(jnp.where(first, x, fill), axis=1, keepdims=True)
    b = op(jnp.where(first, fill, x), axis=1, keepdims=True)
    return jnp.where(first, a, b)


def norm_stats(x):
    center = x - jnp.mean(x, axis=-1, keepdims=True)
    rstd = lax.rsqrt(jnp.mean(center * center, axis=-1, keepdims=True) + EPS)
    return center * rstd, rstd


def norm_back(dn, nh, rstd, gain):
    e = dn * gain
    return (e - jnp.mean(e, axis=-1, keepdims=True) - nh * jnp.mean(e * nh, axis=-1, keepdims=True)) * rstd


def kernel_body(cfg, *refs):
    refs = list(refs)
    take = lambda n: [refs.pop(0) for _ in range(n)]
    rows, n_slot, comm = cfg["rows"], cfg["n_slot"], cfg["comm"]
    n_ch = rows // CH
    rb = rows if rows <= 768 else 256
    n_rb = rows // rb
    (tok_in, seg_in, og_in) = take(3)
    if comm:
        (wq_in, wk_in, wv_in, wo_in, wc_in, wu_in, wd_in, *norm_in) = take(11)
        out_h, tg_h, *grad_h = take(10)
    else:
        (g_in, gn_in) = take(2)
        (out_h, tg_h, pg, ng_o) = take(4)
    (g, gn, xb, seg, og, n1, qs, kk_, vv_, wb, ew, num, inv_z, prob, rr_, oo_, hid, n2, act, du, da, do) = take(22)
    (n1t, n2t, dq_, dk_, dv_, dphi_, hsum) = take(7)
    (s_kw, s_wv, z_st, s_r, s_n, z_r) = take(6)
    (cur_a, cur_b, cur_z, e_a, e_b, e_z) = take(6)
    (msk, mskt, g_prev, g_last, g_next, g_first) = take(6)
    (snd_a, snd_b, rcv_a, rcv_b, snd_c, snd_d, rcv_c, rcv_d) = take(8)
    (wc_s, st_send, st_recv, in_sem, out_sem) = take(5)
    if comm:
        (pg, ngp, rc, rx1, ry1, ry2, rx2, rz, nrc, nrx, nry, nrz) = take(12)
        (ag_send, ag_recv, rs_send, rs_recv) = take(4)
        (wct, nv) = take(2)
        (up_s, up_g) = take(2)
        grad_s = take(8)
        (wq_o, wk_o, wv_o, wo_o, wc_o, wu_o, wd_o, ng_o) = grad_s
    assert not refs
    tg_o, out_o = prob, oo_
    dnum_, dz_ = du.at[:, 0:D], du.at[:, D : 2 * D]

    dp = lax.axis_index("dp")
    z = lax.axis_index("slot")
    left, right = half_lanes(BF16)
    leftf, rightf = half_lanes(F32)
    ri = lax.broadcasted_iota(jnp.int32, (CH, CH), 0)
    ci = lax.broadcasted_iota(jnp.int32, (CH, CH), 1)
    block_diag = jnp.where((ri < HEAD_DIM) == (ci < HEAD_DIM), 1.0, 0.0).astype(F32)
    ones_diag = block_diag.astype(BF16)
    pairs = range(PAIRS)

    if comm:
        ny, nx, nc, nz = GRID
        py, px, pc = dp // (nx * nc), lax.rem(dp // nc, nx), lax.rem(dp, nc)
        at_x = ((py * nx + (1 - px)) * nc + pc, z)
        at_y = (((1 - py) * nx + px) * nc + pc, z)
        at_c = ((py * nx + px) * nc + (1 - pc), z)

    def at_z(s):
        return (dp, lax.rem(z + s, n_slot))

    def remote(src, dst, send_sem, recv_sem, idx, where):
        return pltpu.make_async_remote_copy(
            src_ref=src, dst_ref=dst, send_sem=send_sem.at[idx], recv_sem=recv_sem.at[idx],
            device_id=where, device_id_type=MESH,
        )

    loads = {}

    def load(name, src, dst):
        copy = pltpu.make_async_copy(src, dst, in_sem.at[sum(map(len, loads.values()))])
        copy.start()
        loads.setdefault(name, []).append(copy)

    def loaded(name):
        for copy in loads.get(name, ()):
            copy.wait()

    if comm:
        my = g.at[py, px, pc, z]
        load(PK, wk_in, my.at[K0:C0])
        for i, ref in enumerate(norm_in):
            load(PN, ref, nv.at[i])
        load(PC, wc_in, wct)
        load(PV, wv_in, my.at[V0:Q0])
        load(PQ, wq_in, my.at[Q0:O0])
    else:
        load(PK, g_in, g)
        load(PK, gn_in, gn)
    load("tok", tok_in.at[pl.ds(pl.multiple_of(z * rows, CH), rows)], xb)
    load("seg", seg_in, seg)
    if comm:
        load(PO, wo_in, my.at[O0:U0])
        load("up", wu_in, up_s)
        for j in range(4):
            load(PF + j, wd_in.at[16 * j : 16 * j + 16], my.at[U0 + 32 * j + 16 : U0 + 32 * j + 32])
    load("og", og_in, og)

    for ref in (rcv_a, rcv_b, rcv_c, rcv_d):
        ref[...] = jnp.zeros_like(ref)
    bar = pltpu.get_barrier_semaphore()
    peers = [at_z(s) for s in range(1, n_slot)]
    if comm:
        peers += [at_x, at_y, at_c]
    for peer in peers:
        pl.semaphore_signal(bar, inc=1, device_id=peer, device_id_type=MESH)
    pl.semaphore_wait(bar, len(peers))

    la, lb = pl.ds(0, D // 2), pl.ds(D // 2, D // 2)

    EARLY = (PF, PF + 1, PF + 2, PF + 3)

    def gather_copies(p, stage):
        put = lambda ref, idx, where, src=None: remote(ref if src is None else src, ref, ag_send, ag_recv, p * 24 + idx, where)
        if p == PN:
            if stage == 0:
                return [put(gn.at[py, px, pc, z], s - 1, at_z(s)) for s in range(1, n_slot)]
            return [put(*((gn.at[py, px, pc], 3, at_x), (gn.at[py, :, pc], 5, at_y), (gn.at[:, :, pc], 7, at_c))[stage - 1])]
        r0, r1 = ROWS[p]
        sl = pl.ds(r0, r1 - r0)
        if stage == 0:
            src = wk_in if p == PK else None
            return [put(g.at[py, px, pc, z, sl], s - 1, at_z(s), src) for s in range(1, n_slot)]
        if stage == 3:
            return [put(g.at[:, :, pc, :, sl, :], 7, at_c)]
        if p not in EARLY:
            which, base_idx = [slice(None)], 3
        elif stage > 3:
            which, base_idx = [z], 8
        else:
            which, base_idx = [lax.rem(z + s, n_slot) for s in range(1, n_slot)], 12
        copies = []
        for k, zz in enumerate(which):
            if stage in (1, 4):
                copies += [
                    put(g.at[py, px, pc, zz, sl, la], base_idx + 4 * k, at_x),
                    put(g.at[py, px, pc, zz, sl, lb], base_idx + 4 * k + 1, at_y),
                ]
            else:
                copies += [
                    put(g.at[py, :, pc, zz, sl, la], base_idx + 4 * k + 2, at_y),
                    put(g.at[:, px, pc, zz, sl, lb], base_idx + 4 * k + 3, at_x),
                ]
        return copies

    def gather(p, stage):
        if not comm:
            return
        if stage == 0:
            if p not in (PK, PC, PN, *EARLY):
                loaded(p)
        else:
            for copy in gather_copies(p, stage - 1):
                copy.wait_recv()
        if stage == 3 and p in EARLY:
            for copy in gather_copies(p, 5):
                copy.wait_recv()
        if stage < 4:
            for copy in gather_copies(p, stage):
                copy.start()

    def gather_own(p, stage):
        if not comm:
            return
        if stage == 4:
            loaded(p)
        else:
            for copy in gather_copies(p, 4):
                copy.wait_recv()
        for copy in gather_copies(p, stage):
            copy.start()

    def quarters():
        a = lax.broadcasted_iota(jnp.int32, (D, D), 0)
        b = lax.broadcasted_iota(jnp.int32, (D, D), 1)
        return jnp.where(b == (lax.rem(a, 64) // 16) * CH + (a // 64) * 16 + lax.rem(a, 16), 1.0, 0.0).astype(BF16)

    def weight(r0):
        return g[:, :, :, :, r0 : r0 + 16, :].reshape(D, D)

    gather(PK, 0)
    if comm:
        loaded(PN)
        each = nv.shape[2]
        dev = dp * n_slot + z
        vals = [nv[i].astype(F32) for i in range(4)] + [jnp.zeros((12, each), F32)]
        a = lax.broadcasted_iota(jnp.int32, (each, CH), 0)
        b = lax.broadcasted_iota(jnp.int32, (each, CH), 1)
        place = jnp.where(b == a + each * lax.rem(dev, CH // each), 1.0, 0.0).astype(BF16)
        a = lax.broadcasted_iota(jnp.int32, (16, 16), 0)
        b = lax.broadcasted_iota(jnp.int32, (16, 16), 1)
        down = jnp.where(a == b + 4 * (dev // (CH // each)), 1.0, 0.0).astype(BF16)
        vals = mm(jnp.concatenate(vals, axis=0).astype(BF16), place).astype(BF16)
        gn[py, px, pc, z] = mm(down, vals).astype(BF16)
        gather(PN, 0)
        loaded(PC)
        a = lax.broadcasted_iota(jnp.int32, (wct.shape[1], wct.shape[1]), 0)
        b = lax.broadcasted_iota(jnp.int32, (wct.shape[1], wct.shape[1]), 1)
        flat = mm_t(jnp.where(a == b, 1.0, 0.0).astype(BF16), wct[...]).astype(BF16)
        for i in range(4):
            my[C0:V0, CH * i : CH * i + CH] = flat[16 * i : 16 * i + 16, :]
        gather(PC, 0)
        loaded(PK)
        loaded("up")
        for b in range(4):
            some = mm(up_s[:, D * b : D * b + D], quarters()).astype(BF16)
            for j in range(4):
                my[U0 + 32 * j : U0 + 32 * j + 16, CH * b : CH * b + CH] = some[:, CH * j : CH * j + CH]
        for p in EARLY:
            gather_own(p, 4)
    else:
        loaded(PK)

    seg_rows = seg.shape[0]

    def seg_row(i):
        return seg[pl.ds(jnp.clip(i, 0, seg_rows - 1), 1), :].astype(F32)

    def first_of(i):
        return seg_row(i)[:, 0:1]

    def last_of(i):
        return seg_row(i)[:, CH - 1 : CH]

    base = z * n_ch

    def same(a, b):
        return jnp.where(a == b, 1.0, 0.0).astype(F32)

    def rows_at(i, n=rb):
        return pl.ds(i * n if isinstance(i, int) else pl.multiple_of(i * n, n), n)

    def chunks(step):
        for i in range(n_ch):
            step(i)

    def make_masks(c):
        row = jnp.broadcast_to(seg_row(base + c), (CH, CH))
        col = row.T
        eq = row == col
        msk[c] = jnp.where(eq & (ci <= ri), 1.0, 0.0).astype(BF16)
        mskt[c] = jnp.where(eq & (ri <= ci), 1.0, 0.0).astype(BF16)
        g_prev[c] = same(col, last_of(base + c - 1)).astype(BF16)
        g_last[c] = same(col, last_of(base + c)).astype(BF16)
        g_next[c] = same(col, first_of(base + c + 1)).astype(BF16)
        g_first[c] = same(col, first_of(base + c)).astype(BF16)

    def center(i, _):
        at = rows_at(i)
        nh, _r = norm_stats(xb[at, :].astype(F32))
        hid[at, :] = nh
        return 0

    loaded("seg")
    chunks(make_masks)
    loaded("tok")
    lax.fori_loop(0, n_rb, center, 0)
    for p in (PK, PN, PC):
        gather(p, 1)
    for p in (PV, PQ):
        gather(p, 0)
    for p in (PK, PN, PC):
        gather(p, 2)
    for p in (PV, PQ):
        gather(p, 1)
    for p in (PO, *EARLY):
        gather(p, 0)
    for p in (PK, PN, PC):
        gather(p, 3)
    for p in (PV, PQ):
        gather(p, 2)
    for p in (PK, PN):
        gather(p, 4)
    for p in EARLY:
        gather_own(p, 5)

    norms = jnp.sum(gn[...].astype(F32).reshape(math.prod(GRID), 16, CH), axis=0)
    gain1, bias1, gain2, bias2 = (
        jnp.concatenate([norms[4 * q + i : 4 * q + i + 1, :] for q in range(4)], axis=1) for i in range(4)
    )

    def project_k(i, _):
        at = rows_at(i)
        n = (hid[at, :] * gain1 + bias1).astype(BF16)
        n1[at, :] = n
        n1t[:, at] = n.T
        kk_[at, :] = mm(n, weight(K0)).astype(BF16)
        return 0

    lax.fori_loop(0, n_rb, project_k, 0)
    gather(PC, 4)

    def permutation():
        gw = SLOTS // GRID[3]
        a = lax.broadcasted_iota(jnp.int32, (D, D), 0)
        b = lax.broadcasted_iota(jnp.int32, (D, D), 1)
        h, s = b // SLOTS, lax.rem(b, SLOTS)
        src = (s // gw) * (HEADS * gw) + h * gw + lax.rem(s, gw)
        return jnp.where(a == src, 1.0, 0.0).astype(BF16)

    def control_weight():
        parts = []
        for y in range(2):
            for x in range(2):
                for c in range(2):
                    for i in range(4):
                        tiles = [g[y, x, c, j, C0 : C0 + 16, CH * i : CH * i + CH] for j in range(4)]
                        parts.append(jnp.concatenate(tiles, axis=1))
        return jnp.concatenate(parts, axis=0)

    wc_s[...] = mm(control_weight(), permutation()).astype(BF16)

    def project_c(i, _):
        at = rows_at(i)
        e = jnp.exp(mm(n1[at, :], wc_s[...]))
        ew[at, :] = e
        wb[at, :] = e.astype(BF16)
        return 0

    def project_v(i, _):
        at = rows_at(i)
        vv_[at, :] = mm(n1[at, :], weight(V0)).astype(BF16)
        return 0

    def project_q(i, _):
        at = rows_at(i)
        qs[at, :] = (mm(n1[at, :], weight(Q0)).astype(BF16) * (HEAD_DIM**-0.5)).astype(BF16)
        return 0

    def lanes(p):
        return slice(CH * p, CH * p + CH)

    def split(x):
        return [x[:, lanes(p)] for p in pairs]

    def compact(x):
        return x[0:HEAD_DIM, :] + x[HEAD_DIM:CH, :]

    def expand(x):
        return jnp.concatenate([x * leftf, x * rightf], axis=0)

    def pack_row(ref, row):
        hi = row.astype(BF16).astype(F32)
        lo = row - hi
        parts = [a[:, lanes(p)] for a in (hi, lo) for p in pairs]
        parts.append(jnp.zeros((8, CH), F32))
        ref[256:272, :] = jnp.concatenate(parts, axis=0).astype(BF16)

    def unpack_row(x):
        x = x.astype(F32)
        x = x[0:PAIRS, :] + x[PAIRS : 2 * PAIRS, :]
        return jnp.concatenate([x[p : p + 1, :] for p in pairs], axis=1)

    def wide(x):
        return jnp.concatenate([x] * PAIRS, axis=1)

    def scan_step(cur, saved, c, keep, rows_a, rows_b):
        new = [t_mm(a, b) * block_diag for a, b in zip(split(rows_a), split(rows_b))]
        old = [cur[p] for p in pairs]
        for p in pairs:
            saved[c, p] = old[p].astype(BF16)
        for p in pairs:
            cur[p] = keep * old[p] + new[p]

    def place(up):
        return z if up else n_slot - 1 - z

    def toward(up, s):
        return (dp, z + s if up else z - s)

    def edge_gate(up, far):
        if up:
            return same(last_of(base - (far - 1) * n_ch - 1), last_of(base - (far - 2) * n_ch - 1))
        return same(first_of(base + far * n_ch), first_of(base + (far - 1) * n_ch))

    def exchange_copy(idx, src, dst, up, step):
        k = idx * max(n_slot, 4) + step
        if n_slot == 4:
            return remote(src, dst.at[0 if step == 0 else 1], st_send, st_recv, k, toward(up, max(step, 1)))
        return remote(src, dst.at[step], st_send, st_recv, k, toward(up, step))

    def exchange_start(idx, src, dst, up):
        if n_slot == 4:
            @pl.when(lax.rem(place(up), 2) == 0)
            def _():
                exchange_copy(idx, src, dst, up, 0).start()
            return
        for s in range(1, n_slot):
            @pl.when(place(up) + s < n_slot)
            def _():
                exchange_copy(idx, src, dst, up, s).start()

    def exchange_pass(idx, src, dst, up):
        if n_slot == 4:
            @pl.when(place(up) == 1)
            def _():
                exchange_copy(idx, src, dst, up, 0).wait_recv()
                src[...] = (src[...].astype(F32) + edge_gate(up, 1) * dst[0].astype(F32)).astype(BF16)
                for s in (1, 2):
                    exchange_copy(idx, src, dst, up, s).start()

    def exchange_wait(idx, src, dst, up):
        if n_slot == 4:
            @pl.when(place(up) == 3)
            def _():
                exchange_copy(idx, src, dst, up, 0).wait_recv()
                exchange_copy(idx, src, dst, up, 2).wait_recv()
            @pl.when(place(up) == 2)
            def _():
                exchange_copy(idx, src, dst, up, 1).wait_recv()
            gate = jnp.where(place(up) == 3, edge_gate(up, 2), 1.0)
            return dst[0].astype(F32) + gate * dst[1].astype(F32)
        total = 0.0
        for s in range(1, n_slot):
            @pl.when(place(up) >= s)
            def _():
                exchange_copy(idx, src, dst, up, s).wait_recv()
            gate = 1.0
            for far in range(2, s + 1):
                gate = gate * edge_gate(up, far)
            total = total + gate * dst[s].astype(F32)
        return total

    def exchange_end(idx, src, dst, up):
        if n_slot == 4:
            @pl.when(lax.rem(place(up), 2) == 0)
            def _():
                exchange_copy(idx, src, dst, up, 0).wait_send()
            @pl.when(place(up) == 1)
            def _():
                for s in (1, 2):
                    exchange_copy(idx, src, dst, up, s).wait_send()
            return
        for s in range(1, n_slot):
            @pl.when(place(up) + s < n_slot)
            def _():
                exchange_copy(idx, src, dst, up, s).wait_send()

    def pack_state(snd, cur):
        for p in pairs:
            snd[64 * p : 64 * p + 64, :] = compact(cur[p]).astype(BF16)

    def entering(total, e):
        for p in pairs:
            e[p] = expand(total[64 * p : 64 * p + 64, :])
        if total.shape[0] > 256:
            e_z[0:1, :] = unpack_row(total[256:272, :])

    cur_a[...] = jnp.zeros_like(cur_a)
    cur_b[...] = jnp.zeros_like(cur_b)
    cur_z[...] = jnp.zeros_like(cur_z)

    def key_states(c):
        at = rows_at(c, CH)
        keep = same(last_of(base + c - 1), last_of(base + c))
        w = wb[at, :]
        zi = mm(msk[c], w)
        scan_step(cur_a, s_kw, c, keep, kk_[at, :] * wide(g_last[c]), w)
        z_old = cur_z[0:1, :]
        z_st[pl.ds(c, 1), :] = z_old
        inv_z[at, :] = zi
        cur_z[0:1, :] = keep * z_old + zi[CH - 1 : CH, :]

    def value_states(c):
        at = rows_at(c, CH)
        keep = same(last_of(base + c - 1), last_of(base + c))
        scan_step(cur_b, s_wv, c, keep, wb[at, :] * wide(g_last[c]), vv_[at, :])

    lax.fori_loop(0, n_rb, project_c, 0)
    gather(PV, 3)
    gather(PQ, 3)
    chunks(key_states)
    pack_state(snd_a, cur_a)
    pack_row(snd_a, cur_z[0:1, :])
    exchange_start(0, snd_a, rcv_a, True)
    gather(PO, 1)
    gather(PF, 1)
    gather(PV, 4)
    lax.fori_loop(0, n_rb, project_v, 0)
    chunks(value_states)
    pack_state(snd_b, cur_b)
    exchange_start(1, snd_b, rcv_b, True)
    exchange_pass(0, snd_a, rcv_a, True)
    gather(PF + 1, 1)
    gather(PQ, 4)
    lax.fori_loop(0, n_rb, project_q, 0)
    gather(PO, 2)
    gather(PF, 2)

    def two(x):
        return jnp.concatenate([x, x], axis=1)

    def stacks(x):
        return [stack2(a, left, right) for a in split(x)]

    def numerators(c):
        at = rows_at(c, CH)
        m2 = two(msk[c])
        q, k2, w2 = split(qs[at, :]), stacks(kk_[at, :]), stacks(wb[at, :])
        sc = [mm_t(q[p], k2[p]).astype(BF16) * m2 for p in pairs]
        num[at, :] = jnp.concatenate([mm(sc[p], w2[p]) for p in pairs], axis=1)

    chunks(numerators)
    exchange_pass(1, snd_b, rcv_b, True)
    gather(PF + 1, 2)
    gather(PF + 2, 1)
    gather(PO, 3)
    entering(exchange_wait(0, snd_a, rcv_a, True), e_a)

    def softmax(c):
        at = rows_at(c, CH)
        reach = same(last_of(base - 1), last_of(base + c - 1))
        gpw = wide(g_prev[c])
        z_in = z_st[pl.ds(c, 1), :] + reach * e_z[0:1, :]
        skw = [(s_kw[c, p].astype(F32) + reach * e_a[p]).astype(BF16) for p in pairs]
        q = split(qs[at, :] * gpw)
        iz = 1.0 / (inv_z[at, :] + gpw.astype(F32) * z_in)
        from_state = jnp.concatenate([mm(q[p], skw[p]) for p in pairs], axis=1)
        lg = (num[at, :] + from_state) * iz
        top = jnp.concatenate([per_head(jnp.max, a, -jnp.inf) for a in split(lg)], axis=1)
        ex = jnp.exp(lg - top)
        tot = jnp.concatenate([mm(a.astype(BF16), ones_diag) for a in split(ex)], axis=1)
        pr = ex / tot
        for p in pairs:
            s_kw[c, p] = skw[p]
        num[at, :] = lg
        inv_z[at, :] = iz
        prob[at, :] = pr
        rr_[at, :] = (pr * iz).astype(BF16)

    def mixture(c):
        at = rows_at(c, CH)
        reach = same(last_of(base - 1), last_of(base + c - 1))
        m2 = two(msk[c])
        swv = [(s_wv[c, p].astype(F32) + reach * e_b[p]).astype(BF16) for p in pairs]
        w2, v2 = stacks(wb[at, :]), stacks(vv_[at, :])
        r = rr_[at, :]
        rs, rg = split(r), split(r * wide(g_prev[c]))
        mix = [mm_t(rs[p], w2[p]).astype(BF16) * m2 for p in pairs]
        o = jnp.concatenate([mm(mix[p], v2[p]) + mm(rg[p], swv[p]) for p in pairs], axis=1)
        for p in pairs:
            s_wv[c, p] = swv[p]
        oo_[at, :] = o.astype(BF16)

    chunks(softmax)
    gather(PF, 3)
    gather(PF + 3, 1)
    entering(exchange_wait(1, snd_b, rcv_b, True), e_b)
    chunks(mixture)
    gather(PO, 4)
    gather(PF + 2, 2)

    def up_w(j):
        return weight(U0 + 32 * j)

    def down_w(j):
        return weight(U0 + 32 * j + 16)

    c0, c1 = math.sqrt(2.0 / math.pi), 0.044715

    def hidden(i, _):
        at = rows_at(i)
        h = xb[at, :].astype(F32) + mm(oo_[at, :], weight(O0))
        hsum[at, :] = h
        nh, _r = norm_stats(h)
        n = (nh * gain2 + bias2).astype(BF16)
        n2[at, :] = n
        n2t[:, at] = n.T
        return 0

    def feed(j, _):
        def rows_of(i, _):
            at = rows_at(i)
            u = mm(n2[at, :], up_w(j)).astype(BF16)
            dg = mm_t(og[at, :], down_w(j)).astype(BF16)
            sq = u * u
            t = jnp.tanh(u * (c0 + c0 * c1 * sq))
            half = 0.5 + 0.5 * t
            slope = half + u * (1.0 - t * t) * (0.5 * c0 + 1.5 * c0 * c1 * sq)
            cols = pl.ds(D * j, D)
            act[at, cols] = u * half
            du[at, cols] = dg * slope
            return 0

        return lax.fori_loop(0, n_rb, rows_of, 0)

    lax.fori_loop(0, n_rb, hidden, 0)
    loaded("og")
    gather(PF + 1, 3)
    gather(PF, 4)
    gather(PF + 3, 2)

    def put_grad(r0, y, val):
        pg[y, :, :, :, r0 : r0 + 16, :] = val.astype(BF16).reshape(2, 2, 4, 16, D)

    def quarter_grads(j):
        a, d = act[:, D * j : D * j + D], du[:, D * j : D * j + D]
        for y in range(2):
            put_grad(U0 + 32 * j, y, mm(n2t[256 * y : 256 * y + 256, :], d))
        val = t_mm(a, og[...])
        for y in range(2):
            put_grad(U0 + 32 * j + 16, y, val[256 * y : 256 * y + 256, :])

    def out_copy(ref):
        i = [ref is a for a in grad_s].index(True)
        return pltpu.make_async_copy(ref, grad_h[i], out_sem.at[i])

    def store(ref):
        out_copy(ref).start()

    def add_to(dst, src):
        dst[...] = dst[...] + src[...]

    def scatter_copies(p, stage):
        put = lambda src, dst, idx, where: remote(src, dst, rs_send, rs_recv, p * 8 + idx, where)
        if p == PN:
            if stage == 0:
                return [put(ngp.at[:, :, 1 - pc], nrc, 0, at_c)]
            if stage == 1:
                return [put(ngp.at[:, 1 - px, pc], nrx, 1, at_x)]
            if stage == 2:
                return [put(ngp.at[1 - py, px, pc], nry, 2, at_y)]
            return [put(ngp.at[py, px, pc, lax.rem(z + s, n_slot)], nrz.at[s - 1], 4 + s, at_z(s)) for s in range(1, n_slot)]
        r0, r1 = ROWS[p]
        sl = pl.ds(r0, r1 - r0)
        if stage == 0:
            return [put(pg.at[:, :, 1 - pc, :, sl, :], rc.at[:, :, :, sl, :], 0, at_c)]
        if stage == 1:
            return [
                put(pg.at[:, 1 - px, pc, :, sl, la], rx1.at[:, :, sl, :], 1, at_x),
                put(pg.at[1 - py, :, pc, :, sl, lb], ry1.at[:, :, sl, :], 2, at_y),
            ]
        if stage == 2:
            return [
                put(pg.at[1 - py, px, pc, :, sl, la], ry2.at[:, sl, :], 3, at_y),
                put(pg.at[py, 1 - px, pc, :, sl, lb], rx2.at[:, sl, :], 4, at_x),
            ]
        return [
            put(pg.at[py, px, pc, lax.rem(z + s, n_slot), sl, :], rz.at[s - 1, sl, :], 4 + s, at_z(s))
            for s in range(1, n_slot)
        ]

    def scatter_add(p, stage):
        if p == PN:
            if stage == 1:
                for y in range(2):
                    for x in range(2):
                        add_to(ngp.at[y, x, pc], nrc.at[y, x])
            elif stage == 2:
                for y in range(2):
                    add_to(ngp.at[y, px, pc], nrx.at[y])
            elif stage == 3:
                add_to(ngp.at[py, px, pc], nry)
            else:
                total = ngp[py, px, pc, z].astype(F32)
                for s in range(1, n_slot):
                    total = total + nrz[s - 1].astype(F32)
                ng_o[...] = total
                store(ng_o)
            return
        r0, r1 = ROWS[p]
        sl = pl.ds(r0, r1 - r0)
        if stage == 1:
            def body(i, _):
                y, x = i // 2, lax.rem(i, 2)
                add_to(pg.at[y, x, pc, :, sl, :], rc.at[y, x, :, sl, :])
                return 0
            lax.fori_loop(0, 4, body, 0)
        elif stage == 2:
            def body(i, _):
                add_to(pg.at[i, px, pc, :, sl, la], rx1.at[i, :, sl, :])
                add_to(pg.at[py, i, pc, :, sl, lb], ry1.at[i, :, sl, :])
                return 0
            lax.fori_loop(0, 2, body, 0)
        elif stage == 3:
            add_to(pg.at[py, px, pc, :, sl, la], ry2.at[:, sl, :])
            add_to(pg.at[py, px, pc, :, sl, lb], rx2.at[:, sl, :])
        else:
            total = pg[py, px, pc, z, sl, :].astype(F32)
            for s in range(1, n_slot):
                total = total + rz[s - 1, sl, :].astype(F32)
            if PF <= p < PF + 4:
                j = p - PF
                up_g[:, D * j : D * j + D] = total[0:16, :]
                wd_o[16 * j : 16 * j + 16, :] = total[16:32, :]
                if j == 3:
                    store(wd_o)
                    for b in range(4):
                        some = jnp.concatenate([up_g[:, D * i + CH * b : D * i + CH * b + CH] for i in range(4)], axis=1)
                        high = some.astype(BF16)
                        low = (some - high.astype(F32)).astype(BF16)
                        wu_o[:, D * b : D * b + D] = mm_t(high, quarters()) + mm_t(low, quarters())
                    store(wu_o)
            elif p == PC:
                for i in range(4):
                    wc_o[16 * i : 16 * i + 16, :] = total[:, lanes(i)]
                store(wc_o)
            else:
                dst = {PV: wv_o, PQ: wq_o, PK: wk_o, PO: wo_o}[p]
                dst[...] = total
                store(dst)

    def scatter(p, stage):
        if not comm:
            return
        if stage > 0:
            for copy in scatter_copies(p, stage - 1):
                copy.wait_recv()
            scatter_add(p, stage)
        if stage < 4:
            for copy in scatter_copies(p, stage):
                copy.start()

    feed(0, 0)
    quarter_grads(0)
    scatter(PF, 0)
    gather(PF + 1, 4)
    gather(PF + 2, 3)
    feed(1, 0)
    quarter_grads(1)
    scatter(PF + 1, 0)
    scatter(PF, 1)
    gather(PF + 2, 4)
    gather(PF + 3, 3)
    feed(2, 0)
    quarter_grads(2)
    scatter(PF + 2, 0)
    scatter(PF + 1, 1)
    gather(PF + 3, 4)
    feed(3, 0)
    quarter_grads(3)
    scatter(PF + 3, 0)
    scatter(PF + 2, 1)

    def feed_back(i, acc):
        at = rows_at(i)
        dn = jnp.zeros((rb, D), F32)
        for j in range(4):
            dn = dn + mm_t(du[at, D * j : D * j + D], up_w(j))
        nh, rstd = norm_stats(hsum[at, :])
        dh = og[at, :].astype(F32) + norm_back(dn, nh, rstd, gain2)
        hid[at, :] = dh
        a = dh.astype(BF16)
        da[at, :] = a
        do[at, :] = mm_t(a, weight(O0)).astype(BF16)
        return (acc[0] + jnp.sum(dn * nh, axis=0, keepdims=True), acc[1] + jnp.sum(dn, axis=0, keepdims=True))

    zero_row = jnp.zeros((1, D), F32)
    gain2_g, bias2_g = lax.fori_loop(0, n_rb, feed_back, (zero_row, zero_row))
    for y in range(2):
        put_grad(O0, y, t_mm(oo_[:, 256 * y : 256 * y + 256], da[...]))
    scatter(PF, 2)
    scatter(PO, 0)
    scatter(PF + 3, 1)
    scatter(PF + 1, 2)

    cur_a[...] = jnp.zeros_like(cur_a)
    cur_b[...] = jnp.zeros_like(cur_b)
    cur_z[...] = jnp.zeros_like(cur_z)

    def slot_states(i):
        c = n_ch - 1 - i
        at = rows_at(c, CH)
        keep = same(first_of(base + c), first_of(base + c + 1))
        scan_step(cur_a, s_r, c, keep, rr_[at, :] * wide(g_first[c]), do[at, :])

    chunks(slot_states)
    pack_state(snd_d, cur_a)
    exchange_start(3, snd_d, rcv_d, False)

    def slot_grads(i):
        c = n_ch - 1 - i
        at = rows_at(c, CH)
        m2 = two(msk[c])
        gpw = wide(g_prev[c])
        keep = same(first_of(base + c), first_of(base + c + 1))
        w2, v2 = stacks(wb[at, :]), stacks(vv_[at, :])
        do_c = do[at, :]
        ds, dg = split(do_c), split(do_c * gpw)
        dmix = [mm_t(ds[p], v2[p]).astype(BF16) * m2 for p in pairs]
        dr = jnp.concatenate([mm(dmix[p], w2[p]) + mm_t(dg[p], s_wv[c, p]) for p in pairs], axis=1)
        iz, pr, lg = inv_z[at, :], prob[at, :], num[at, :]
        dpr = dr * iz
        inner = jnp.concatenate([mm(a.astype(BF16), ones_diag) for a in split(pr * dpr)], axis=1)
        dl = pr * (dpr - inner)
        dn_c = (dl * iz).astype(BF16)
        dz_c = (-(dpr * pr + dl * lg) * iz).astype(BF16)
        firsts = mm(mskt[c][0:16, :], dz_c)
        scan_step(cur_b, s_n, c, keep, qs[at, :] * wide(g_first[c]), dn_c)
        z_old = cur_z[0:1, :]
        z_r[pl.ds(c, 1), :] = z_old
        cur_z[0:1, :] = keep * z_old + firsts[0:1, :]
        dnum_[at, :] = dn_c
        dz_[at, :] = dz_c

    chunks(slot_grads)
    pack_state(snd_c, cur_b)
    pack_row(snd_c, cur_z[0:1, :])
    exchange_start(2, snd_c, rcv_c, False)
    exchange_pass(3, snd_d, rcv_d, False)
    scatter(PF + 2, 2)
    scatter(PF, 3)
    scatter(PF + 3, 2)
    scatter(PO, 1)

    def query_grads(c):
        at = rows_at(c, CH)
        m2 = two(msk[c])
        dn_c = dnum_[at, :]
        dn, dg = split(dn_c), split(dn_c * wide(g_prev[c]))
        w2, k2 = stacks(wb[at, :]), stacks(kk_[at, :])
        dsc = [mm_t(dn[p], w2[p]).astype(BF16) * m2 for p in pairs]
        dq = jnp.concatenate([mm(dsc[p], k2[p]) + mm_t(dg[p], s_kw[c, p]) for p in pairs], axis=1)
        dq_[at, :] = (dq * (HEAD_DIM**-0.5)).astype(BF16)

    chunks(query_grads)
    for y in range(2):
        put_grad(Q0, y, mm(n1t[256 * y : 256 * y + 256, :], dq_[...]))
    scatter(PQ, 0)
    exchange_pass(2, snd_c, rcv_c, False)

    def near_grads(c):
        at = rows_at(c, CH)
        mt = mskt[c]
        mt2 = two(mt)
        w, v, k = split(wb[at, :]), split(vv_[at, :]), split(kk_[at, :])
        q2, dn2, r2, do2 = (stacks(ref[at, :]) for ref in (qs, dnum_, rr_, do))
        dsc_t = [mm_t(w[p], dn2[p]).astype(BF16) * mt2 for p in pairs]
        dmix_t = [mm_t(v[p], do2[p]).astype(BF16) * mt2 for p in pairs]
        sc_t = [mm_t(k[p], q2[p]).astype(BF16) * mt2 for p in pairs]
        dk = jnp.concatenate([mm(dsc_t[p], q2[p]) for p in pairs], axis=1)
        dw = jnp.concatenate([mm(dmix_t[p], r2[p]) + mm(sc_t[p], dn2[p]) for p in pairs], axis=1)
        num[at, :] = dk
        inv_z[at, :] = dw + mm(mt, dz_[at, :])

    chunks(near_grads)
    scatter(PQ, 1)
    scatter(PF + 1, 3)
    scatter(PO, 2)
    entering(exchange_wait(3, snd_d, rcv_d, False), e_b)

    def value_grads(c):
        at = rows_at(c, CH)
        mt2 = two(mskt[c])
        w_c = wb[at, :]
        w, wg = split(w_c), split(w_c * wide(g_next[c]))
        reach = same(first_of(base + n_ch), first_of(base + c + 1))
        r2, do2 = stacks(rr_[at, :]), stacks(do[at, :])
        st_r = [(s_r[c, p].astype(F32) + reach * e_b[p]).astype(BF16) for p in pairs]
        mix_t = [mm_t(w[p], r2[p]).astype(BF16) * mt2 for p in pairs]
        dv = jnp.concatenate([mm(mix_t[p], do2[p]) + mm(wg[p], st_r[p]) for p in pairs], axis=1)
        for p in pairs:
            s_r[c, p] = st_r[p]
        dv_[at, :] = dv.astype(BF16)

    chunks(value_grads)
    for y in range(2):
        put_grad(V0, y, mm(n1t[256 * y : 256 * y + 256, :], dv_[...]))
    scatter(PV, 0)
    scatter(PF + 2, 3)
    scatter(PQ, 2)
    entering(exchange_wait(2, snd_c, rcv_c, False), e_a)

    def far_grads(c):
        at = rows_at(c, CH)
        reach = same(first_of(base + n_ch), first_of(base + c + 1))
        gnw = wide(g_next[c])
        z_in = z_r[pl.ds(c, 1), :] + reach * e_z[0:1, :]
        wg, vg, kg = (split(ref[at, :] * gnw) for ref in (wb, vv_, kk_))
        st_n = [(s_n[c, p].astype(F32) + reach * e_a[p]).astype(BF16) for p in pairs]
        st_r = [s_r[c, p] for p in pairs]
        dk = num[at, :] + jnp.concatenate([mm_t(wg[p], st_n[p]) for p in pairs], axis=1)
        dw = inv_z[at, :] + gnw.astype(F32) * z_in
        dw = dw + jnp.concatenate([mm_t(vg[p], st_r[p]) + mm(kg[p], st_n[p]) for p in pairs], axis=1)
        dk_[at, :] = dk.astype(BF16)
        dphi_[at, :] = (dw * ew[at, :]).astype(BF16)

    chunks(far_grads)

    for y in range(2):
        cols = slice(256 * y, 256 * y + 256)
        val = mm_t(mm(n1t[cols, :], dphi_[...]).astype(BF16), permutation()).astype(BF16)
        for x in range(2):
            for c in range(2):
                for i in range(4):
                    r = ((x * 2 + c) * 4 + i) * 16
                    for j in range(4):
                        pg[y, x, c, j, C0 : C0 + 16, CH * i : CH * i + CH] = val[r : r + 16, lanes(j)]
    scatter(PC, 0)
    for y in range(2):
        put_grad(K0, y, mm(n1t[256 * y : 256 * y + 256, :], dk_[...]))
    scatter(PK, 0)
    scatter(PV, 1)
    scatter(PO, 3)
    scatter(PQ, 3)
    scatter(PF + 3, 3)

    def input_grads(i, acc):
        at = rows_at(i)
        dn = mm_t(dq_[at, :], weight(Q0)) + mm_t(dk_[at, :], weight(K0)) + mm_t(dv_[at, :], weight(V0)) + mm_t(dphi_[at, :], wc_s[...])
        nh, rstd = norm_stats(xb[at, :].astype(F32))
        tg_o[at, :] = hid[at, :] + norm_back(dn, nh, rstd, gain1)
        return (acc[0] + jnp.sum(dn * nh, axis=0, keepdims=True), acc[1] + jnp.sum(dn, axis=0, keepdims=True))

    def outputs(i, _):
        at = rows_at(i)
        out = hsum[at, :]
        for j in range(4):
            out = out + mm(act[at, D * j : D * j + D], down_w(j))
        out_o[at, :] = out.astype(BF16)
        return 0

    gain1_g, bias1_g = lax.fori_loop(0, n_rb, input_grads, (zero_row, zero_row))
    tg_copy = pltpu.make_async_copy(tg_o, tg_h, out_sem.at[8])
    tg_copy.start()
    norm_g = jnp.concatenate([gain1_g, bias1_g, gain2_g, bias2_g, jnp.zeros((12, D), F32)], axis=0)
    if comm:
        for y in range(2):
            for x in range(2):
                for c in range(2):
                    for j in range(4):
                        d = ((y * 2 + x) * 2 + c) * 4 + j
                        ngp[y, x, c, j] = norm_g[:, lanes(d // 8)].astype(BF16)
    else:
        ng_o[...] = norm_g
    scatter(PN, 0)
    scatter(PC, 1)
    scatter(PK, 1)
    scatter(PV, 2)
    scatter(PN, 1)
    lax.fori_loop(0, n_rb, outputs, 0)
    out_done = pltpu.make_async_copy(out_o, out_h, out_sem.at[9])
    out_done.start()
    scatter(PC, 2)
    scatter(PK, 2)
    scatter(PN, 2)
    for args in ((0, snd_a, rcv_a, True), (1, snd_b, rcv_b, True), (2, snd_c, rcv_c, False), (3, snd_d, rcv_d, False)):
        exchange_end(*args)
    if comm:
        for p in range(len(ROWS) + 1):
            for stage in (*range(4), 4, 5) if p in EARLY else range(4):
                for copy in gather_copies(p, stage):
                    copy.wait_send()
    scatter(PV, 3)
    for j in range(3):
        scatter(PF + j, 4)
    scatter(PC, 3)
    scatter(PK, 3)
    scatter(PN, 3)
    if comm:
        for p in range(len(ROWS) + 1):
            for stage in range(3):
                for copy in scatter_copies(p, stage):
                    copy.wait_send()
    for p in (PF + 3, PO, PQ, PV, PC, PK, PN):
        scatter(p, 4)
    tg_copy.wait()
    out_done.wait()
    if comm:
        for ref in grad_s:
            out_copy(ref).wait()
        for p in range(len(ROWS) + 1):
            for copy in scatter_copies(p, 3):
                copy.wait_send()


def vm(shape, dtype):
    return pltpu.VMEM(shape, dtype)


def run_layer(rows, n_slot, seg_rows, comm, operands):
    n_ch = rows // CH
    act_shape = (rows, D)
    hbm, vmem = pl.BlockSpec(memory_space=pl.ANY), pl.BlockSpec(memory_space=pltpu.VMEM)
    sds = jax.ShapeDtypeStruct
    outs = [sds(act_shape, BF16), sds(act_shape, F32)]
    grads = [(16, D)] * 4 + [(64, CH), (16, FF), (64, D), (16, CH)]
    if comm:
        outs += [sds(shape, F32) for shape in grads]
        out_specs = [hbm] * len(outs)
    else:
        outs += [sds((*GRID, END, D), BF16), sds((16, D), F32)]
        out_specs = [hbm, hbm, vmem, vmem]
    b, f = (lambda: vm(act_shape, BF16)), (lambda: vm(act_shape, F32))
    state = lambda dtype: vm((n_ch, PAIRS, CH, CH), dtype)
    sems = lambda n: pltpu.SemaphoreType.DMA((n,))
    scratch = [
        vm((*GRID, END, D), BF16), vm((*GRID, 16, CH), BF16), b(), vm((seg_rows, CH), jnp.int32), b(), b(), b(), b(), b(), b(),
        f(), f(), f(), f(), b(), b(), f(), b(), vm((rows, FF), BF16), vm((rows, FF), BF16), b(), b(),
        vm((D, rows), BF16), vm((D, rows), BF16), b(), b(), b(), b(), f(),
        state(BF16), state(BF16), vm((max(8, n_ch), D), F32), state(BF16), state(BF16), vm((max(8, n_ch), D), F32),
        vm((PAIRS, CH, CH), F32), vm((PAIRS, CH, CH), F32), vm((8, D), F32),
        vm((PAIRS, CH, CH), F32), vm((PAIRS, CH, CH), F32), vm((8, D), F32),
    ]
    scratch += [vm((n_ch, CH, CH), BF16)] * 6
    long, short = (272, CH), (256, CH)
    scratch += [vm(long, BF16), vm(short, BF16), vm((n_slot, *long), BF16), vm((n_slot, *short), BF16)] * 2
    scratch += [vm((D, D), BF16), sems(4 * max(n_slot, 4)), sems(4 * max(n_slot, 4)), sems(20), sems(10)]
    if comm:
        ny, nx, nc, nz = GRID
        scratch += [
            vm((*GRID, END, D), BF16), vm((*GRID, 16, CH), BF16),
            vm((ny, nx, nz, END, D), BF16), vm((ny, nz, END, D // 2), BF16), vm((nx, nz, END, D // 2), BF16),
            vm((nz, END, D // 2), BF16), vm((nz, END, D // 2), BF16), vm((nz - 1, END, D), BF16),
            vm((ny, nx, nz, 16, CH), BF16), vm((ny, nz, 16, CH), BF16), vm((nz, 16, CH), BF16), vm((nz - 1, 16, CH), BF16),
        ]
        scratch += [sems(24 * (len(ROWS) + 1))] * 2 + [sems(8 * (len(ROWS) + 1))] * 2
        scratch += [vm(operands[7].shape, BF16), vm((4, 1, operands[-1].shape[1]), BF16), vm((16, FF), BF16), vm((16, FF), F32)] + [vm(shape, F32) for shape in grads]
    cfg = dict(rows=rows, n_slot=n_slot, comm=comm)
    return pl.pallas_call(
        functools.partial(kernel_body, cfg),
        out_shape=outs,
        in_specs=[hbm] * len(operands),
        out_specs=out_specs,
        scratch_shapes=scratch,
        compiler_params=pltpu.CompilerParams(collective_id=0, has_side_effects=True, vmem_limit_bytes=63 * 2**20),
    )(*operands)


def finish_body(*refs):
    src, dst, rest = refs[:10], refs[10:23], refs[23:]
    *held, sem_in, sem_out = rest
    jobs = [(1, 0), (1, 1), (1, 2), (1, 3), (0, 0), (0, 1), (0, 2), (0, 3)] + [(i, None) for i in (8, 7, 2, 3, 4, 5)]

    def copy(k, come):
        i, part = jobs[k]
        buf = held[(0, 1, 2, 3, 4, 5, None, 6, 7)[i]]
        cut = lambda ref: ref if part is None else ref.at[pl.ds(part * (ref.shape[0] // 4), ref.shape[0] // 4)]
        if come:
            return pltpu.make_async_copy(cut(src[i]), cut(buf), sem_in.at[k])
        return pltpu.make_async_copy(cut(buf), cut(dst[i]), sem_out.at[k])

    for k in range(len(jobs)):
        copy(k, True).start()
    dst[6][...] = src[6][...].T
    wide = dst[9].shape[1]
    dev = lax.axis_index("dp") * lax.axis_size("slot") + lax.axis_index("slot")
    vals = pltpu.roll(src[9][...], lax.rem(CH - wide * lax.rem(dev, CH // wide), CH), 1)
    for i in range(4):
        dst[9 + i][...] = vals[i : i + 1, 0:wide]
    for k in range(len(jobs)):
        copy(k, True).wait()
        copy(k, False).start()
    for k in range(len(jobs)):
        copy(k, False).wait()


def finish(outs, wide):
    hbm, vmem = pl.BlockSpec(memory_space=pl.ANY), pl.BlockSpec(memory_space=pltpu.VMEM)
    sds = jax.ShapeDtypeStruct
    shapes = [sds(a.shape, a.dtype) for a in outs[:9]] + [sds((1, wide), F32)] * 4
    shapes[6] = sds(outs[6].shape[::-1], F32)
    return pl.pallas_call(
        finish_body,
        out_shape=shapes,
        in_specs=[vmem if i in (6, 9) else hbm for i in range(10)],
        out_specs=[vmem if i == 6 or i > 8 else hbm for i in range(13)],
        scratch_shapes=[vm(outs[i].shape, outs[i].dtype) for i in (0, 1, 2, 3, 4, 5, 7, 8)] + [pltpu.SemaphoreType.DMA((14,))] * 2,
        compiler_params=pltpu.CompilerParams(vmem_limit_bytes=63 * 2**20),
    )(*outs)


def layer(
    tokens, segment_ids, w_query, w_key, w_value, w_out, w_control, w_up, w_down,
    norm1_gain, norm1_bias, norm2_gain, norm2_bias, out_grad,
):
    n_slot, n_dp = lax.axis_size("slot"), lax.axis_size("dp")
    n_dev = n_slot * n_dp
    rows = tokens.shape[0] // n_slot
    seg = segment_ids.reshape(-1, CH)
    norms = (norm1_gain, norm1_bias, norm2_gain, norm2_bias)
    if n_dev == math.prod(GRID) and n_slot == GRID[3]:
        outs = run_layer(rows, n_slot, seg.shape[0], True, (
            tokens, seg, out_grad, w_query, w_key, w_value, w_out,
            w_control.transpose(1, 2, 0).reshape(CH, -1), w_up, w_down, *(a.reshape(1, -1) for a in norms),
        ))
        outs = finish(outs, norm1_gain.shape[0])
        control = outs[6].reshape(*w_control.shape[1:], -1).transpose(2, 0, 1)
        return (*outs[:6], control, *outs[7:9], *(a.reshape(-1) for a in outs[9:]))

    norms = jnp.stack(norms)
    both = ("dp", "slot")
    gather = lambda a: lax.all_gather(a, both, axis=0, tiled=True)
    n_blk = math.prod(GRID)
    wc = lax.all_gather(lax.all_gather(w_control, "dp", axis=0, tiled=True), "slot", axis=2, tiled=True)
    gw = SLOTS // GRID[3]
    wc = wc.reshape(8, 4, 16, HEADS, GRID[3], gw).transpose(0, 4, 2, 1, 3, 5).reshape(n_blk, 16, D)
    norm_all = lax.all_gather(norms, both, axis=1, tiled=True)
    norm_all = norm_all.reshape(4, 4, CH).transpose(1, 0, 2).reshape(16, CH)
    norm_blk = jnp.zeros((n_blk, 16, CH), BF16).at[0].set(norm_all).reshape(*GRID, 16, CH)
    split = lambda a: gather(a).reshape(n_blk, -1, D)
    up = gather(w_up).reshape(n_blk, 16, n_blk, 4, 16).transpose(0, 3, 1, 2, 4).reshape(n_blk, 4, 16, D)
    feed = jnp.concatenate([up, gather(w_down).reshape(n_blk, 4, 16, D)], axis=2).reshape(n_blk, 128, D)
    packed = jnp.concatenate(
        [split(w_key), wc, split(w_value), split(w_query), split(w_out), feed], axis=1
    ).reshape(*GRID, END, D)
    out, tg, part, ng = run_layer(rows, n_slot, seg.shape[0], False, (tokens, seg, out_grad, packed, norm_blk))
    part = part.reshape(n_blk, END, D).astype(F32)
    scatter = lambda a, dim=0: lax.psum_scatter(a, both, scatter_dimension=dim, tiled=True)
    full = lambda r0, r1: part[:, r0:r1].reshape(-1, D)
    wcg = part[:, C0:V0].reshape(8, GRID[3], 16, 4, HEADS, gw).transpose(0, 3, 2, 4, 1, 5).reshape(D, HEADS, SLOTS)
    wcg = lax.psum_scatter(lax.psum_scatter(wcg, "dp", scatter_dimension=0, tiled=True), "slot", scatter_dimension=2, tiled=True)
    feed = part[:, U0:END].reshape(n_blk, 4, 2, 16, D)
    upg = feed[:, :, 0].reshape(n_blk, 4, 16, n_blk, 16).transpose(0, 2, 3, 1, 4).reshape(D, FF)
    ng = scatter(ng[:4], 1)
    return (
        out, tg, scatter(full(Q0, O0)), scatter(full(K0, C0)), scatter(full(V0, Q0)), scatter(full(O0, U0)),
        wcg, scatter(upg), scatter(feed[:, :, 1].reshape(FF, D)), ng[0], ng[1], ng[2], ng[3],
    )


def solution(mesh):
    both = P(("dp", "slot"), None)
    vec = P(("dp", "slot"))
    control = P("dp", None, "slot")
    in_specs = (
        P("dp", None), P("dp"), both, both, both, both, control, both, both, vec, vec, vec, vec, both,
    )
    out_specs = (both, both, both, both, both, both, control, both, both, vec, vec, vec, vec)
    return jax.shard_map(layer, mesh=mesh, in_specs=in_specs, out_specs=out_specs, check_vma=False)
```
